768 devices in a mesh: dom: 96 (over x, z, core), sub: 8 (over y).
Axes of the slice: x: 4, y: 8, z: 12, core: 2. Of those that a mesh axis runs over, the one named last changes fastest.
Arguments:
- state: float32 [5, 64, 24576], P(None, None, ('dom', 'sub')), may hold values from -0.9 to 0.9
- adjoint_final: float32 [5, 64, 24576], P(None, None, ('dom', 'sub')), may hold values from -6 to 6
- send_slot: int32 [768, 384], P(('dom', 'sub')), may hold values from 0 to 192, as said below
- ext_index: int32 [6, 24576], P(None, ('dom', 'sub')), may hold values from 0 to 576, as said below
- ext_perm: int32 [6, 24576], P(None, ('dom', 'sub')), may hold values from 0 to 7
Outputs:
- state_end: float32 [5, 64, 24576], P(None, None, ('dom', 'sub'))
- adjoint_start: float32 [5, 64, 24576], P(None, None, ('dom', 'sub'))
The draws below stay inside these ranges and needn't reach their ends.
Inputs may be any that keep to these rules, and one draw needn't show every extreme that they name: `send_slot`: A value of 192 marks an empty slot, which carries zeros; the share of occupied slots differs from device to device, and device 0 fills all its slots. `ext_index`: values below 192 name a face of the same device, values from 192 to 575 a received slot, and 576 a wall.
All inputs are finite; a program needn't handle non-finite values.
Results may differ from the reference program's by a relative error of at most 0.0006.
Values may be sent and summed in bfloat16 or wider, within the bound.
No kernel may reach another device: no remote copies, remote signals or barrier semaphores. Data moves between devices by JAX's collectives and lax.ppermute only.
A program may use at most 64 MiB of HBM per device.

```python
import jax
import jax.numpy as jnp
import numpy as np
from jax import lax

VARS = 5
NODES = 64
E_DEV = 32
SLOTS = 384
ELEMS = 24576
N_DOM = 96
N_SUB = 8
DEVICES = 768


def draw_send_slot(key, part):
    key = jax.random.fold_in(key, 11)
    first_key, second_key, third_key = jax.random.split(key, 3)
    fill_level = jax.random.randint(first_key, (DEVICES, 1), 30, 101)
    fill_level = jnp.where(jnp.arange(DEVICES)[:, None] == 0, 100, fill_level)
    occupied = jax.random.randint(second_key, (DEVICES, SLOTS), 0, 100) < fill_level
    faces = jax.random.randint(third_key, (DEVICES, SLOTS), 0, 6 * E_DEV)
    return jnp.where(occupied, faces, 6 * E_DEV).astype(jnp.int32)


def draw_ext_index(key, part):
    key = jax.random.fold_in(key, 23)
    first_key, second_key, third_key = jax.random.split(key, 3)
    selector = jax.random.randint(first_key, (6, ELEMS), 0, 100)
    local_face = jax.random.randint(second_key, (6, ELEMS), 0, 6 * E_DEV)
    remote_slot = 6 * E_DEV + jax.random.randint(third_key, (6, ELEMS), 0, SLOTS)
    wall_value = 6 * E_DEV + SLOTS
    chosen = jnp.where(selector < 10, wall_value, jnp.where(selector < 30, remote_slot, local_face))
    return chosen.astype(jnp.int32)


def set_ends(values, key, smallest, high):
    shape = values.shape
    place = [jax.random.randint(jax.random.fold_in(key, axis), (), 0, shape[axis]) for axis in range(len(shape))]
    values = values.at[tuple(place)].set(smallest)
    longest = shape.index(max(shape))
    place[longest] = (place[longest] + 1) % shape[longest]
    return values.at[tuple(place)].set(high)


def steps_of(key, extent, pieces, least, high):
    factor_of = 1.0
    for axis_at, shards_of in pieces:
        steps = jax.random.uniform(jax.random.fold_in(jax.random.fold_in(key, 6), axis_at), (shards_of,), jnp.float32, least / len(pieces), high / len(pieces))
        factor_of = factor_of * jnp.repeat(jnp.exp(steps), extent[axis_at] // shards_of).reshape((-1,) + (1,) * (len(extent) - 1 - axis_at))
    return factor_of


def bell_draw(rng, extent, scale, most, cuts=(), kind=jnp.bfloat16):
    drawn = scale * jax.random.normal(rng, extent, jnp.float32)
    if cuts:
        drawn = drawn * steps_of(rng, extent, cuts, -0.22, 0.18)
    return jnp.clip(drawn, -most, most).astype(kind)


def setup_inputs(seed: int = 0) -> dict:
    seeds = jax.random.split(jax.random.key(seed), 6)
    state = bell_draw(seeds[0], (VARS, NODES, ELEMS), 0.3, 0.9, ((2, 768),), jnp.float32)
    adjoint_final = bell_draw(seeds[1], (VARS, NODES, ELEMS), 1.0, 6.0, ((2, 768),), jnp.float32)
    send_slot = draw_send_slot(jax.random.fold_in(seeds[5], 71), 0)
    ext_index = draw_ext_index(jax.random.fold_in(seeds[5], 71), 0)
    ext_perm = set_ends(jax.random.randint(seeds[4], (6, ELEMS), 0, 8), jax.random.fold_in(seeds[4], 1), 0, 7).astype(jnp.int32)
    return dict(state=state, adjoint_final=adjoint_final, send_slot=send_slot, ext_index=ext_index, ext_perm=ext_perm)


step_size = 0.02
mean_flow = 0.3
penalty = 2.0
metric = 2.0
lift_factor = 12.0

def derivative_table():
    points = np.array([-1.0, -1.0 / np.sqrt(5.0), 1.0 / np.sqrt(5.0), 1.0])
    products = np.array([np.prod([points[target] - points[source] for source in range(4) if source != target]) for target in range(4)])
    result = np.zeros((4, 4))
    for target in range(4):
        for source in range(4):
            if target != source:
                result[target, source] = products[target] / (products[source] * (points[target] - points[source]))
        result[target, target] = -np.sum(result[target])
    return result.astype(np.float32)

def symmetry_table():
    result = np.zeros((8, 16), np.int32)
    for symmetry in range(8):
        layout = np.arange(16).reshape(4, 4)
        if symmetry & 4:
            layout = layout.T
        if symmetry & 1:
            layout = layout[::-1]
        if symmetry & 2:
            layout = layout[:, ::-1]
        result[symmetry] = layout.reshape(-1)
    return result

def normal_table():
    result = np.zeros((3, 6), np.float32)
    for facet in range(6):
        result[facet // 2, facet] = 2.0 * (facet % 2) - 1.0
    return result

def flux_along(fields, drift, normal_speed, pressure_weights):
    density = fields[0]
    pressure = fields[4]
    components = [drift * density + (1.0 + density) * normal_speed]
    for member in range(3):
        velocity = fields[1 + member]
        components.append(drift * velocity + velocity * normal_speed + pressure_weights[member] * pressure)
    components.append(drift * pressure + (1.0 + pressure) * normal_speed)
    return jnp.stack(components)

def volume_term(field):
    elements = field.shape[2]
    derivative = derivative_table()
    forms = ['ai,vijke->vajke', 'aj,vijke->viake', 'ak,vijke->vijae']
    total = jnp.zeros((5, 4, 4, 4, elements), jnp.float32)
    for direction in range(3):
        drift = mean_flow if direction == 0 else 0.0
        weights = [1.0 if member == direction else 0.0 for member in range(3)]
        flux = flux_along(field, drift, field[1 + direction], weights).reshape(5, 4, 4, 4, elements)
        total = total + jnp.einsum(forms[direction], jnp.asarray(derivative, jnp.float32), flux, precision=lax.Precision.HIGHEST)
    return -metric * total.reshape(5, 64, elements)

def normal_flux(trace):
    normals = normal_table()
    weights = [jnp.asarray(normals[member], jnp.float32)[:, None] for member in range(3)]
    normal_speed = weights[0] * trace[1] + weights[1] * trace[2] + weights[2] * trace[3]
    return flux_along(trace, mean_flow * weights[0], normal_speed, weights)

def face_traces(field):
    elements = field.shape[2]
    cube = field.reshape(5, 4, 4, 4, elements)
    surfaces = [cube[:, 0], cube[:, 3], cube[:, :, 0], cube[:, :, 3], cube[:, :, :, 0], cube[:, :, :, 3]]
    return jnp.stack([surface.reshape(5, 16, elements) for surface in surfaces], axis=2).reshape(5, 16, 6 * elements)

def pack_sends(field, slots, n_sub):
    traces = face_traces(field)
    padded = jnp.concatenate([traces, jnp.zeros((5, 16, 1), traces.dtype)], axis=2)
    picked = jnp.take(padded, slots, axis=2)
    return picked.transpose(2, 0, 1).reshape(3, n_sub, -1)

def residual(field, arrived, ext_index, ext_perm):
    elements = field.shape[2]
    symmetries = symmetry_table()
    traces = face_traces(field)
    incoming = arrived.reshape(-1, 5, 16).transpose(1, 2, 0)
    lookup = jnp.concatenate([traces, incoming, jnp.zeros((5, 16, 1), traces.dtype)], axis=2)
    count = lookup.shape[2]
    flattened = ext_index.reshape(-1).astype(jnp.int32)
    orient = ext_perm.reshape(-1).astype(jnp.int32)
    matches = orient[None, None, :] == jnp.arange(8, dtype=jnp.int32)[:, None, None]
    node_map = lax.optimization_barrier(jnp.sum(jnp.where(matches, jnp.asarray(symmetries)[:, :, None], 0), axis=0)).astype(jnp.int32)
    gather_index = node_map * count + flattened[None, :]
    exterior = jnp.take(lookup.reshape(5, -1), gather_index, axis=1)
    direction = jnp.arange(6 * elements, dtype=jnp.int32) // elements // 2
    component = jnp.arange(5, dtype=jnp.int32)[:, None]
    mirror_sign = jnp.where(component == 1 + direction[None, :], -1.0, 1.0).astype(jnp.float32)[:, None, :]
    at_wall = (flattened == count - 1)[None, None, :]
    exterior = jnp.where(at_wall, traces * mirror_sign, exterior)
    interior = traces.reshape(5, 16, 6, elements)
    exterior = exterior.reshape(5, 16, 6, elements)
    penalty_jump = 0.5 * (normal_flux(interior) - normal_flux(exterior)) + 0.5 * penalty * (exterior - interior)
    jumps = penalty_jump.reshape(5, 4, 4, 6, elements)
    lifted = jnp.zeros((5, 4, 4, 4, elements), jnp.float32)
    lifted = lifted.at[:, 0].add(jumps[:, :, :, 0])
    lifted = lifted.at[:, 3].add(jumps[:, :, :, 1])
    lifted = lifted.at[:, :, 0].add(jumps[:, :, :, 2])
    lifted = lifted.at[:, :, 3].add(jumps[:, :, :, 3])
    lifted = lifted.at[:, :, :, 0].add(jumps[:, :, :, 4])
    lifted = lifted.at[:, :, :, 3].add(jumps[:, :, :, 5])
    return volume_term(field) + lift_factor * lifted.reshape(5, 64, elements)

def global_forward(buffers):
    layout = buffers.reshape(N_DOM, N_SUB, 3, N_SUB, -1)
    groups = []
    for group_id in range(3):
        portion = jnp.roll(layout[:, :, group_id], group_id - 1, axis=0)
        groups.append(jnp.swapaxes(portion, 1, 2))
    return jnp.stack(groups, axis=2).reshape(N_DOM * N_SUB, 3, N_SUB, -1)

def global_backward(gradients):
    layout = gradients.reshape(N_DOM, N_SUB, 3, N_SUB, -1)
    groups = []
    for group_id in range(3):
        portion = jnp.swapaxes(layout[:, :, group_id], 1, 2)
        groups.append(jnp.roll(portion, 1 - group_id, axis=0))
    return jnp.stack(groups, axis=2).reshape(N_DOM * N_SUB, 3, N_SUB, -1)

def reference(state, adjoint_final, send_slot, ext_index, ext_perm):
    devices = N_DOM * N_SUB
    fields = state.reshape(5, 64, devices, E_DEV).transpose(2, 0, 1, 3)
    finals = adjoint_final.reshape(5, 64, devices, E_DEV).transpose(2, 0, 1, 3)
    indices = ext_index.reshape(6, devices, E_DEV).transpose(1, 0, 2)
    orients = ext_perm.reshape(6, devices, E_DEV).transpose(1, 0, 2)

    def evaluate(current):
        outgoing = lax.map(lambda items: pack_sends(items[0], items[1], N_SUB), (current, send_slot))
        rounded = lax.optimization_barrier(outgoing.astype(jnp.bfloat16)).astype(jnp.float32)
        arrived = global_forward(rounded)
        rates = lax.map(lambda items: residual(items[0], items[1], items[2], items[3]), (current, arrived, indices, orients))
        return (rates, arrived)

    def pull_back(current, arrived, cotangent):

        def local_part(items):
            _, pullback = jax.vjp(lambda first, second: residual(first, second, items[3], items[4]), items[0], items[1])
            return pullback(items[2])
        grad_state, grad_arrived = lax.map(local_part, (current, arrived, cotangent, indices, orients))
        returned = global_backward(grad_arrived)

        def pack_part(items):
            _, pullback = jax.vjp(lambda first: pack_sends(first, items[1], N_SUB), items[0])
            return items[2] + pullback(items[3])[0]
        return lax.map(pack_part, (current, send_slot, grad_state, returned))
    rate_first, arrived_first = evaluate(fields)
    middle = fields + step_size * rate_first
    rate_second, arrived_second = evaluate(middle)
    final = 0.5 * fields + 0.5 * (middle + step_size * rate_second)
    back_middle = 0.5 * finals + 0.5 * step_size * pull_back(middle, arrived_second, finals)
    back_start = 0.5 * finals + back_middle + step_size * pull_back(fields, arrived_first, back_middle)
    state_end = final.transpose(1, 2, 0, 3).reshape(5, 64, devices * E_DEV)
    adjoint_start = back_start.transpose(1, 2, 0, 3).reshape(5, 64, devices * E_DEV)
    return (state_end, adjoint_start)
```

```python
import jax
import jax.numpy as jnp
import numpy as np
import ml_dtypes
from jax import lax
from jax.experimental import pallas as pl
from jax.experimental.pallas import tpu as pltpu
from jax.sharding import PartitionSpec as P

step_size = 0.02
mean_flow = 0.3
lift_factor = 12.0

E = 32
F = 192
S = 384
G = 128
f32 = jnp.float32
bf16 = jnp.bfloat16
i32 = jnp.int32


def derivative_table():
    points = np.array([-1.0, -1.0 / np.sqrt(5.0), 1.0 / np.sqrt(5.0), 1.0])
    products = np.array(
        [np.prod([points[t] - points[s] for s in range(4) if s != t]) for t in range(4)]
    )
    result = np.zeros((4, 4))
    for t in range(4):
        for s in range(4):
            if t != s:
                result[t, s] = products[t] / (products[s] * (points[t] - points[s]))
        result[t, t] = -np.sum(result[t])
    return result.astype(np.float32)


def halves_of(matrix):
    hi = matrix.astype(ml_dtypes.bfloat16)
    lo = (matrix - hi.astype(np.float32)).astype(ml_dtypes.bfloat16)
    return hi, lo


def derivative_operands():
    d = -2.0 * derivative_table()
    eye = np.eye(4, dtype=np.float32)
    along = [
        np.kron(d, np.kron(eye, eye)),
        np.kron(eye, np.kron(d, eye)),
        np.kron(eye, np.kron(eye, d)),
    ]
    two = [np.kron(np.eye(2, dtype=np.float32), a).astype(np.float32) for a in along]
    hi, lo = halves_of(np.concatenate([t.T for t in two], axis=0))
    forward = np.concatenate([hi, lo], axis=1)
    hi, lo = halves_of(np.concatenate(two, axis=1))
    backward = np.concatenate([hi, lo], axis=1)
    return forward, backward


def lanes(rows):
    return lax.broadcasted_iota(i32, (rows, 128), 1)


def take(x, index):
    return jnp.take_along_axis(x, index, axis=1)


def turn(x, shift):
    return pltpu.roll(x, shift, 1)


def halves(x):
    hi = x.astype(bf16)
    lo = (x - hi.astype(f32)).astype(bf16)
    return hi, lo


def dot(a, b):
    return jnp.dot(a, b, preferred_element_type=f32)


def select_rows(onehot, x):
    hi, lo = halves(x)
    r = dot(onehot, jnp.concatenate([hi, lo], axis=1))
    return r[:, :128] + r[:, 128:]


def to_tiles(ref):
    zero = jnp.zeros((64, E), f32)
    tiles = []
    for j in range(3):
        low = ref[2 * j]
        high = ref[2 * j + 1] if j < 2 else zero
        tiles.append(jnp.transpose(jnp.concatenate([low, high], axis=0)))
    return tiles


def from_tiles(tiles, ref):
    for j in range(3):
        t = jnp.transpose(tiles[j])
        ref[2 * j] = t[:64]
        if j < 2:
            ref[2 * j + 1] = t[64:]


def load_tiles(ref):
    return [ref[:, 128 * j : 128 * (j + 1)] for j in range(3)]


def store_tiles(ref, tiles):
    for j in range(3):
        ref[:, 128 * j : 128 * (j + 1)] = tiles[j]


def spread(tiles):
    low = lanes(E) < 64
    back0, back1, back2 = turn(tiles[0], 64), turn(tiles[1], 64), turn(tiles[2], 64)
    ux = jnp.where(low, back0, tiles[0])
    uy = jnp.where(low, tiles[1], back1)
    uz = jnp.where(low, back1, tiles[1])
    p = tiles[2] + back2
    return low, (ux, uy, uz), p


def volume(tiles, table):
    low, speeds, p = spread(tiles)
    fluxes = []
    for a in range(3):
        u = speeds[a]
        c = u + mean_flow if a == 0 else u
        high0 = p if a == 0 else jnp.zeros_like(p)
        parts = [c * tiles[0] + jnp.where(low, u, high0), c * tiles[1], c * tiles[2] + jnp.where(low, u, 0.0)]
        if a == 1:
            parts[1] = parts[1] + jnp.where(low, p, 0.0)
        if a == 2:
            parts[1] = parts[1] + jnp.where(low, 0.0, p)
        fluxes.append(jnp.concatenate(parts, axis=0))
    hi, lo = halves(jnp.concatenate(fluxes, axis=1))
    r = dot(jnp.concatenate([hi, lo], axis=0), table)
    out = r[:96, :128] + (r[:96, 128:] + r[96:, :128])
    return [out[:32], out[32:64], out[64:96]]


def derivative_back(tiles, table):
    hi, lo = halves(jnp.concatenate(tiles, axis=0))
    r = dot(jnp.concatenate([hi, lo], axis=0), table)
    return r[:96, :384] + (r[:96, 384:] + r[96:, :384])


def volume_back(tiles, z):
    low, speeds, _ = spread(tiles)
    one = jnp.where(low, 1.0, 0.0).astype(f32)
    plus = [tiles[0] + one, tiles[1], tiles[2] + one]
    out = [jnp.zeros((E, 128), f32) for _ in range(3)]
    sums = []
    parts = []
    for a in range(3):
        c = speeds[a] + mean_flow if a == 0 else speeds[a]
        za = [z[32 * j : 32 * (j + 1), 128 * a : 128 * (a + 1)] for j in range(3)]
        total = plus[0] * za[0] + plus[1] * za[1] + plus[2] * za[2]
        sums.append(total + turn(total, 64))
        parts.append(za)
        out = [out[j] + c * za[j] for j in range(3)]
    pressure = turn(parts[0][0], 64) + parts[1][1] + turn(parts[2][1], 64)
    out[0] = out[0] + jnp.where(low, 0.0, sums[0])
    out[1] = out[1] + jnp.where(low, sums[1], sums[2])
    out[2] = out[2] + jnp.where(low, pressure, 0.0)
    return out


def traces(tiles):
    lane = lanes(E)
    m = lane & 15
    r, s = m >> 2, m & 3
    base = ((lane >> 4) & 1) * 64
    rows = []
    for f in range(6):
        b = f % 2
        node = (48 * b + m, 16 * r + 12 * b + s, 4 * m + 3 * b)[f // 2]
        index = base + node
        t = jnp.where(
            lane < 32,
            take(tiles[0], index),
            jnp.where(lane < 64, take(tiles[1], index), take(tiles[2], index)),
        )
        rows.append(jnp.where(lane < 80, t, 0.0))
    return jnp.concatenate(rows, axis=0)


def lifted(x):
    lane = lanes(E)
    n = lane & 63
    i, j, k = n >> 4, (n >> 2) & 3, n & 3
    grid = ((i, 4 * j + k), (j, 4 * i + k), (k, 4 * i + j))
    tiles = []
    for tile in range(3):
        v = 2 * tile + (lane >> 6)
        total = jnp.zeros((E, 128), f32)
        for a in range(3):
            layer, m = grid[a]
            index = v * 16 + m
            first = take(x[64 * a : 64 * a + 32], index)
            last = take(x[64 * a + 32 : 64 * a + 64], index)
            total = total + jnp.where(layer == 0, first, jnp.where(layer == 3, last, 0.0))
        tiles.append(total)
    return tiles


class Faces:
    def __init__(self):
        row = lax.broadcasted_iota(i32, (F, 128), 0)
        lane = lanes(F)
        self.v = lane >> 4
        m = lane & 15
        axis = row >> 6
        self.sign = jnp.where((row >> 5) & 1 == 1, 1.0, -1.0).astype(f32)
        self.drift = jnp.where(axis == 0, mean_flow, 0.0).astype(f32)
        self.normal = self.v == axis + 1
        self.normal_index = (axis + 1) * 16 + m
        self.pressure_index = 64 + m
        self.m = m
        self.ends = (self.v == 0) | (self.v == 4)
        self.ones = jnp.where(self.ends, 1.0, 0.0).astype(f32)
        self.axis = axis

    def flux(self, x):
        u = take(x, self.normal_index)
        p = take(x, self.pressure_index)
        return self.sign * (
            (self.drift + u) * x + jnp.where(self.ends, u, 0.0) + jnp.where(self.normal, p, 0.0)
        )

    def flux_back(self, x, w):
        u = take(x, self.normal_index)
        n = take(w, self.normal_index)
        h = over_fields((x + self.ones) * w)
        return self.sign * (
            (self.drift + u) * w + jnp.where(self.v == 4, n, 0.0) + jnp.where(self.normal, h, 0.0)
        )

    def flux_back_along(self, a, x, w):
        index = (a + 1) * 16 + self.m
        u = take(x, index)
        n = take(w, index)
        h = over_fields((x + self.ones) * w)
        c = u + mean_flow if a == 0 else u
        return c * w + jnp.where(self.v == 4, n, 0.0) + jnp.where(self.v == a + 1, h, 0.0)

    def mirror(self, x):
        return jnp.where(self.normal, -x, x)


def over_fields(h):
    h = h + turn(h, 16)
    h = h + turn(h, 32)
    return h + turn(h, 64)


def column_of(table_ref):
    x = table_ref[...].astype(f32)
    x = jnp.concatenate([x, jnp.zeros((2, E), f32)], axis=0)
    t = jnp.transpose(x)
    return jnp.concatenate([t[:, f : f + 1] for f in range(6)], axis=0).astype(i32)


def row_of(table_ref):
    return jnp.concatenate([table_ref[f : f + 1, :] for f in range(6)], axis=1)


def slot_column(send_ref):
    x = jnp.broadcast_to(send_ref[...].astype(f32), (8, S))
    return jnp.transpose(x)[:, :1].astype(i32)


def onehot(rows, columns, first, second):
    return jnp.where(first == second, 1.0, 0.0).astype(bf16)


def faces_from_columns(ext_col):
    return onehot(F, F, ext_col, lax.broadcasted_iota(i32, (F, F), 1))


def columns_from_faces(ext_row):
    return onehot(F, F, ext_row, lax.broadcasted_iota(i32, (F, F), 0))


def faces_from_slots(ext_col):
    return onehot(F, S, ext_col - F, lax.broadcasted_iota(i32, (F, S), 1))


def slots_from_faces(ext_row):
    return onehot(S, F, ext_row - F, lax.broadcasted_iota(i32, (S, F), 0))


def slots_from_columns(send_col):
    return onehot(S, F, send_col, lax.broadcasted_iota(i32, (S, F), 1))


def columns_from_slots(send_row):
    return onehot(F, S, send_row, lax.broadcasted_iota(i32, (F, S), 0))


def orientation(perm_col):
    lane = lanes(F)
    m = lane & 15
    r, s = m >> 2, m & 3
    k = jnp.broadcast_to(perm_col, (F, 128))
    flip_r = (k & 1) == 1
    flip_s = (k & 2) == 2
    swap = (k & 4) == 4
    r1 = jnp.where(flip_r, 3 - r, r)
    s1 = jnp.where(flip_s, 3 - s, s)
    base = lane - m
    index = base + jnp.where(swap, 4 * s1 + r1, 4 * r1 + s1)
    r2 = jnp.where(swap, s, r)
    s2 = jnp.where(swap, r, s)
    r2 = jnp.where(flip_r, 3 - r2, r2)
    s2 = jnp.where(flip_s, 3 - s2, s2)
    inverse = base + 4 * r2 + s2
    return index, inverse


def packed(x):
    tail = lanes(F) >= 80
    first = jnp.where(tail, turn(x, 80), 0.0)
    second = jnp.where(tail, turn(x, 32), 0.0)
    return jnp.concatenate([first, second], axis=1).astype(bf16)


def unpacked(g):
    lane = lanes(F)
    first = jnp.where(lane < 48, turn(g[:, :128], 48), 0.0)
    second = jnp.where((lane >= 48) & (lane < 80), turn(g[:, 128:256], 96), 0.0)
    return first + second


def write_buffers(forward, back, refs):
    for o, ref in enumerate(refs):
        fw = forward[G * o : G * (o + 1)]
        bk = back[G * (2 - o) : G * (3 - o)]
        wide = bk.shape[1]
        ref[:, :256] = (fw + bk[:, :256]).astype(bf16) if wide > 128 else (fw + jnp.concatenate([bk, jnp.zeros_like(bk)], axis=1)).astype(bf16)
        if wide > 256:
            ref[:, 256:] = bk[:, 256:].astype(bf16)


def exterior(faces, wall, index, onehot_local, t):
    return jnp.where(wall, faces.mirror(t), take(select_rows(onehot_local, t), index))


def arrivals(z_ref):
    width = z_ref.shape[3]
    return [z_ref[:, o].reshape(G, width) for o in range(3)]


def pack_kernel(state_ref, final_ref, send_ref, ext_ref, perm_ref,
                minus_ref, own_ref, plus_ref, q_ref, w_ref, t_ref, lam_ref):
    faces = Faces()
    q = to_tiles(state_ref)
    w = to_tiles(final_ref)
    store_tiles(q_ref, q)
    store_tiles(w_ref, w)
    t = traces(q)
    lam = lift_factor * traces(w)
    t_ref[...] = t
    lam_ref[...] = lam
    _, inverse = orientation(column_of(perm_ref))
    y = take(lam, inverse)
    signed = faces.sign * y
    stack = [y] + [jnp.where(faces.axis == a, signed, 0.0) for a in range(3)]
    stack = jnp.concatenate([x.astype(bf16) for x in stack], axis=1)
    back = dot(slots_from_faces(row_of(ext_ref)), stack)
    forward = dot(slots_from_columns(slot_column(send_ref)), packed(t))
    write_buffers(forward, back, (minus_ref, own_ref, plus_ref))


def first_local_kernel(q_ref, w_ref, t_ref, ext_ref, perm_ref, forward_ref, backward_ref, base_ref, z_ref):
    faces = Faces()
    ext_col = column_of(ext_ref)
    index, _ = orientation(column_of(perm_ref))
    wall = jnp.broadcast_to(ext_col, (F, 128)) == F + S
    q = load_tiles(q_ref)
    t = t_ref[...]
    x = exterior(faces, wall, index, faces_from_columns(ext_col), t)
    jump = 0.5 * (faces.flux(t) - faces.flux(x)) + (x - t)
    faced = lifted(lift_factor * jump)
    inner = volume(q, forward_ref[...])
    store_tiles(base_ref, [q[j] + step_size * (inner[j] + faced[j]) for j in range(3)])
    z_ref[...] = derivative_back(load_tiles(w_ref), backward_ref[...])


def middle_kernel(base_ref, w_ref, t_lam_ref, z_ref, arrived_ref, send_ref, ext_ref, perm_ref,
                  minus_ref, own_ref, plus_ref, q1_ref, w1_ref, t1_ref, x1_ref, lam1_ref):
    faces = Faces()
    ext_col = column_of(ext_ref)
    ext_row = row_of(ext_ref)
    index, inverse = orientation(column_of(perm_ref))
    ext_wide = jnp.broadcast_to(ext_col, (F, 128))
    wall = ext_wide == F + S
    remote = (ext_wide >= F) & (ext_wide < F + S)
    from_plus, from_own, from_minus = arrivals(arrived_ref)
    incoming = jnp.concatenate([from_plus[:, :256], from_own[:, :256], from_minus[:, :256]], axis=0)
    xr = take(unpacked(dot(faces_from_slots(ext_col), incoming)), index)
    faced = lifted((lift_factor * step_size) * (xr - 0.5 * faces.flux(xr)))
    base = load_tiles(base_ref)
    q1 = [base[j] + faced[j] for j in range(3)]
    store_tiles(q1_ref, q1)
    t1 = traces(q1)
    t1_ref[...] = t1
    send_row = send_ref[...]
    forward = dot(slots_from_columns(slot_column(send_ref)), packed(t1))
    lam = t_lam_ref[...]
    x1 = exterior(faces, wall, index, faces_from_columns(ext_col), t1)
    x1_ref[...] = x1
    bar = jnp.where(remote, 0.0, lam - 0.5 * faces.flux_back(x1, lam))
    total = 0.5 * faces.flux_back(t1, lam) - lam + jnp.where(wall, faces.mirror(bar), 0.0)
    total = total + select_rows(columns_from_faces(ext_row), take(bar, inverse))
    returned = jnp.concatenate([from_minus, from_own, from_plus], axis=0)
    sums = dot(columns_from_slots(send_row), returned)
    valid = lanes(F) < 80
    sums = [jnp.where(valid, sums[:, 128 * a : 128 * (a + 1)], 0.0) for a in range(4)]
    t1_sent = t1.astype(bf16).astype(f32)
    through = [faces.flux_back_along(a, t1_sent, sums[a + 1]) for a in range(3)]
    total = total + sums[0] - 0.5 * (through[0] + through[1] + through[2])
    inner = volume_back(q1, z_ref[...])
    faced = lifted(total)
    w = load_tiles(w_ref)
    w1 = [0.5 * w[j] + (0.5 * step_size) * (inner[j] + faced[j]) for j in range(3)]
    store_tiles(w1_ref, w1)
    lam1 = lift_factor * traces(w1)
    lam1_ref[...] = lam1
    y = take(lam1 - 0.5 * faces.flux_back(xr, lam1), inverse)
    back = dot(slots_from_faces(ext_row), y.astype(bf16))
    write_buffers(forward, back, (minus_ref, own_ref, plus_ref))


def second_local_kernel(q_ref, w_ref, t_ref, q1_ref, w1_ref, t1_ref, x1_ref, lam1_ref, ext_ref, perm_ref,
                        forward_ref, backward_ref, end_ref, start_ref):
    faces = Faces()
    ext_col = column_of(ext_ref)
    index, inverse = orientation(column_of(perm_ref))
    ext_wide = jnp.broadcast_to(ext_col, (F, 128))
    wall = ext_wide == F + S
    remote = (ext_wide >= F) & (ext_wide < F + S)
    q = load_tiles(q_ref)
    q1 = load_tiles(q1_ref)
    t1 = t1_ref[...]
    x1 = x1_ref[...]
    jump = 0.5 * (faces.flux(t1) - faces.flux(x1)) + (x1 - t1)
    faced = lifted(lift_factor * jump)
    inner = volume(q1, forward_ref[...])
    store_tiles(end_ref, [0.5 * q[j] + 0.5 * (q1[j] + step_size * (inner[j] + faced[j])) for j in range(3)])
    t = t_ref[...]
    lam1 = lam1_ref[...]
    x = exterior(faces, wall, index, faces_from_columns(ext_col), t)
    bar = jnp.where(remote, 0.0, lam1 - 0.5 * faces.flux_back(x, lam1))
    total = 0.5 * faces.flux_back(t, lam1) - lam1 + jnp.where(wall, faces.mirror(bar), 0.0)
    total = total + select_rows(columns_from_faces(row_of(ext_ref)), take(bar, inverse))
    w = load_tiles(w_ref)
    w1 = load_tiles(w1_ref)
    inner = volume_back(q, derivative_back(w1, backward_ref[...]))
    faced = lifted(total)
    store_tiles(start_ref, [0.5 * w[j] + w1[j] + step_size * (inner[j] + faced[j]) for j in range(3)])


def last_kernel(end_base_ref, start_base_ref, arrived_ref, send_ref, ext_ref, perm_ref, end_ref, start_ref):
    faces = Faces()
    index, _ = orientation(column_of(perm_ref))
    from_plus, from_own, from_minus = arrivals(arrived_ref)
    incoming = jnp.concatenate([from_plus, from_own, from_minus], axis=0)
    returned = jnp.concatenate([from_minus[:, :128], from_own[:, :128], from_plus[:, :128]], axis=0)
    xr = take(unpacked(dot(faces_from_slots(column_of(ext_ref)), incoming)), index)
    faced = lifted((0.5 * step_size * lift_factor) * (xr - 0.5 * faces.flux(xr)))
    base = load_tiles(end_base_ref)
    from_tiles([base[j] + faced[j] for j in range(3)], end_ref)
    bar = dot(columns_from_slots(send_ref[...]), returned)
    bar = jnp.where(lanes(F) < 80, bar, 0.0)
    faced = lifted(step_size * bar)
    base = load_tiles(start_base_ref)
    from_tiles([base[j] + faced[j] for j in range(3)], start_ref)


def shape(*dims, dtype=f32):
    return jax.ShapeDtypeStruct(dims, dtype)


def call(kernel, outs, *args):
    return pl.pallas_call(
        kernel,
        out_shape=outs,
        cost_estimate=pl.CostEstimate(flops=200_000_000, bytes_accessed=1_000_000, transcendentals=0),
        compiler_params=pltpu.CompilerParams(vmem_limit_bytes=32 * 1024 * 1024),
    )(*args)


def exchange(to_minus, to_own, to_plus):
    count = lax.axis_size("dom")
    width = to_own.shape[1]

    def moved(value, steps):
        pairs = [(source, (source + steps) % count) for source in range(count)]
        return lax.ppermute(value, "dom", pairs)

    pieces = [moved(to_minus, -1), to_own, moved(to_plus, 1)]
    whole = jnp.stack([x.reshape(8, 16, width) for x in pieces], axis=1)
    return lax.all_to_all(whole, "sub", split_axis=0, concat_axis=0, tiled=True)


def shards(state, adjoint_final, send_slot, ext_index, ext_perm):
    forward, backward = derivative_operands()
    forward, backward = jnp.asarray(forward), jnp.asarray(backward)
    node = shape(E, 384)
    face = shape(F, 128)
    wide = shape(G, 512, dtype=bf16)
    slim = shape(G, 256, dtype=bf16)

    *buffers, q, w, t, lam = call(
        pack_kernel, (wide, wide, wide, node, node, face, face),
        state, adjoint_final, send_slot, ext_index, ext_perm)
    arrived = exchange(*buffers)
    base, z = call(first_local_kernel, (node, shape(96, 384)), q, w, t, ext_index, ext_perm, forward, backward)
    *buffers, q1, w1, t1, x1, lam1 = call(
        middle_kernel, (slim, slim, slim, node, node, face, face, face),
        base, w, lam, z, arrived, send_slot, ext_index, ext_perm)
    arrived = exchange(*buffers)
    end_base, start_base = call(
        second_local_kernel, (node, node),
        q, w, t, q1, w1, t1, x1, lam1, ext_index, ext_perm, forward, backward)
    out = shape(5, 64, E)
    return tuple(call(
        last_kernel, (out, out), end_base, start_base, arrived, send_slot, ext_index, ext_perm))


def solution(mesh):
    return jax.shard_map(
        shards,
        mesh=mesh,
        in_specs=(
            P(None, None, ("dom", "sub")),
            P(None, None, ("dom", "sub")),
            P(("dom", "sub"), None),
            P(None, ("dom", "sub")),
            P(None, ("dom", "sub")),
        ),
        out_specs=(P(None, None, ("dom", "sub")), P(None, None, ("dom", "sub"))),
        check_vma=False,
    )
```

```python
import jax
import jax.numpy as jnp
import numpy as np
import ml_dtypes
from jax import lax
from jax.experimental import pallas as pl
from jax.experimental.pallas import tpu as pltpu
from jax.sharding import PartitionSpec as P

step_size = 0.02
mean_flow = 0.3
lift_factor = 12.0

E = 32
F = 192
S = 384
G = 128
f32 = jnp.float32
bf16 = jnp.bfloat16
i32 = jnp.int32


def derivative_table():
    points = np.array([-1.0, -1.0 / np.sqrt(5.0), 1.0 / np.sqrt(5.0), 1.0])
    products = np.array(
        [np.prod([points[t] - points[s] for s in range(4) if s != t]) for t in range(4)]
    )
    result = np.zeros((4, 4))
    for t in range(4):
        for s in range(4):
            if t != s:
                result[t, s] = products[t] / (products[s] * (points[t] - points[s]))
        result[t, t] = -np.sum(result[t])
    return result.astype(np.float32)


def halves_of(matrix):
    hi = matrix.astype(ml_dtypes.bfloat16)
    lo = (matrix - hi.astype(np.float32)).astype(ml_dtypes.bfloat16)
    return hi, lo


def derivative_operands():
    d = -2.0 * derivative_table()
    eye = np.eye(4, dtype=np.float32)
    along = [
        np.kron(d, np.kron(eye, eye)),
        np.kron(eye, np.kron(d, eye)),
        np.kron(eye, np.kron(eye, d)),
    ]
    two = [np.kron(np.eye(2, dtype=np.float32), a).astype(np.float32) for a in along]
    hi, lo = halves_of(np.concatenate([t.T for t in two], axis=0))
    forward = np.concatenate([hi, lo], axis=1)
    hi, lo = halves_of(np.concatenate(two, axis=1))
    backward = np.concatenate([hi, lo], axis=1)
    return forward, backward


def lanes(rows):
    return lax.broadcasted_iota(i32, (rows, 128), 1)


def take(x, index):
    return jnp.take_along_axis(x, index, axis=1)


def turn(x, shift):
    return pltpu.roll(x, shift, 1)


def halves(x):
    hi = x.astype(bf16)
    lo = (x - hi.astype(f32)).astype(bf16)
    return hi, lo


def dot(a, b):
    return jnp.dot(a, b, preferred_element_type=f32)


def select_rows(onehot, x):
    hi, lo = halves(x)
    r = dot(onehot, jnp.concatenate([hi, lo], axis=1))
    return r[:, :128] + r[:, 128:]


def to_tiles(ref):
    zero = jnp.zeros((E, 64), f32)
    tiles = []
    for j in range(3):
        high = ref[2 * j + 1] if j < 2 else zero
        tiles.append(jnp.concatenate([ref[2 * j], high], axis=1))
    return tiles


def from_tiles(tiles, ref):
    for j in range(3):
        ref[2 * j] = tiles[j][:, :64]
        if j < 2:
            ref[2 * j + 1] = tiles[j][:, 64:]


def load_tiles(ref):
    return [ref[:, 128 * j : 128 * (j + 1)] for j in range(3)]


def store_tiles(ref, tiles):
    for j in range(3):
        ref[:, 128 * j : 128 * (j + 1)] = tiles[j]


def spread(tiles):
    low = lanes(E) < 64
    back0, back1, back2 = turn(tiles[0], 64), turn(tiles[1], 64), turn(tiles[2], 64)
    ux = jnp.where(low, back0, tiles[0])
    uy = jnp.where(low, tiles[1], back1)
    uz = jnp.where(low, back1, tiles[1])
    p = tiles[2] + back2
    return low, (ux, uy, uz), p


def volume(tiles, table):
    low, speeds, p = spread(tiles)
    fluxes = []
    for a in range(3):
        u = speeds[a]
        c = u + mean_flow if a == 0 else u
        high0 = p if a == 0 else jnp.zeros_like(p)
        parts = [c * tiles[0] + jnp.where(low, u, high0), c * tiles[1], c * tiles[2] + jnp.where(low, u, 0.0)]
        if a == 1:
            parts[1] = parts[1] + jnp.where(low, p, 0.0)
        if a == 2:
            parts[1] = parts[1] + jnp.where(low, 0.0, p)
        fluxes.append(jnp.concatenate(parts, axis=0))
    hi, lo = halves(jnp.concatenate(fluxes, axis=1))
    r = dot(jnp.concatenate([hi, lo], axis=0), table)
    out = r[:96, :128] + (r[:96, 128:] + r[96:, :128])
    return [out[:32], out[32:64], out[64:96]]


def derivative_back(tiles, table):
    hi, lo = halves(jnp.concatenate(tiles, axis=0))
    r = dot(jnp.concatenate([hi, lo], axis=0), table)
    return r[:96, :384] + (r[:96, 384:] + r[96:, :384])


def volume_back(tiles, z):
    low, speeds, _ = spread(tiles)
    one = jnp.where(low, 1.0, 0.0).astype(f32)
    plus = [tiles[0] + one, tiles[1], tiles[2] + one]
    out = [jnp.zeros((E, 128), f32) for _ in range(3)]
    sums = []
    parts = []
    for a in range(3):
        c = speeds[a] + mean_flow if a == 0 else speeds[a]
        za = [z[32 * j : 32 * (j + 1), 128 * a : 128 * (a + 1)] for j in range(3)]
        total = plus[0] * za[0] + plus[1] * za[1] + plus[2] * za[2]
        sums.append(total + turn(total, 64))
        parts.append(za)
        out = [out[j] + c * za[j] for j in range(3)]
    pressure = turn(parts[0][0], 64) + parts[1][1] + turn(parts[2][1], 64)
    out[0] = out[0] + jnp.where(low, 0.0, sums[0])
    out[1] = out[1] + jnp.where(low, sums[1], sums[2])
    out[2] = out[2] + jnp.where(low, pressure, 0.0)
    return out


def traces(tiles):
    lane = lanes(E)
    m = lane & 15
    r, s = m >> 2, m & 3
    base = ((lane >> 4) & 1) * 64
    rows = []
    for f in range(6):
        b = f % 2
        node = (48 * b + m, 16 * r + 12 * b + s, 4 * m + 3 * b)[f // 2]
        index = base + node
        t = jnp.where(
            lane < 32,
            take(tiles[0], index),
            jnp.where(lane < 64, take(tiles[1], index), take(tiles[2], index)),
        )
        rows.append(jnp.where(lane < 80, t, 0.0))
    return jnp.concatenate(rows, axis=0)


def lifted(x):
    lane = lanes(E)
    n = lane & 63
    i, j, k = n >> 4, (n >> 2) & 3, n & 3
    grid = ((i, 4 * j + k), (j, 4 * i + k), (k, 4 * i + j))
    tiles = []
    for tile in range(3):
        v = 2 * tile + (lane >> 6)
        total = jnp.zeros((E, 128), f32)
        for a in range(3):
            layer, m = grid[a]
            index = v * 16 + m
            first = take(x[64 * a : 64 * a + 32], index)
            last = take(x[64 * a + 32 : 64 * a + 64], index)
            total = total + jnp.where(layer == 0, first, jnp.where(layer == 3, last, 0.0))
        tiles.append(total)
    return tiles


class Faces:
    def __init__(self):
        row = lax.broadcasted_iota(i32, (F, 128), 0)
        lane = lanes(F)
        self.v = lane >> 4
        m = lane & 15
        axis = row >> 6
        self.sign = jnp.where((row >> 5) & 1 == 1, 1.0, -1.0).astype(f32)
        self.drift = jnp.where(axis == 0, mean_flow, 0.0).astype(f32)
        self.normal = self.v == axis + 1
        self.normal_index = (axis + 1) * 16 + m
        self.pressure_index = 64 + m
        self.m = m
        self.ends = (self.v == 0) | (self.v == 4)
        self.ones = jnp.where(self.ends, 1.0, 0.0).astype(f32)
        self.axis = axis

    def flux(self, x):
        u = take(x, self.normal_index)
        p = take(x, self.pressure_index)
        return self.sign * (
            (self.drift + u) * x + jnp.where(self.ends, u, 0.0) + jnp.where(self.normal, p, 0.0)
        )

    def flux_back(self, x, w):
        u = take(x, self.normal_index)
        n = take(w, self.normal_index)
        h = over_fields((x + self.ones) * w)
        return self.sign * (
            (self.drift + u) * w + jnp.where(self.v == 4, n, 0.0) + jnp.where(self.normal, h, 0.0)
        )

    def shifted(self, d):
        target = self.v + d
        target = jnp.where(target >= 5, target - 5, target)
        return target, jnp.where(self.v < 5, target * 16 + self.m, 16 * self.v + self.m)

    def hessian(self, d, y):
        target, index = self.shifted(d)
        other = take(y, index)
        inside = self.v < 5
        half = jnp.where(self.normal, other, 0.0)
        half = half + jnp.where(inside & (target == self.axis + 1), y, 0.0)
        return -0.5 * self.sign * half

    def mirror(self, x):
        return jnp.where(self.normal, -x, x)


def over_fields(h):
    h = h + turn(h, 16)
    h = h + turn(h, 32)
    return h + turn(h, 64)


def column_of(table_ref):
    x = table_ref[...].astype(f32)
    x = jnp.concatenate([x, jnp.zeros((2, E), f32)], axis=0)
    t = jnp.transpose(x)
    return jnp.concatenate([t[:, f : f + 1] for f in range(6)], axis=0).astype(i32)


def row_of(table_ref):
    return jnp.concatenate([table_ref[f : f + 1, :] for f in range(6)], axis=1)


def slot_column(send):
    x = jnp.broadcast_to(send.astype(f32), (8, S))
    return jnp.transpose(x)[:, :1].astype(i32)


def onehot(rows, columns, first, second):
    return jnp.where(first == second, 1.0, 0.0).astype(bf16)


def faces_from_columns(ext_col):
    return onehot(F, F, ext_col, lax.broadcasted_iota(i32, (F, F), 1))


def columns_from_faces(ext_row):
    return onehot(F, F, ext_row, lax.broadcasted_iota(i32, (F, F), 0))


def faces_from_slots(ext_col):
    return onehot(F, S, ext_col - F, lax.broadcasted_iota(i32, (F, S), 1))


def slots_from_faces(ext_row):
    return onehot(S, F, ext_row - F, lax.broadcasted_iota(i32, (S, F), 0))


def slots_from_columns(send_col):
    return onehot(S, F, send_col, lax.broadcasted_iota(i32, (S, F), 1))


def columns_from_slots(send_row):
    return onehot(F, S, send_row, lax.broadcasted_iota(i32, (F, S), 0))


def orientation(perm_col):
    lane = lanes(F)
    m = lane & 15
    r, s = m >> 2, m & 3
    k = jnp.broadcast_to(perm_col, (F, 128))
    flip_r = (k & 1) == 1
    flip_s = (k & 2) == 2
    swap = (k & 4) == 4
    r1 = jnp.where(flip_r, 3 - r, r)
    s1 = jnp.where(flip_s, 3 - s, s)
    base = lane - m
    index = base + jnp.where(swap, 4 * s1 + r1, 4 * r1 + s1)
    r2 = jnp.where(swap, s, r)
    s2 = jnp.where(swap, r, s)
    r2 = jnp.where(flip_r, 3 - r2, r2)
    s2 = jnp.where(flip_s, 3 - s2, s2)
    inverse = base + 4 * r2 + s2
    return index, inverse


def peer_tables(send_ref, ext_ref):
    odd = (lax.axis_index("dom") & 1) == 1
    send = send_ref[...]
    swapped = jnp.concatenate([send[:, 2 * G :], send[:, G : 2 * G], send[:, :G]], axis=1)
    send = jnp.where(odd, send, swapped)

    def reordered(table):
        slot = table - F
        turned = jnp.where(slot < G, slot + 2 * G, jnp.where(slot >= 2 * G, slot - 2 * G, slot))
        turned = jnp.where((slot >= 0) & (slot < S), turned + F, table)
        return jnp.where(odd, turned, table)

    return send, reordered(column_of(ext_ref)), reordered(row_of(ext_ref))


def packed(x):
    tail = lanes(F) >= 80
    first = jnp.where(tail, turn(x, 80), 0.0)
    second = jnp.where(tail, turn(x, 32), 0.0)
    return jnp.concatenate([first, second], axis=1).astype(bf16)


def unpacked(g):
    lane = lanes(F)
    first = jnp.where(lane < 48, turn(g[:, :128], 48), 0.0)
    second = jnp.where((lane >= 48) & (lane < 80), turn(g[:, 128:256], 96), 0.0)
    return first + second


def exterior(faces, wall, index, onehot_local, t):
    return jnp.where(wall, faces.mirror(t), take(select_rows(onehot_local, t), index))


def pack_kernel(state_ref, final_ref, send_ref, ext_ref, perm_ref,
                out_ref, q_ref, w_ref, t_ref, lam_ref, send_slots_ref, back_slots_ref, inverse_ref):
    faces = Faces()
    q = to_tiles(state_ref)
    w = to_tiles(final_ref)
    store_tiles(q_ref, q)
    store_tiles(w_ref, w)
    t = traces(q)
    lam = lift_factor * traces(w)
    t_ref[...] = t
    lam_ref[...] = lam
    send, _, ext_row = peer_tables(send_ref, ext_ref)
    send_slots = slots_from_columns(slot_column(send))
    back_slots = slots_from_faces(ext_row)
    send_slots_ref[...] = send_slots
    back_slots_ref[...] = back_slots
    _, inverse = orientation(column_of(perm_ref))
    inverse_ref[...] = inverse
    y = take(lam, inverse)
    diagonal = jnp.where(faces.normal, -faces.sign * y, 0.0)
    first = y - 0.5 * faces.flux_back(jnp.zeros_like(y), y) + turn(diagonal, 64)
    stack = jnp.concatenate([x.astype(bf16) for x in (first, faces.hessian(1, y), faces.hessian(2, y))], axis=1)
    back = dot(back_slots, stack)
    forward = dot(send_slots, packed(t))
    whole = jnp.concatenate([back[:, :128], back[:, 128:] + forward], axis=1).astype(bf16)
    for o in range(3):
        for peer in range(8):
            at = G * o + 16 * peer
            out_ref[peer, o] = whole[at : at + 16]


def first_local_kernel(q_ref, w_ref, t_ref, send_ref, ext_ref, perm_ref, forward_ref, backward_ref,
                       base_ref, z_ref, from_slots_ref, to_columns_ref, local_ref, local_back_ref, index_ref, kind_ref):
    faces = Faces()
    send, ext_col, ext_row = peer_tables(send_ref, ext_ref)
    index, _ = orientation(column_of(perm_ref))
    index_ref[...] = index
    ext_wide = jnp.broadcast_to(ext_col, (F, 128))
    wall = ext_wide == F + S
    kind_ref[...] = jnp.where(wall, 2, jnp.where(ext_wide >= F, 1, 0))
    from_slots_ref[...] = faces_from_slots(ext_col)
    to_columns_ref[...] = columns_from_slots(send)
    local = faces_from_columns(ext_col)
    local_ref[...] = local
    local_back_ref[...] = columns_from_faces(ext_row)
    q = load_tiles(q_ref)
    t = t_ref[...]
    x = exterior(faces, wall, index, local, t)
    jump = 0.5 * (faces.flux(t) - faces.flux(x)) + (x - t)
    faced = lifted(lift_factor * jump)
    inner = volume(q, forward_ref[...])
    store_tiles(base_ref, [q[j] + step_size * (inner[j] + faced[j]) for j in range(3)])
    z_ref[...] = derivative_back(load_tiles(w_ref), backward_ref[...])


def middle_kernel(base_ref, w_ref, lam_ref, z_ref, chip_ref, own_ref, next_ref,
                  from_slots_ref, to_columns_ref, local_ref, local_back_ref, send_slots_ref, back_slots_ref,
                  index_ref, inverse_ref, kind_ref,
                  out_ref, q1_ref, w1_ref, t1_ref, x1_ref, lam1_ref):
    faces = Faces()
    index = index_ref[...]
    inverse = inverse_ref[...]
    kind = kind_ref[...]
    wall = kind == 2
    arrived = jnp.concatenate(
        [chip_ref[...].reshape(G, 384), own_ref[:, 1].reshape(G, 384), next_ref[...].reshape(G, 384)], axis=0)
    xr = take(unpacked(dot(from_slots_ref[...], arrived[:, 128:])), index)
    sums = dot(to_columns_ref[...], arrived)
    faced = lifted((lift_factor * step_size) * (xr - 0.5 * faces.flux(xr)))
    base = load_tiles(base_ref)
    q1 = [base[j] + faced[j] for j in range(3)]
    store_tiles(q1_ref, q1)
    t1 = traces(q1)
    t1_ref[...] = t1
    forward = dot(send_slots_ref[...], packed(t1))
    lam = lam_ref[...]
    x1 = exterior(faces, wall, index, local_ref[...], t1)
    x1_ref[...] = x1
    bar = jnp.where(kind == 1, 0.0, lam - 0.5 * faces.flux_back(x1, lam))
    total = 0.5 * faces.flux_back(t1, lam) - lam + jnp.where(wall, faces.mirror(bar), 0.0)
    total = total + select_rows(local_back_ref[...], take(bar, inverse))
    lane = lanes(F)
    sent = t1.astype(bf16).astype(f32)
    h1, h2 = sums[:, 128:256], sums[:, 256:]
    _, index1 = faces.shifted(1)
    _, index2 = faces.shifted(2)
    _, index3 = faces.shifted(3)
    _, index4 = faces.shifted(4)
    through = sums[:, :128] + h1 * take(sent, index1) + h2 * take(sent, index2)
    through = through + take(h1, index4) * take(sent, index4) + take(h2, index3) * take(sent, index3)
    through = through + jnp.where((lane >= 16) & (lane < 64), turn(sums[:, :128], 64) * sent, 0.0)
    total = total + jnp.where(lane < 80, through, 0.0)
    inner = volume_back(q1, z_ref[...])
    faced = lifted(total)
    w = load_tiles(w_ref)
    w1 = [0.5 * w[j] + (0.5 * step_size) * (inner[j] + faced[j]) for j in range(3)]
    store_tiles(w1_ref, w1)
    lam1 = lift_factor * traces(w1)
    lam1_ref[...] = lam1
    y = take(lam1 - 0.5 * faces.flux_back(xr, lam1), inverse)
    back = dot(back_slots_ref[...], y.astype(bf16))
    main = (back + forward[:, :128]).astype(bf16)
    tail = [turn(forward[G * o : G * (o + 1), 128:], 48 + 32 * o) for o in range(3)]
    shared = (tail[0] + tail[1] + tail[2]).astype(bf16)
    for peer in range(8):
        at = 16 * peer
        out_ref[peer, 0] = main[at : at + 16]
        out_ref[peer, 1] = shared[at : at + 16]
        out_ref[peer, 2] = main[2 * G + at : 2 * G + at + 16]
        out_ref[peer, 3] = main[G + at : G + at + 16]


def second_local_kernel(q_ref, w_ref, t_ref, q1_ref, w1_ref, t1_ref, x1_ref, lam1_ref,
                        local_ref, local_back_ref, index_ref, inverse_ref, kind_ref,
                        forward_ref, backward_ref, end_ref, start_ref):
    faces = Faces()
    index = index_ref[...]
    inverse = inverse_ref[...]
    kind = kind_ref[...]
    wall = kind == 2
    q = load_tiles(q_ref)
    q1 = load_tiles(q1_ref)
    t1 = t1_ref[...]
    x1 = x1_ref[...]
    jump = 0.5 * (faces.flux(t1) - faces.flux(x1)) + (x1 - t1)
    faced = lifted(lift_factor * jump)
    inner = volume(q1, forward_ref[...])
    store_tiles(end_ref, [0.5 * q[j] + 0.5 * (q1[j] + step_size * (inner[j] + faced[j])) for j in range(3)])
    t = t_ref[...]
    lam1 = lam1_ref[...]
    x = exterior(faces, wall, index, local_ref[...], t)
    bar = jnp.where(kind == 1, 0.0, lam1 - 0.5 * faces.flux_back(x, lam1))
    total = 0.5 * faces.flux_back(t, lam1) - lam1 + jnp.where(wall, faces.mirror(bar), 0.0)
    total = total + select_rows(local_back_ref[...], take(bar, inverse))
    w = load_tiles(w_ref)
    w1 = load_tiles(w1_ref)
    inner = volume_back(q, derivative_back(w1, backward_ref[...]))
    faced = lifted(total)
    store_tiles(start_ref, [0.5 * w[j] + w1[j] + step_size * (inner[j] + faced[j]) for j in range(3)])


def last_kernel(end_base_ref, start_base_ref, chip_ref, own_ref, next_ref, from_slots_ref, to_columns_ref, index_ref,
                end_ref, start_ref):
    faces = Faces()
    main = jnp.concatenate(
        [chip_ref[:, 0].reshape(G, 128), own_ref[:, 3].reshape(G, 128), next_ref[:, 1].reshape(G, 128)], axis=0)
    lane = lanes(G)
    zero = jnp.zeros((G, 128), bf16)
    shared = jnp.concatenate([
        jnp.where(lane < 32, chip_ref[:, 1].reshape(G, 128), zero),
        jnp.where((lane >= 32) & (lane < 64), own_ref[:, 1].reshape(G, 128), zero),
        jnp.where((lane >= 64) & (lane < 96), next_ref[:, 0].reshape(G, 128), zero)], axis=0)
    g = dot(from_slots_ref[...], jnp.concatenate([main, shared], axis=1))
    lane = lanes(F)
    x = jnp.where(lane < 48, turn(g[:, :128], 48), 0.0)
    high = g[:, 128:]
    high = turn(high, 48) + turn(high, 16) + turn(high, 112)
    x = x + jnp.where((lane >= 48) & (lane < 80), high, 0.0)
    xr = take(x, index_ref[...])
    faced = lifted((0.5 * step_size * lift_factor) * (xr - 0.5 * faces.flux(xr)))
    base = load_tiles(end_base_ref)
    from_tiles([base[j] + faced[j] for j in range(3)], end_ref)
    bar = dot(to_columns_ref[...], main)
    bar = jnp.where(lane < 80, bar, 0.0)
    faced = lifted(step_size * bar)
    base = load_tiles(start_base_ref)
    from_tiles([base[j] + faced[j] for j in range(3)], start_ref)


def shape(*dims, dtype=f32):
    return jax.ShapeDtypeStruct(dims, dtype)


def call(kernel, outs, *args):
    return pl.pallas_call(
        kernel,
        out_shape=outs,
        cost_estimate=pl.CostEstimate(flops=200_000_000, bytes_accessed=1_000_000, transcendentals=0),
        compiler_params=pltpu.CompilerParams(vmem_limit_bytes=32 * 1024 * 1024),
    )(*args)


def all_peers(whole):
    return lax.all_to_all(whole, "sub", split_axis=0, concat_axis=0, tiled=True)


def next_partner(value):
    count = lax.axis_size("dom")
    pairs = [(d, (d + 1) % count if d % 2 else (d - 1) % count) for d in range(count)]
    return lax.ppermute(value, "dom", pairs)


def chip_partner(value):
    return lax.ppermute(value, "dom", [(d, d ^ 1) for d in range(lax.axis_size("dom"))])


def shards(state, adjoint_final, send_slot, ext_index, ext_perm):
    forward, backward = derivative_operands()
    forward, backward = jnp.asarray(forward), jnp.asarray(backward)
    state, adjoint_final = jnp.swapaxes(state, 1, 2), jnp.swapaxes(adjoint_final, 1, 2)
    node = shape(E, 384)
    face = shape(F, 128)
    index_face = shape(F, 128, dtype=i32)

    out, q, w, t, lam, send_slots, back_slots, inverse = call(
        pack_kernel,
        (shape(8, 3, 16, 384, dtype=bf16), node, node, face, face,
         shape(S, F, dtype=bf16), shape(S, F, dtype=bf16), index_face),
        state, adjoint_final, send_slot, ext_index, ext_perm)
    arrived = all_peers(out)
    base, z, from_slots, to_columns, local, local_back, index, kind = call(
        first_local_kernel,
        (node, shape(96, 384), shape(F, S, dtype=bf16), shape(F, S, dtype=bf16),
         shape(F, F, dtype=bf16), shape(F, F, dtype=bf16), index_face, index_face),
        q, w, t, send_slot, ext_index, ext_perm, forward, backward)
    from_next = next_partner(arrived[:, 2])
    from_chip = chip_partner(arrived[:, 0])
    out, q1, w1, t1, x1, lam1 = call(
        middle_kernel, (shape(8, 4, 16, 128, dtype=bf16), node, node, face, face, face),
        base, w, lam, z, from_chip, arrived, from_next,
        from_slots, to_columns, local, local_back, send_slots, back_slots, index, inverse, kind)
    arrived = all_peers(out)
    end_base, start_base = call(
        second_local_kernel, (node, node),
        q, w, t, q1, w1, t1, x1, lam1, local, local_back, index, inverse, kind, forward, backward)
    from_next = next_partner(arrived[:, 1:3])
    from_chip = chip_partner(arrived[:, 0:2])
    out = shape(5, E, 64)
    end, start = call(
        last_kernel, (out, out),
        end_base, start_base, from_chip, arrived, from_next, from_slots, to_columns, index)
    return jnp.swapaxes(end, 1, 2), jnp.swapaxes(start, 1, 2)


def solution(mesh):
    return jax.shard_map(
        shards,
        mesh=mesh,
        in_specs=(
            P(None, None, ("dom", "sub")),
            P(None, None, ("dom", "sub")),
            P(("dom", "sub"), None),
            P(None, ("dom", "sub")),
            P(None, ("dom", "sub")),
        ),
        out_specs=(P(None, None, ("dom", "sub")), P(None, None, ("dom", "sub"))),
        check_vma=False,
    )
```

```python
import jax
import jax.numpy as jnp
import numpy as np
import ml_dtypes
from jax import lax
from jax.experimental import pallas as pl
from jax.experimental.pallas import tpu as pltpu
from jax.sharding import PartitionSpec as P

step_size = 0.02
mean_flow = 0.3
lift_factor = 12.0

E = 32
F = 192
S = 384
G = 128
f32 = jnp.float32
bf16 = jnp.bfloat16
i32 = jnp.int32


def derivative_table():
    points = np.array([-1.0, -1.0 / np.sqrt(5.0), 1.0 / np.sqrt(5.0), 1.0])
    products = np.array(
        [np.prod([points[t] - points[s] for s in range(4) if s != t]) for t in range(4)]
    )
    result = np.zeros((4, 4))
    for t in range(4):
        for s in range(4):
            if t != s:
                result[t, s] = products[t] / (products[s] * (points[t] - points[s]))
        result[t, t] = -np.sum(result[t])
    return result.astype(np.float32)


def halves_of(matrix):
    hi = matrix.astype(ml_dtypes.bfloat16)
    lo = (matrix - hi.astype(np.float32)).astype(ml_dtypes.bfloat16)
    return hi, lo


def derivative_operands():
    d = -2.0 * derivative_table()
    eye = np.eye(4, dtype=np.float32)
    along = [
        np.kron(d, np.kron(eye, eye)),
        np.kron(eye, np.kron(d, eye)),
        np.kron(eye, np.kron(eye, d)),
    ]
    two = [np.kron(np.eye(2, dtype=np.float32), a).astype(np.float32) for a in along]
    hi, lo = halves_of(np.concatenate([t.T for t in two], axis=0))
    forward = np.concatenate([hi, lo], axis=1)
    hi, lo = halves_of(np.concatenate(two, axis=1))
    backward = np.concatenate([hi, lo], axis=1)
    return forward, backward


def lanes(rows=1):
    return lax.broadcasted_iota(i32, (rows, 128), 1)


def take(x, index):
    return jnp.take_along_axis(x, jnp.broadcast_to(index, x.shape), axis=1)


def mask(condition):
    return jnp.where(condition, 1.0, 0.0).astype(f32)


def turn(x, shift):
    return pltpu.roll(x, shift, 1)


def halves(x):
    hi = x.astype(bf16)
    lo = (x - hi.astype(f32)).astype(bf16)
    return hi, lo


def dot(a, b):
    return jnp.dot(a, b, preferred_element_type=f32)


def select_rows(onehot, x):
    hi, lo = halves(x)
    r = dot(onehot, jnp.concatenate([hi, lo], axis=1))
    return r[:, :128] + r[:, 128:]


def to_tiles(ref):
    zero = jnp.zeros((E, 64), f32)
    tiles = []
    for j in range(3):
        high = ref[2 * j + 1] if j < 2 else zero
        tiles.append(jnp.concatenate([ref[2 * j], high], axis=1))
    return tiles


def from_tiles(tiles, ref):
    for j in range(3):
        ref[2 * j] = tiles[j][:, :64]
        if j < 2:
            ref[2 * j + 1] = tiles[j][:, 64:]


def load_tiles(ref):
    return [ref[:, 128 * j : 128 * (j + 1)] for j in range(3)]


def store_tiles(ref, tiles):
    for j in range(3):
        ref[:, 128 * j : 128 * (j + 1)] = tiles[j]


def spread(tiles):
    low = lanes(E) < 64
    back0, back1, back2 = turn(tiles[0], 64), turn(tiles[1], 64), turn(tiles[2], 64)
    ux = jnp.where(low, back0, tiles[0])
    uy = jnp.where(low, tiles[1], back1)
    uz = jnp.where(low, back1, tiles[1])
    p = tiles[2] + back2
    return low, (ux, uy, uz), p


def volume(tiles, table):
    low, speeds, p = spread(tiles)
    fluxes = []
    for a in range(3):
        u = speeds[a]
        c = u + mean_flow if a == 0 else u
        high0 = p if a == 0 else jnp.zeros_like(p)
        parts = [c * tiles[0] + jnp.where(low, u, high0), c * tiles[1], c * tiles[2] + jnp.where(low, u, 0.0)]
        if a == 1:
            parts[1] = parts[1] + jnp.where(low, p, 0.0)
        if a == 2:
            parts[1] = parts[1] + jnp.where(low, 0.0, p)
        fluxes.append(jnp.concatenate(parts, axis=0))
    hi, lo = halves(jnp.concatenate(fluxes, axis=1))
    r = dot(jnp.concatenate([hi, lo], axis=0), table)
    out = r[:96, :128] + (r[:96, 128:] + r[96:, :128])
    return [out[:32], out[32:64], out[64:96]]


def derivative_back(tiles, table):
    hi, lo = halves(jnp.concatenate(tiles, axis=0))
    r = dot(jnp.concatenate([hi, lo], axis=0), table)
    return r[:96, :384] + (r[:96, 384:] + r[96:, :384])


def volume_back(tiles, z):
    low, speeds, _ = spread(tiles)
    one = jnp.where(low, 1.0, 0.0).astype(f32)
    plus = [tiles[0] + one, tiles[1], tiles[2] + one]
    out = [jnp.zeros((E, 128), f32) for _ in range(3)]
    sums = []
    parts = []
    for a in range(3):
        c = speeds[a] + mean_flow if a == 0 else speeds[a]
        za = [z[32 * j : 32 * (j + 1), 128 * a : 128 * (a + 1)] for j in range(3)]
        total = plus[0] * za[0] + plus[1] * za[1] + plus[2] * za[2]
        sums.append(total + turn(total, 64))
        parts.append(za)
        out = [out[j] + c * za[j] for j in range(3)]
    pressure = turn(parts[0][0], 64) + parts[1][1] + turn(parts[2][1], 64)
    out[0] = out[0] + jnp.where(low, 0.0, sums[0])
    out[1] = out[1] + jnp.where(low, sums[1], sums[2])
    out[2] = out[2] + jnp.where(low, pressure, 0.0)
    return out


def traces(tiles):
    lane = lanes()
    wide = lanes(E)
    m = lane & 15
    r, s = m >> 2, m & 3
    base = ((lane >> 4) & 1) * 64
    rows = []
    for f in range(6):
        b = f % 2
        index = base + (48 * b + m, 16 * r + 12 * b + s, 4 * m + 3 * b)[f // 2]
        index = jnp.where(lane < 80, index, 64)
        t = jnp.where(
            wide < 32,
            take(tiles[0], index),
            jnp.where(wide < 64, take(tiles[1], index), take(tiles[2], index)),
        )
        rows.append(t)
    return jnp.concatenate(rows, axis=0)


def lifted(x):
    lane = lanes()
    wide = lanes(E)
    n = lane & 63
    i, j, k = n >> 4, (n >> 2) & 3, n & 3
    places = (4 * j + k, 4 * i + k, 4 * i + j)
    layers = ((wide >> 4) & 3, (wide >> 2) & 3, wide & 3)
    tiles = []
    for tile in range(3):
        v = 2 * tile + (lane >> 6)
        total = None
        for a in range(3):
            index = v * 16 + places[a]
            first = take(x[64 * a : 64 * a + 32], index)
            last = take(x[64 * a + 32 : 64 * a + 64], index)
            part = jnp.where(layers[a] == 0, first, jnp.where(layers[a] == 3, last, 0.0))
            total = part if total is None else total + part
        tiles.append(total)
    return tiles


def by_axis(function, *arrays):
    return jnp.concatenate(
        [function(a, *[x[64 * a : 64 * (a + 1)] for x in arrays]) for a in range(3)], axis=0)


def signed(x):
    return jnp.concatenate([-x[:32], x[32:]], axis=0)


class Faces:
    def __init__(self):
        lane = lanes()
        self.v = lane >> 4
        self.m = lane & 15
        self.ends = mask((self.v == 0) | (self.v == 4))
        self.last = mask(self.v == 4)
        self.normal = [mask(self.v == a + 1) for a in range(3)]
        self.normal_index = [(a + 1) * 16 + self.m for a in range(3)]
        self.pressure_index = 64 + self.m

    def flux(self, x):
        def along(a, x):
            u = take(x, self.normal_index[a])
            p = take(x, self.pressure_index)
            c = u + mean_flow if a == 0 else u
            return signed(c * x + self.ends * u + self.normal[a] * p)

        return by_axis(along, x)

    def flux_back(self, x, w):
        def along(a, x, w):
            u = take(x, self.normal_index[a])
            n = take(w, self.normal_index[a])
            c = u + mean_flow if a == 0 else u
            h = over_fields((x + self.ends) * w)
            return signed(c * w + self.last * n + self.normal[a] * h)

        return by_axis(along, x, w)

    def rest_back(self, w):
        def along(a, w):
            n = take(w, self.normal_index[a])
            h = over_fields(self.ends * w)
            part = self.last * n + self.normal[a] * h
            return signed(mean_flow * w + part if a == 0 else part)

        return by_axis(along, w)

    def shifted(self, d):
        target = self.v + d
        target = jnp.where(target >= 5, target - 5, target)
        return target, jnp.where(self.v < 5, target * 16 + self.m, 16 * self.v + self.m)

    def hessian(self, d, y):
        target, index = self.shifted(d)

        def along(a, y):
            back = mask((self.v < 5) & (target == a + 1))
            return signed(-0.5 * (self.normal[a] * take(y, index) + back * y))

        return by_axis(along, y)

    def mirror(self, x):
        return by_axis(lambda a, x: x * (1.0 - 2.0 * self.normal[a]), x)


def over_fields(h):
    h = h + turn(h, 16)
    h = h + turn(h, 32)
    return h + turn(h, 64)


def column_of(table_ref):
    x = table_ref[...].astype(f32)
    x = jnp.concatenate([x, jnp.zeros((2, E), f32)], axis=0)
    t = jnp.transpose(x)
    return jnp.concatenate([t[:, f : f + 1] for f in range(6)], axis=0).astype(i32)


def row_of(table_ref):
    return jnp.concatenate([table_ref[f : f + 1, :] for f in range(6)], axis=1)


def slot_column(send):
    x = jnp.broadcast_to(send.astype(f32), (8, S))
    return jnp.transpose(x)[:, :1].astype(i32)


def onehot(rows, columns, first, second):
    return jnp.where(first == second, 1.0, 0.0).astype(bf16)


def faces_from_columns(ext_col):
    return onehot(F, F, ext_col, lax.broadcasted_iota(i32, (F, F), 1))


def columns_from_faces(ext_row):
    return onehot(F, F, ext_row, lax.broadcasted_iota(i32, (F, F), 0))


def faces_from_slots(ext_col):
    return onehot(F, S, ext_col - F, lax.broadcasted_iota(i32, (F, S), 1))


def slots_from_faces(ext_row):
    return onehot(S, F, ext_row - F, lax.broadcasted_iota(i32, (S, F), 0))


def slots_from_columns(send_col):
    return onehot(S, F, send_col, lax.broadcasted_iota(i32, (S, F), 1))


def columns_from_slots(send_row):
    return onehot(F, S, send_row, lax.broadcasted_iota(i32, (F, S), 0))


def orientation(perm_col):
    lane = lanes(F)
    m = lane & 15
    crossed = lane - m + ((m & 3) * 4 + (m >> 2))
    k = jnp.broadcast_to(perm_col, (F, 128))
    flips = (k & 1) * 12 + ((k & 2) >> 1) * 3
    crossed_flips = (k & 1) * 3 + ((k & 2) >> 1) * 12
    swap = (k & 4) == 4
    place = jnp.where(swap, crossed, lane)
    return place ^ jnp.where(swap, crossed_flips, flips), place ^ flips


def peer_tables(send_ref, ext_ref):
    odd = (lax.axis_index("dom") & 1) == 1
    send = send_ref[...]
    swapped = jnp.concatenate([send[:, 2 * G :], send[:, G : 2 * G], send[:, :G]], axis=1)
    send = jnp.where(odd, send, swapped)

    def reordered(table):
        slot = table - F
        turned = jnp.where(slot < G, slot + 2 * G, jnp.where(slot >= 2 * G, slot - 2 * G, slot))
        turned = jnp.where((slot >= 0) & (slot < S), turned + F, table)
        return jnp.where(odd, turned, table)

    return send, reordered(column_of(ext_ref)), reordered(row_of(ext_ref))


def packed(x):
    tail = lanes(F) >= 80
    first = jnp.where(tail, turn(x, 80), 0.0)
    second = jnp.where(tail, turn(x, 32), 0.0)
    return jnp.concatenate([first, second], axis=1).astype(bf16)


def unpacked(g):
    lane = lanes(F)
    first = jnp.where(lane < 48, turn(g[:, :128], 48), 0.0)
    second = jnp.where((lane >= 48) & (lane < 80), turn(g[:, 128:256], 96), 0.0)
    return first + second


def exterior(faces, wall, index, onehot_local, t):
    return jnp.where(wall, faces.mirror(t), take(select_rows(onehot_local, t), index))


def pack_kernel(state_hbm, final_hbm, send_hbm, ext_hbm, perm_hbm,
                out_ref, q_ref, w_ref, t_ref, lam_ref, send_slots_ref, back_slots_ref, inverse_ref,
                send_ref, ext_ref, perm_ref, state_ref, final_ref, sems):
    pairs = ((send_hbm, send_ref), (ext_hbm, ext_ref), (perm_hbm, perm_ref), (final_hbm, final_ref), (state_hbm, state_ref))
    copies = [pltpu.make_async_copy(a, b, sems.at[i]) for i, (a, b) in enumerate(pairs)]
    for copy in copies:
        copy.start()
    faces = Faces()
    for copy in copies[:3]:
        copy.wait()
    send, _, ext_row = peer_tables(send_ref, ext_ref)
    send_slots = slots_from_columns(slot_column(send))
    back_slots = slots_from_faces(ext_row)
    send_slots_ref[...] = send_slots
    back_slots_ref[...] = back_slots
    _, inverse = orientation(column_of(perm_ref))
    inverse_ref[...] = inverse
    for copy in copies[3:]:
        copy.wait()
    q = to_tiles(state_ref)
    w = to_tiles(final_ref)
    store_tiles(q_ref, q)
    store_tiles(w_ref, w)
    t = traces(q)
    lam = lift_factor * traces(w)
    t_ref[...] = t
    lam_ref[...] = lam
    y = take(lam, inverse)
    diagonal = by_axis(lambda a, y: signed(-faces.normal[a] * y), y)
    first = y - 0.5 * faces.rest_back(y) + turn(diagonal, 64)
    stack = jnp.concatenate([x.astype(bf16) for x in (first, faces.hessian(1, y), faces.hessian(2, y))], axis=1)
    back = dot(back_slots, stack)
    forward = dot(send_slots, packed(t))
    whole = jnp.concatenate([back[:, :128], back[:, 128:] + forward], axis=1).astype(bf16)
    for o in range(3):
        for peer in range(8):
            at = G * o + 16 * peer
            out_ref[peer, o] = whole[at : at + 16]


def first_local_kernel(q_ref, w_ref, t_ref, send_ref, ext_ref, perm_ref, forward_ref, backward_ref,
                       base_ref, z_ref, from_slots_ref, to_columns_ref, local_ref, local_back_ref, index_ref, kind_ref):
    faces = Faces()
    send, ext_col, ext_row = peer_tables(send_ref, ext_ref)
    index, _ = orientation(column_of(perm_ref))
    index_ref[...] = index
    ext_wide = jnp.broadcast_to(ext_col, (F, 128))
    wall = ext_wide == F + S
    kind_ref[...] = jnp.where(wall, 2, jnp.where(ext_wide >= F, 1, 0))
    from_slots_ref[...] = faces_from_slots(ext_col)
    to_columns_ref[...] = columns_from_slots(send)
    local = faces_from_columns(ext_col)
    local_ref[...] = local
    local_back_ref[...] = columns_from_faces(ext_row)
    q = load_tiles(q_ref)
    t = t_ref[...]
    x = exterior(faces, wall, index, local, t)
    jump = 0.5 * (faces.flux(t) - faces.flux(x)) + (x - t)
    faced = lifted(lift_factor * jump)
    inner = volume(q, forward_ref[...])
    store_tiles(base_ref, [q[j] + step_size * (inner[j] + faced[j]) for j in range(3)])
    z_ref[...] = derivative_back(load_tiles(w_ref), backward_ref[...])


def middle_kernel(base_ref, w_ref, lam_ref, z_ref, chip_ref, own_ref, next_ref,
                  from_slots_ref, to_columns_ref, local_ref, local_back_ref, send_slots_ref, back_slots_ref,
                  index_ref, inverse_ref, kind_ref,
                  out_ref, q1_ref, w1_ref, t1_ref, x1_ref, lam1_ref):
    faces = Faces()
    index = index_ref[...]
    inverse = inverse_ref[...]
    kind = kind_ref[...]
    wall = kind == 2
    arrived = jnp.concatenate(
        [chip_ref[...].reshape(G, 384), own_ref[:, 1].reshape(G, 384), next_ref[...].reshape(G, 384)], axis=0)
    xr = take(unpacked(dot(from_slots_ref[...], arrived[:, 128:])), index)
    sums = dot(to_columns_ref[...], arrived)
    faced = lifted((lift_factor * step_size) * (xr - 0.5 * faces.flux(xr)))
    base = load_tiles(base_ref)
    q1 = [base[j] + faced[j] for j in range(3)]
    store_tiles(q1_ref, q1)
    t1 = traces(q1)
    t1_ref[...] = t1
    forward = dot(send_slots_ref[...], packed(t1))
    lam = lam_ref[...]
    x1 = exterior(faces, wall, index, local_ref[...], t1)
    x1_ref[...] = x1
    bar = jnp.where(kind == 1, 0.0, lam - 0.5 * faces.flux_back(x1, lam))
    total = 0.5 * faces.flux_back(t1, lam) - lam + jnp.where(wall, faces.mirror(bar), 0.0)
    total = total + select_rows(local_back_ref[...], take(bar, inverse))
    lane = lanes()
    sent = t1.astype(bf16).astype(f32)
    h1, h2 = sums[:, 128:256], sums[:, 256:]
    _, index1 = faces.shifted(1)
    _, index2 = faces.shifted(2)
    _, index3 = faces.shifted(3)
    _, index4 = faces.shifted(4)
    through = sums[:, :128] + h1 * take(sent, index1) + h2 * take(sent, index2)
    through = through + take(h1, index4) * take(sent, index4) + take(h2, index3) * take(sent, index3)
    through = through + mask((lane >= 16) & (lane < 64)) * turn(sums[:, :128], 64) * sent
    total = total + mask(lane < 80) * through
    inner = volume_back(q1, z_ref[...])
    faced = lifted(total)
    w = load_tiles(w_ref)
    w1 = [0.5 * w[j] + (0.5 * step_size) * (inner[j] + faced[j]) for j in range(3)]
    store_tiles(w1_ref, w1)
    lam1 = lift_factor * traces(w1)
    lam1_ref[...] = lam1
    y = take(lam1 - 0.5 * faces.flux_back(xr, lam1), inverse)
    back = dot(back_slots_ref[...], y.astype(bf16))
    main = (back + forward[:, :128]).astype(bf16)
    tail = [turn(forward[G * o : G * (o + 1), 128:], 48 + 32 * o) for o in range(3)]
    shared = (tail[0] + tail[1] + tail[2]).astype(bf16)
    for peer in range(8):
        at = 16 * peer
        out_ref[peer, 0] = main[at : at + 16]
        out_ref[peer, 1] = shared[at : at + 16]
        out_ref[peer, 2] = main[2 * G + at : 2 * G + at + 16]
        out_ref[peer, 3] = main[G + at : G + at + 16]


def second_local_kernel(q_ref, w_ref, t_ref, q1_ref, w1_ref, t1_ref, x1_ref, lam1_ref,
                        local_ref, local_back_ref, index_ref, inverse_ref, kind_ref,
                        forward_ref, backward_ref, end_ref, start_ref):
    faces = Faces()
    index = index_ref[...]
    inverse = inverse_ref[...]
    kind = kind_ref[...]
    wall = kind == 2
    q = load_tiles(q_ref)
    q1 = load_tiles(q1_ref)
    t1 = t1_ref[...]
    x1 = x1_ref[...]
    jump = 0.5 * (faces.flux(t1) - faces.flux(x1)) + (x1 - t1)
    faced = lifted(lift_factor * jump)
    inner = volume(q1, forward_ref[...])
    store_tiles(end_ref, [0.5 * q[j] + 0.5 * (q1[j] + step_size * (inner[j] + faced[j])) for j in range(3)])
    t = t_ref[...]
    lam1 = lam1_ref[...]
    x = exterior(faces, wall, index, local_ref[...], t)
    bar = jnp.where(kind == 1, 0.0, lam1 - 0.5 * faces.flux_back(x, lam1))
    total = 0.5 * faces.flux_back(t, lam1) - lam1 + jnp.where(wall, faces.mirror(bar), 0.0)
    total = total + select_rows(local_back_ref[...], take(bar, inverse))
    w = load_tiles(w_ref)
    w1 = load_tiles(w1_ref)
    inner = volume_back(q, derivative_back(w1, backward_ref[...]))
    faced = lifted(total)
    store_tiles(start_ref, [0.5 * w[j] + w1[j] + step_size * (inner[j] + faced[j]) for j in range(3)])


def last_kernel(end_base_ref, start_base_ref, chip_ref, own_ref, next_ref, from_slots_ref, to_columns_ref, index_ref,
                end_ref, start_ref):
    faces = Faces()
    main = jnp.concatenate(
        [chip_ref[:, 0].reshape(G, 128), own_ref[:, 3].reshape(G, 128), next_ref[:, 1].reshape(G, 128)], axis=0)
    lane = lanes(G)
    zero = jnp.zeros((G, 128), bf16)
    shared = jnp.concatenate([
        jnp.where(lane < 32, chip_ref[:, 1].reshape(G, 128), zero),
        jnp.where((lane >= 32) & (lane < 64), own_ref[:, 1].reshape(G, 128), zero),
        jnp.where((lane >= 64) & (lane < 96), next_ref[:, 0].reshape(G, 128), zero)], axis=0)
    g = dot(from_slots_ref[...], jnp.concatenate([main, shared], axis=1))
    lane = lanes(F)
    x = jnp.where(lane < 48, turn(g[:, :128], 48), 0.0)
    high = g[:, 128:]
    high = turn(high, 48) + turn(high, 16) + turn(high, 112)
    x = x + jnp.where((lane >= 48) & (lane < 80), high, 0.0)
    xr = take(x, index_ref[...])
    faced = lifted((0.5 * step_size * lift_factor) * (xr - 0.5 * faces.flux(xr)))
    base = load_tiles(end_base_ref)
    from_tiles([base[j] + faced[j] for j in range(3)], end_ref)
    bar = dot(to_columns_ref[...], main)
    bar = jnp.where(lane < 80, bar, 0.0)
    faced = lifted(step_size * bar)
    base = load_tiles(start_base_ref)
    from_tiles([base[j] + faced[j] for j in range(3)], start_ref)


def shape(*dims, dtype=f32):
    return jax.ShapeDtypeStruct(dims, dtype)


def call(kernel, outs, *args, scratch=(), in_hbm=False):
    return pl.pallas_call(
        kernel,
        out_shape=outs,
        in_specs=[pl.BlockSpec(memory_space=pl.ANY if in_hbm else pltpu.VMEM)] * len(args),
        scratch_shapes=scratch,
        cost_estimate=pl.CostEstimate(flops=200_000_000, bytes_accessed=1_000_000, transcendentals=0),
        compiler_params=pltpu.CompilerParams(vmem_limit_bytes=32 * 1024 * 1024),
    )(*args)


def all_peers(whole):
    return lax.all_to_all(whole, "sub", split_axis=0, concat_axis=0, tiled=True)


def next_partner(value):
    count = lax.axis_size("dom")
    pairs = [(d, (d + 1) % count if d % 2 else (d - 1) % count) for d in range(count)]
    return lax.ppermute(value, "dom", pairs)


def chip_partner(value):
    return lax.ppermute(value, "dom", [(d, d ^ 1) for d in range(lax.axis_size("dom"))])


def shards(state, adjoint_final, send_slot, ext_index, ext_perm):
    forward, backward = derivative_operands()
    forward, backward = jnp.asarray(forward), jnp.asarray(backward)
    state, adjoint_final = jnp.swapaxes(state, 1, 2), jnp.swapaxes(adjoint_final, 1, 2)
    node = shape(E, 384)
    face = shape(F, 128)
    index_face = shape(F, 128, dtype=i32)

    out, q, w, t, lam, send_slots, back_slots, inverse, send_slot, ext_index, ext_perm = call(
        pack_kernel,
        (shape(8, 3, 16, 384, dtype=bf16), node, node, face, face,
         shape(S, F, dtype=bf16), shape(S, F, dtype=bf16), index_face,
         shape(1, S, dtype=i32), shape(6, E, dtype=i32), shape(6, E, dtype=i32)),
        *[pltpu.with_memory_space_constraint(x, pltpu.HBM) for x in (state, adjoint_final, send_slot, ext_index, ext_perm)], in_hbm=True,
        scratch=[pltpu.VMEM((5, E, 64), f32), pltpu.VMEM((5, E, 64), f32), pltpu.SemaphoreType.DMA((5,))])
    arrived = all_peers(out)
    base, z, from_slots, to_columns, local, local_back, index, kind = call(
        first_local_kernel,
        (node, shape(96, 384), shape(F, S, dtype=bf16), shape(F, S, dtype=bf16),
         shape(F, F, dtype=bf16), shape(F, F, dtype=bf16), index_face, index_face),
        q, w, t, send_slot, ext_index, ext_perm, forward, backward)
    from_next = next_partner(arrived[:, 2])
    from_chip = chip_partner(arrived[:, 0])
    out, q1, w1, t1, x1, lam1 = call(
        middle_kernel, (shape(8, 4, 16, 128, dtype=bf16), node, node, face, face, face),
        base, w, lam, z, from_chip, arrived, from_next,
        from_slots, to_columns, local, local_back, send_slots, back_slots, index, inverse, kind)
    arrived = all_peers(out)
    end_base, start_base = call(
        second_local_kernel, (node, node),
        q, w, t, q1, w1, t1, x1, lam1, local, local_back, index, inverse, kind, forward, backward)
    from_next = next_partner(arrived[:, 1:3])
    from_chip = chip_partner(arrived[:, 0:2])
    out = shape(5, E, 64)
    end, start = call(
        last_kernel, (out, out),
        end_base, start_base, from_chip, arrived, from_next, from_slots, to_columns, index)
    return jnp.swapaxes(end, 1, 2), jnp.swapaxes(start, 1, 2)


def solution(mesh):
    return jax.shard_map(
        shards,
        mesh=mesh,
        in_specs=(
            P(None, None, ("dom", "sub")),
            P(None, None, ("dom", "sub")),
            P(("dom", "sub"), None),
            P(None, ("dom", "sub")),
            P(None, ("dom", "sub")),
        ),
        out_specs=(P(None, None, ("dom", "sub")), P(None, None, ("dom", "sub"))),
        check_vma=False,
    )
```

```python
import jax
import jax.numpy as jnp
import numpy as np
import ml_dtypes
from jax import lax
from jax.experimental import pallas as pl
from jax.experimental.pallas import tpu as pltpu
from jax.sharding import PartitionSpec as P

step_size = 0.02
mean_flow = 0.3
lift_factor = 12.0

E = 32
F = 192
S = 384
G = 128
f32 = jnp.float32
bf16 = jnp.bfloat16
i32 = jnp.int32


def derivative_table():
    points = np.array([-1.0, -1.0 / np.sqrt(5.0), 1.0 / np.sqrt(5.0), 1.0])
    products = np.array(
        [np.prod([points[t] - points[s] for s in range(4) if s != t]) for t in range(4)]
    )
    result = np.zeros((4, 4))
    for t in range(4):
        for s in range(4):
            if t != s:
                result[t, s] = products[t] / (products[s] * (points[t] - points[s]))
        result[t, t] = -np.sum(result[t])
    return result.astype(np.float32)


def halves_of(matrix):
    hi = matrix.astype(ml_dtypes.bfloat16)
    lo = (matrix - hi.astype(np.float32)).astype(ml_dtypes.bfloat16)
    return hi, lo


def derivative_operands():
    d = -2.0 * derivative_table()
    eye = np.eye(4, dtype=np.float32)
    along = [
        np.kron(d, np.kron(eye, eye)),
        np.kron(eye, np.kron(d, eye)),
        np.kron(eye, np.kron(eye, d)),
    ]
    two = [np.kron(np.eye(2, dtype=np.float32), a).astype(np.float32) for a in along]
    hi, lo = halves_of(np.concatenate([t.T for t in two], axis=0))
    forward = np.concatenate([hi, lo], axis=1)
    hi, lo = halves_of(np.concatenate(two, axis=1))
    backward = np.concatenate([hi, lo], axis=1)
    return forward, backward


def lanes(rows=1):
    return lax.broadcasted_iota(i32, (rows, 128), 1)


def take(x, index):
    return jnp.take_along_axis(x, jnp.broadcast_to(index, x.shape), axis=1)


def mask(condition):
    return jnp.where(condition, 1.0, 0.0).astype(f32)


def turn(x, shift):
    return pltpu.roll(x, shift, 1)


def halves(x):
    hi = x.astype(bf16)
    lo = (x - hi.astype(f32)).astype(bf16)
    return hi, lo


def dot(a, b):
    return jnp.dot(a, b, preferred_element_type=f32)


def select_rows(onehot, x):
    hi, lo = halves(x)
    r = dot(onehot, jnp.concatenate([hi, lo], axis=1))
    return r[:, :128] + r[:, 128:]


def to_tiles(ref):
    zero = jnp.zeros((E, 64), f32)
    tiles = []
    for j in range(3):
        high = ref[2 * j + 1] if j < 2 else zero
        tiles.append(jnp.concatenate([ref[2 * j], high], axis=1))
    return tiles


def from_tiles(tiles, ref):
    for j in range(3):
        ref[2 * j] = tiles[j][:, :64]
        if j < 2:
            ref[2 * j + 1] = tiles[j][:, 64:]


def load_tiles(ref):
    return [ref[:, 128 * j : 128 * (j + 1)] for j in range(3)]


def store_tiles(ref, tiles):
    for j in range(3):
        ref[:, 128 * j : 128 * (j + 1)] = tiles[j]


def spread(tiles):
    low = lanes(E) < 64
    back0, back1, back2 = turn(tiles[0], 64), turn(tiles[1], 64), turn(tiles[2], 64)
    ux = jnp.where(low, back0, tiles[0])
    uy = jnp.where(low, tiles[1], back1)
    uz = jnp.where(low, back1, tiles[1])
    p = tiles[2] + back2
    return low, (ux, uy, uz), p


def volume(tiles, table):
    low, speeds, p = spread(tiles)
    fluxes = []
    for a in range(3):
        u = speeds[a]
        c = u + mean_flow if a == 0 else u
        high0 = p if a == 0 else jnp.zeros_like(p)
        parts = [c * tiles[0] + jnp.where(low, u, high0), c * tiles[1], c * tiles[2] + jnp.where(low, u, 0.0)]
        if a == 1:
            parts[1] = parts[1] + jnp.where(low, p, 0.0)
        if a == 2:
            parts[1] = parts[1] + jnp.where(low, 0.0, p)
        fluxes.append(jnp.concatenate(parts, axis=0))
    hi, lo = halves(jnp.concatenate(fluxes, axis=1))
    r = dot(jnp.concatenate([hi, lo], axis=0), table)
    out = r[:96, :128] + (r[:96, 128:] + r[96:, :128])
    return [out[:32], out[32:64], out[64:96]]


def derivative_back(tiles, table):
    hi, lo = halves(jnp.concatenate(tiles, axis=0))
    r = dot(jnp.concatenate([hi, lo], axis=0), table)
    return r[:96, :384] + (r[:96, 384:] + r[96:, :384])


def volume_back(tiles, z):
    low, speeds, _ = spread(tiles)
    one = jnp.where(low, 1.0, 0.0).astype(f32)
    plus = [tiles[0] + one, tiles[1], tiles[2] + one]
    out = [jnp.zeros((E, 128), f32) for _ in range(3)]
    sums = []
    parts = []
    for a in range(3):
        c = speeds[a] + mean_flow if a == 0 else speeds[a]
        za = [z[32 * j : 32 * (j + 1), 128 * a : 128 * (a + 1)] for j in range(3)]
        total = plus[0] * za[0] + plus[1] * za[1] + plus[2] * za[2]
        sums.append(total + turn(total, 64))
        parts.append(za)
        out = [out[j] + c * za[j] for j in range(3)]
    pressure = turn(parts[0][0], 64) + parts[1][1] + turn(parts[2][1], 64)
    out[0] = out[0] + jnp.where(low, 0.0, sums[0])
    out[1] = out[1] + jnp.where(low, sums[1], sums[2])
    out[2] = out[2] + jnp.where(low, pressure, 0.0)
    return out


def traces(tiles):
    lane = lanes()
    wide = lanes(E)
    m = lane & 15
    r, s = m >> 2, m & 3
    base = ((lane >> 4) & 1) * 64
    rows = []
    for f in range(6):
        b = f % 2
        index = base + (48 * b + m, 16 * r + 12 * b + s, 4 * m + 3 * b)[f // 2]
        index = jnp.where(lane < 80, index, 64)
        t = jnp.where(
            wide < 32,
            take(tiles[0], index),
            jnp.where(wide < 64, take(tiles[1], index), take(tiles[2], index)),
        )
        rows.append(t)
    return jnp.concatenate(rows, axis=0)


def lifted(x):
    lane = lanes()
    wide = lanes(E)
    n = lane & 63
    i, j, k = n >> 4, (n >> 2) & 3, n & 3
    places = (4 * j + k, 4 * i + k, 4 * i + j)
    layers = (i, j, k)
    wide_layers = ((wide >> 4) & 3, (wide >> 2) & 3, wide & 3)
    tiles = [None] * 3
    for a in range(3):
        first, last = x[64 * a : 64 * a + 32], turn(x[64 * a + 32 : 64 * a + 64], 64)
        pair = jnp.where(wide < 64, first, last)
        tail = jnp.where(wide < 16, last, first)
        ends = (wide_layers[a] == 0) | (wide_layers[a] == 3)
        for tile in range(3):
            v = 2 * tile + (lane >> 6)
            index = v * 16 + places[a]
            at_last = jnp.where(layers[a] == 3, 64, 0)
            if tile < 2:
                part = take(pair, index + at_last)
            else:
                part = take(tail, jnp.where(lane < 64, index - at_last, 80))
            part = jnp.where(ends, part, 0.0)
            tiles[tile] = part if tiles[tile] is None else tiles[tile] + part
    return tiles


def by_axis(function, *arrays):
    return jnp.concatenate(
        [function(a, *[x[64 * a : 64 * (a + 1)] for x in arrays]) for a in range(3)], axis=0)


def signed(x):
    return jnp.concatenate([-x[:32], x[32:]], axis=0)


class Faces:
    def __init__(self):
        lane = lanes()
        self.v = lane >> 4
        self.m = lane & 15
        self.ends = mask((self.v == 0) | (self.v == 4))
        self.last = mask(self.v == 4)
        self.normal = [mask(self.v == a + 1) for a in range(3)]
        self.normal_index = [(a + 1) * 16 + self.m for a in range(3)]
        self.pressure_index = 64 + self.m

    def normal_of(self, x):
        return by_axis(lambda a, x: take(x, self.normal_index[a]), x)

    def pressure_of(self, x):
        return take(x, self.pressure_index)

    def flux(self, x, u=None, p=None):
        u = self.normal_of(x) if u is None else u
        p = self.pressure_of(x) if p is None else p

        def along(a, x, u, p):
            c = u + mean_flow if a == 0 else u
            return signed(c * x + self.ends * u + self.normal[a] * p)

        return by_axis(along, x, u, p)

    def flux_back(self, x, u, w):
        def along(a, x, u, w):
            n = take(w, self.normal_index[a])
            c = u + mean_flow if a == 0 else u
            h = over_fields((x + self.ends) * w)
            return signed(c * w + self.last * n + self.normal[a] * h)

        return by_axis(along, x, u, w)

    def rest_back(self, w):
        def along(a, w):
            n = take(w, self.normal_index[a])
            h = over_fields(self.ends * w)
            part = self.last * n + self.normal[a] * h
            return signed(mean_flow * w + part if a == 0 else part)

        return by_axis(along, w)

    def state_back(self, x, u, w):
        def along(a, x, u, w):
            return signed(u * w + self.normal[a] * over_fields(x * w))

        return by_axis(along, x, u, w)

    def shifted(self, d):
        target = self.v + d
        target = jnp.where(target >= 5, target - 5, target)
        return target, jnp.where(self.v < 5, target * 16 + self.m, 16 * self.v + self.m)

    def hessian(self, d, y):
        target, index = self.shifted(d)

        def along(a, y):
            back = mask((self.v < 5) & (target == a + 1))
            return signed(-0.5 * (self.normal[a] * take(y, index) + back * y))

        return by_axis(along, y)

    def mirror(self, x):
        return by_axis(lambda a, x: x * (1.0 - 2.0 * self.normal[a]), x)


def over_fields(h):
    table = ((lax.broadcasted_iota(i32, (128, 128), 0) ^ lax.broadcasted_iota(i32, (128, 128), 1)) & 15) == 0
    table = mask(table).astype(bf16)
    hi, lo = halves(h)
    return dot(jnp.concatenate([hi, lo], axis=1), jnp.concatenate([table, table], axis=0))


def column_of(table_ref):
    x = table_ref[...].astype(f32)
    x = jnp.concatenate([x, jnp.zeros((2, E), f32)], axis=0)
    t = jnp.transpose(x)
    return jnp.concatenate([t[:, f : f + 1] for f in range(6)], axis=0).astype(i32)


def row_of(table_ref):
    return jnp.concatenate([table_ref[f : f + 1, :] for f in range(6)], axis=1)


def slot_column(send):
    x = jnp.broadcast_to(send.astype(f32), (8, S))
    return jnp.transpose(x)[:, :1].astype(i32)


def onehot(rows, columns, first, second):
    return jnp.where(first == second, 1.0, 0.0).astype(bf16)


def faces_from_columns(ext_col):
    return onehot(F, F, ext_col, lax.broadcasted_iota(i32, (F, F), 1))


def columns_from_faces(ext_row):
    return onehot(F, F, ext_row, lax.broadcasted_iota(i32, (F, F), 0))


def faces_from_slots(ext_col):
    return onehot(F, S, ext_col - F, lax.broadcasted_iota(i32, (F, S), 1))


def slots_from_faces(ext_row):
    return onehot(S, F, ext_row - F, lax.broadcasted_iota(i32, (S, F), 0))


def slots_from_columns(send_col):
    return onehot(S, F, send_col, lax.broadcasted_iota(i32, (S, F), 1))


def columns_from_slots(send_row):
    return onehot(F, S, send_row, lax.broadcasted_iota(i32, (F, S), 0))


def orientation(perm_col):
    lane = lanes(F)
    m = lane & 15
    crossed = lane - m + ((m & 3) * 4 + (m >> 2))
    k = jnp.broadcast_to(perm_col, (F, 128))
    flips = (k & 1) * 12 + ((k & 2) >> 1) * 3
    crossed_flips = (k & 1) * 3 + ((k & 2) >> 1) * 12
    swap = (k & 4) == 4
    place = jnp.where(swap, crossed, lane)
    return place ^ jnp.where(swap, crossed_flips, flips), place ^ flips


def peer_tables(send_ref, ext_ref):
    odd = (lax.axis_index("dom") & 1) == 1
    send = send_ref[...]
    swapped = jnp.concatenate([send[:, 2 * G :], send[:, G : 2 * G], send[:, :G]], axis=1)
    send = jnp.where(odd, send, swapped)

    def reordered(table):
        slot = table - F
        turned = jnp.where(slot < G, slot + 2 * G, jnp.where(slot >= 2 * G, slot - 2 * G, slot))
        turned = jnp.where((slot >= 0) & (slot < S), turned + F, table)
        return jnp.where(odd, turned, table)

    return send, reordered(column_of(ext_ref)), reordered(row_of(ext_ref))


def packed(x):
    tail = lanes(F) >= 80
    first = jnp.where(tail, turn(x, 80), 0.0)
    second = jnp.where(tail, turn(x, 32), 0.0)
    return jnp.concatenate([first, second], axis=1).astype(bf16)


def exterior(faces, wall, index, onehot_local, t, u):
    g = select_rows(onehot_local, t)
    node = index & 15
    x = jnp.where(wall, faces.mirror(t), take(g, index))
    v = by_axis(lambda a, g, node: take(g, (a + 1) * 16 + node), g, node)
    return x, jnp.where(wall, -u, v)


def block_of(ref, row):
    return ref[:, row : row + 16].reshape(G, 128)


def pack_kernel(state_hbm, final_hbm, send_hbm, ext_hbm, perm_hbm,
                out_ref, q_ref, w_ref, t_ref, lam_ref, send_slots_ref, back_slots_ref, inverse_ref,
                send_ref, ext_ref, perm_ref, state_ref, final_ref, sems):
    pairs = ((send_hbm, send_ref), (ext_hbm, ext_ref), (perm_hbm, perm_ref), (final_hbm, final_ref), (state_hbm, state_ref))
    copies = [pltpu.make_async_copy(a, b, sems.at[i]) for i, (a, b) in enumerate(pairs)]
    for copy in copies:
        copy.start()
    faces = Faces()
    for copy in copies[:3]:
        copy.wait()
    send, _, ext_row = peer_tables(send_ref, ext_ref)
    send_slots = slots_from_columns(slot_column(send))
    back_slots = slots_from_faces(ext_row)
    send_slots_ref[...] = send_slots
    back_slots_ref[...] = back_slots
    _, inverse = orientation(column_of(perm_ref))
    inverse_ref[...] = inverse
    for copy in copies[3:]:
        copy.wait()
    q = to_tiles(state_ref)
    w = to_tiles(final_ref)
    store_tiles(q_ref, q)
    store_tiles(w_ref, w)
    t = traces(q)
    lam = lift_factor * traces(w)
    t_ref[...] = t
    lam_ref[...] = lam
    y = take(lam, inverse)
    diagonal = by_axis(lambda a, y: signed(-faces.normal[a] * y), y)
    first = y - 0.5 * faces.rest_back(y) + turn(diagonal, 64)
    stack = jnp.concatenate([x.astype(bf16) for x in (first, faces.hessian(1, y), faces.hessian(2, y))], axis=1)
    back = dot(back_slots, stack)
    forward = dot(send_slots, packed(t))
    whole = jnp.concatenate([back[:, :128], back[:, 128:] + forward], axis=1).astype(bf16)
    for o in range(3):
        for peer in range(8):
            at = G * o + 16 * peer
            for j in range(3):
                row = 48 * o + 16 * j
                out_ref[peer, row : row + 16] = whole[at : at + 16, 128 * j : 128 * (j + 1)]


def first_local_kernel(q_ref, w_ref, t_ref, lam_ref, send_ref, ext_ref, perm_ref, forward_ref, backward_ref,
                       base_ref, z_ref, rest_ref, from_slots_ref, to_columns_ref, local_ref, local_back_ref,
                       index_ref, kind_ref):
    faces = Faces()
    send, ext_col, ext_row = peer_tables(send_ref, ext_ref)
    index, _ = orientation(column_of(perm_ref))
    index_ref[...] = index
    ext_wide = jnp.broadcast_to(ext_col, (F, 128))
    wall = ext_wide == F + S
    kind_ref[...] = jnp.where(wall, 2, jnp.where(ext_wide >= F, 1, 0))
    from_slots_ref[...] = faces_from_slots(ext_col)
    to_columns_ref[...] = columns_from_slots(send)
    local = faces_from_columns(ext_col)
    local_ref[...] = local
    local_back_ref[...] = columns_from_faces(ext_row)
    q = load_tiles(q_ref)
    t = t_ref[...]
    lam = lam_ref[...]
    rest_ref[...] = lam - 0.5 * faces.rest_back(lam)
    u = faces.normal_of(t)
    x, v = exterior(faces, wall, index, local, t, u)
    jump = 0.5 * (faces.flux(t, u) - faces.flux(x, v)) + (x - t)
    faced = lifted(lift_factor * jump)
    inner = volume(q, forward_ref[...])
    store_tiles(base_ref, [q[j] + step_size * (inner[j] + faced[j]) for j in range(3)])
    z_ref[...] = derivative_back(load_tiles(w_ref), backward_ref[...])


def middle_kernel(base_ref, w_ref, lam_ref, rest_ref, z_ref, chip_ref, own_ref, next_ref,
                  from_slots_ref, to_columns_ref, local_ref, local_back_ref, send_slots_ref, back_slots_ref,
                  index_ref, inverse_ref, kind_ref,
                  out_ref, q1_ref, w1_ref, t1_ref, u1_ref, x1_ref, v1_ref, lam1_ref):
    faces = Faces()
    index = index_ref[...]
    inverse = inverse_ref[...]
    kind = kind_ref[...]
    wall = kind == 2
    wide = lanes(F)
    lane = lanes()
    node = index & 15
    arrived = jnp.concatenate(
        [jnp.concatenate([block_of(ref, at + 16 * j) for j in range(3)], axis=1)
         for ref, at in ((chip_ref, 0), (own_ref, 48), (next_ref, 0))], axis=0)
    g = dot(from_slots_ref[...], arrived[:, 128:])
    sums = dot(to_columns_ref[...], arrived)
    g0, g1 = g[:, :128], g[:, 128:]
    place = jnp.where(wide < 48, index + 80, jnp.where(wide < 80, index + 32, 112 + node))
    xr = jnp.where(wide < 48, take(g0, place), take(g1, place))
    ur = jnp.concatenate(
        [take(g0[:64], 96 + node[:64]), take(g0[64:128], 112 + node[64:128]), take(g1[128:], 80 + node[128:])], axis=0)
    pr = take(g1, 96 + node)
    faced = lifted((lift_factor * step_size) * (xr - 0.5 * faces.flux(xr, ur, pr)))
    base = load_tiles(base_ref)
    q1 = [base[j] + faced[j] for j in range(3)]
    store_tiles(q1_ref, q1)
    t1 = traces(q1)
    t1_ref[...] = t1
    t1_sent = t1.astype(bf16)
    forward = dot(send_slots_ref[...], t1_sent)
    lam = lam_ref[...]
    rest = rest_ref[...]
    u1 = faces.normal_of(t1)
    u1_ref[...] = u1
    x1, v1 = exterior(faces, wall, index, local_ref[...], t1, u1)
    x1_ref[...] = x1
    v1_ref[...] = v1
    bar = jnp.where(kind == 1, 0.0, rest - 0.5 * faces.state_back(x1, v1, lam))
    total = 0.5 * faces.state_back(t1, u1, lam) - rest + jnp.where(wall, faces.mirror(bar), 0.0)
    total = total + select_rows(local_back_ref[...], take(bar, inverse))
    sent = t1_sent.astype(f32)
    h0, h1, h2 = sums[:, :128], sums[:, 128:256], sums[:, 256:]
    ahead1, ahead2, behind2, behind1 = [faces.shifted(d)[1] for d in (1, 2, 3, 4)]
    through = h0 + h1 * take(sent, ahead1) + h2 * take(sent, ahead2)
    through = through + take(h1 * sent, behind1) + take(h2 * sent, behind2)
    through = through + mask((lane >= 16) & (lane < 64)) * turn(h0, 64) * sent
    total = total + mask(lane < 80) * through
    inner = volume_back(q1, z_ref[...])
    faced = lifted(total)
    w = load_tiles(w_ref)
    w1 = [0.5 * w[j] + (0.5 * step_size) * (inner[j] + faced[j]) for j in range(3)]
    store_tiles(w1_ref, w1)
    lam1 = lift_factor * traces(w1)
    lam1_ref[...] = lam1
    bar = lam1 - 0.5 * faces.flux_back(xr, ur, lam1)
    first = take(bar, jnp.where(wide >= 80, inverse - 80, 80))
    second = take(bar, jnp.where(wide < 32, inverse + 48, 80))
    back = dot(back_slots_ref[...], jnp.concatenate([first, second], axis=1).astype(bf16))
    main = (back[:, :128] + forward).astype(bf16)
    tail = [back[G * o : G * (o + 1), 128:] for o in range(3)]
    shared = (tail[0] + turn(tail[1], 32) + turn(tail[2], 64)).astype(bf16)
    for peer in range(8):
        at = 16 * peer
        out_ref[peer, :16] = main[at : at + 16]
        out_ref[peer, 16:32] = shared[at : at + 16]
        out_ref[peer, 32:48] = main[2 * G + at : 2 * G + at + 16]
        out_ref[peer, 48:] = main[G + at : G + at + 16]


def second_local_kernel(q_ref, w_ref, t_ref, q1_ref, w1_ref, t1_ref, u1_ref, x1_ref, v1_ref, lam1_ref,
                        local_ref, local_back_ref, index_ref, inverse_ref, kind_ref,
                        forward_ref, backward_ref, end_ref, start_ref):
    faces = Faces()
    index = index_ref[...]
    inverse = inverse_ref[...]
    kind = kind_ref[...]
    wall = kind == 2
    q = load_tiles(q_ref)
    q1 = load_tiles(q1_ref)
    t1 = t1_ref[...]
    x1 = x1_ref[...]
    jump = 0.5 * (faces.flux(t1, u1_ref[...]) - faces.flux(x1, v1_ref[...])) + (x1 - t1)
    faced = lifted(lift_factor * jump)
    inner = volume(q1, forward_ref[...])
    store_tiles(end_ref, [0.5 * q[j] + 0.5 * (q1[j] + step_size * (inner[j] + faced[j])) for j in range(3)])
    t = t_ref[...]
    lam1 = lam1_ref[...]
    u = faces.normal_of(t)
    x, v = exterior(faces, wall, index, local_ref[...], t, u)
    rest = lam1 - 0.5 * faces.rest_back(lam1)
    bar = jnp.where(kind == 1, 0.0, rest - 0.5 * faces.state_back(x, v, lam1))
    total = 0.5 * faces.state_back(t, u, lam1) - rest + jnp.where(wall, faces.mirror(bar), 0.0)
    total = total + select_rows(local_back_ref[...], take(bar, inverse))
    w = load_tiles(w_ref)
    w1 = load_tiles(w1_ref)
    inner = volume_back(q, derivative_back(w1, backward_ref[...]))
    faced = lifted(total)
    store_tiles(start_ref, [0.5 * w[j] + w1[j] + step_size * (inner[j] + faced[j]) for j in range(3)])


def last_kernel(end_base_ref, start_base_ref, chip_ref, own_ref, next_ref, from_slots_ref, to_columns_ref, index_ref,
                end_ref, start_ref):
    faces = Faces()
    main = jnp.concatenate([block_of(chip_ref, 0), block_of(own_ref, 48), block_of(next_ref, 16)], axis=0)
    lane = lanes(G)
    zero = jnp.zeros((G, 128), bf16)
    shared = jnp.concatenate([
        jnp.where(lane < 32, block_of(chip_ref, 16), zero),
        jnp.where((lane >= 32) & (lane < 64), block_of(own_ref, 16), zero),
        jnp.where((lane >= 64) & (lane < 96), block_of(next_ref, 0), zero)], axis=0)
    node = index_ref[...] & 15
    g = dot(from_slots_ref[...], main)
    b = dot(to_columns_ref[...], jnp.concatenate([main, shared], axis=1))
    lane = lanes()
    valid = mask(lane < 80)
    xr = valid * take(g, index_ref[...])
    ur = by_axis(lambda a, g, node: take(g, (a + 1) * 16 + node), g, node)
    pr = take(g, 64 + node)
    faced = lifted((0.5 * step_size * lift_factor) * (xr - 0.5 * faces.flux(xr, ur, pr)))
    base = load_tiles(end_base_ref)
    from_tiles([base[j] + faced[j] for j in range(3)], end_ref)
    high = turn(b[:, 128:], 48) + turn(b[:, 128:], 16) + turn(b[:, 128:], 112)
    bar = mask(lane < 48) * turn(b[:, :128], 48) + mask((lane >= 48) & (lane < 80)) * high
    faced = lifted(step_size * bar)
    base = load_tiles(start_base_ref)
    from_tiles([base[j] + faced[j] for j in range(3)], start_ref)


def shape(*dims, dtype=f32):
    return jax.ShapeDtypeStruct(dims, dtype)


def call(kernel, outs, *args, scratch=(), in_hbm=False):
    return pl.pallas_call(
        kernel,
        out_shape=outs,
        in_specs=[pl.BlockSpec(memory_space=pl.ANY if in_hbm else pltpu.VMEM)] * len(args),
        scratch_shapes=scratch,
        cost_estimate=pl.CostEstimate(flops=200_000_000, bytes_accessed=1_000_000, transcendentals=0),
        compiler_params=pltpu.CompilerParams(vmem_limit_bytes=32 * 1024 * 1024),
    )(*args)


def all_peers(whole):
    return lax.all_to_all(whole, "sub", split_axis=0, concat_axis=0, tiled=True)


def next_partner(value):
    count = lax.axis_size("dom")
    pairs = [(d, (d + 1) % count if d % 2 else (d - 1) % count) for d in range(count)]
    return lax.ppermute(value, "dom", pairs)


def chip_partner(value):
    return lax.ppermute(value, "dom", [(d, d ^ 1) for d in range(lax.axis_size("dom"))])


def shards(state, adjoint_final, send_slot, ext_index, ext_perm):
    forward, backward = derivative_operands()
    forward, backward = jnp.asarray(forward), jnp.asarray(backward)
    state, adjoint_final = jnp.swapaxes(state, 1, 2), jnp.swapaxes(adjoint_final, 1, 2)
    node = shape(E, 384)
    face = shape(F, 128)
    index_face = shape(F, 128, dtype=i32)

    out, q, w, t, lam, send_slots, back_slots, inverse, send_slot, ext_index, ext_perm = call(
        pack_kernel,
        (shape(8, 144, 128, dtype=bf16), node, node, face, face,
         shape(S, F, dtype=bf16), shape(S, F, dtype=bf16), index_face,
         shape(1, S, dtype=i32), shape(6, E, dtype=i32), shape(6, E, dtype=i32)),
        *[pltpu.with_memory_space_constraint(x, pltpu.HBM) for x in (state, adjoint_final, send_slot, ext_index, ext_perm)], in_hbm=True,
        scratch=[pltpu.VMEM((5, E, 64), f32), pltpu.VMEM((5, E, 64), f32), pltpu.SemaphoreType.DMA((5,))])
    arrived = all_peers(out)
    base, z, rest, from_slots, to_columns, local, local_back, index, kind = call(
        first_local_kernel,
        (node, shape(96, 384), face, shape(F, S, dtype=bf16), shape(F, S, dtype=bf16),
         shape(F, F, dtype=bf16), shape(F, F, dtype=bf16), index_face, index_face),
        q, w, t, lam, send_slot, ext_index, ext_perm, forward, backward)
    from_next = next_partner(arrived[:, 96:])
    from_chip = chip_partner(arrived[:, :48])
    out, q1, w1, t1, u1, x1, v1, lam1 = call(
        middle_kernel, (shape(8, 64, 128, dtype=bf16), node, node, face, face, face, face, face),
        base, w, lam, rest, z, from_chip, arrived, from_next,
        from_slots, to_columns, local, local_back, send_slots, back_slots, index, inverse, kind)
    arrived = all_peers(out)
    end_base, start_base = call(
        second_local_kernel, (node, node),
        q, w, t, q1, w1, t1, u1, x1, v1, lam1, local, local_back, index, inverse, kind, forward, backward)
    from_next = next_partner(arrived[:, 16:48])
    from_chip = chip_partner(arrived[:, :32])
    out = shape(5, E, 64)
    end, start = call(
        last_kernel, (out, out),
        end_base, start_base, from_chip, arrived, from_next, from_slots, to_columns, index)
    return jnp.swapaxes(end, 1, 2), jnp.swapaxes(start, 1, 2)


def solution(mesh):
    return jax.shard_map(
        shards,
        mesh=mesh,
        in_specs=(
            P(None, None, ("dom", "sub")),
            P(None, None, ("dom", "sub")),
            P(("dom", "sub"), None),
            P(None, ("dom", "sub")),
            P(None, ("dom", "sub")),
        ),
        out_specs=(P(None, None, ("dom", "sub")), P(None, None, ("dom", "sub"))),
        check_vma=False,
    )
```

```python
import jax
import jax.numpy as jnp
import numpy as np
import ml_dtypes
from jax import lax
from jax.experimental import pallas as pl
from jax.experimental.pallas import tpu as pltpu
from jax.sharding import PartitionSpec as P

step_size = 0.02
mean_flow = 0.3
lift_factor = 12.0

E = 32
F = 192
S = 384
G = 128
f32 = jnp.float32
bf16 = jnp.bfloat16
i32 = jnp.int32


def derivative_table():
    points = np.array([-1.0, -1.0 / np.sqrt(5.0), 1.0 / np.sqrt(5.0), 1.0])
    products = np.array(
        [np.prod([points[t] - points[s] for s in range(4) if s != t]) for t in range(4)]
    )
    result = np.zeros((4, 4))
    for t in range(4):
        for s in range(4):
            if t != s:
                result[t, s] = products[t] / (products[s] * (points[t] - points[s]))
        result[t, t] = -np.sum(result[t])
    return result.astype(np.float32)


def halves_of(matrix):
    hi = matrix.astype(ml_dtypes.bfloat16)
    lo = (matrix - hi.astype(np.float32)).astype(ml_dtypes.bfloat16)
    return hi, lo


def derivative_operands():
    d = -2.0 * derivative_table()
    eye = np.eye(4, dtype=np.float32)
    along = [
        np.kron(d, np.kron(eye, eye)),
        np.kron(eye, np.kron(d, eye)),
        np.kron(eye, np.kron(eye, d)),
    ]
    two = [np.kron(np.eye(2, dtype=np.float32), a).astype(np.float32) for a in along]
    hi, lo = halves_of(np.concatenate([t.T for t in two], axis=0))
    forward = np.concatenate([hi, lo], axis=1)
    hi, lo = halves_of(np.concatenate(two, axis=1))
    backward = np.concatenate([hi, lo], axis=1)
    return forward, backward


def lanes(rows=1):
    return lax.broadcasted_iota(i32, (rows, 128), 1)


def take(x, index):
    return jnp.take_along_axis(x, jnp.broadcast_to(index, x.shape), axis=1)


def mask(condition):
    return jnp.where(condition, 1.0, 0.0).astype(f32)


def turn(x, shift):
    return pltpu.roll(x, shift, 1)


def halves(x):
    hi = x.astype(bf16)
    lo = (x - hi.astype(f32)).astype(bf16)
    return hi, lo


def dot(a, b):
    return jnp.dot(a, b, preferred_element_type=f32)


def select_rows(onehot, x):
    hi, lo = halves(x)
    r = dot(onehot, jnp.concatenate([hi, lo], axis=1))
    return r[:, :128] + r[:, 128:]


def to_tiles(ref):
    zero = jnp.zeros((E, 64), f32)
    tiles = []
    for j in range(3):
        high = ref[2 * j + 1] if j < 2 else zero
        tiles.append(jnp.concatenate([ref[2 * j], high], axis=1))
    return tiles


def from_tiles(tiles, ref):
    for j in range(3):
        ref[2 * j] = tiles[j][:, :64]
        if j < 2:
            ref[2 * j + 1] = tiles[j][:, 64:]


def load_tiles(ref):
    return [ref[:, 128 * j : 128 * (j + 1)] for j in range(3)]


def store_tiles(ref, tiles):
    for j in range(3):
        ref[:, 128 * j : 128 * (j + 1)] = tiles[j]


def spread(tiles):
    low = lanes(E) < 64
    back0, back1, back2 = turn(tiles[0], 64), turn(tiles[1], 64), turn(tiles[2], 64)
    ux = jnp.where(low, back0, tiles[0])
    uy = jnp.where(low, tiles[1], back1)
    uz = jnp.where(low, back1, tiles[1])
    p = tiles[2] + back2
    return low, (ux, uy, uz), p


def volume(tiles, table):
    low, speeds, p = spread(tiles)
    fluxes = []
    for a in range(3):
        u = speeds[a]
        c = u + mean_flow if a == 0 else u
        high0 = p if a == 0 else jnp.zeros_like(p)
        parts = [c * tiles[0] + jnp.where(low, u, high0), c * tiles[1], c * tiles[2] + jnp.where(low, u, 0.0)]
        if a == 1:
            parts[1] = parts[1] + jnp.where(low, p, 0.0)
        if a == 2:
            parts[1] = parts[1] + jnp.where(low, 0.0, p)
        fluxes.append(jnp.concatenate(parts, axis=0))
    hi, lo = halves(jnp.concatenate(fluxes, axis=1))
    r = dot(jnp.concatenate([hi, lo], axis=0), table)
    out = r[:96, :128] + (r[:96, 128:] + r[96:, :128])
    return [out[:32], out[32:64], out[64:96]]


def derivative_back(tiles, table):
    hi, lo = halves(jnp.concatenate(tiles, axis=0))
    r = dot(jnp.concatenate([hi, lo], axis=0), table)
    return r[:96, :384] + (r[:96, 384:] + r[96:, :384])


def volume_back(tiles, z):
    low, speeds, _ = spread(tiles)
    one = jnp.where(low, 1.0, 0.0).astype(f32)
    plus = [tiles[0] + one, tiles[1], tiles[2] + one]
    out = [jnp.zeros((E, 128), f32) for _ in range(3)]
    sums = []
    parts = []
    for a in range(3):
        c = speeds[a] + mean_flow if a == 0 else speeds[a]
        za = [z[32 * j : 32 * (j + 1), 128 * a : 128 * (a + 1)] for j in range(3)]
        total = plus[0] * za[0] + plus[1] * za[1] + plus[2] * za[2]
        sums.append(total + turn(total, 64))
        parts.append(za)
        out = [out[j] + c * za[j] for j in range(3)]
    pressure = turn(parts[0][0], 64) + parts[1][1] + turn(parts[2][1], 64)
    out[0] = out[0] + jnp.where(low, 0.0, sums[0])
    out[1] = out[1] + jnp.where(low, sums[1], sums[2])
    out[2] = out[2] + jnp.where(low, pressure, 0.0)
    return out


def traces(tiles):
    lane = lanes()
    wide = lanes(E)
    m = lane & 15
    r, s = m >> 2, m & 3
    base = ((lane >> 4) & 1) * 64
    rows = []
    for f in range(6):
        b = f % 2
        index = base + (48 * b + m, 16 * r + 12 * b + s, 4 * m + 3 * b)[f // 2]
        index = jnp.where(lane < 80, index, 64)
        t = jnp.where(
            wide < 32,
            take(tiles[0], index),
            jnp.where(wide < 64, take(tiles[1], index), take(tiles[2], index)),
        )
        rows.append(t)
    return jnp.concatenate(rows, axis=0)


def lifted(x):
    lane = lanes()
    wide = lanes(E)
    n = lane & 63
    i, j, k = n >> 4, (n >> 2) & 3, n & 3
    places = (4 * j + k, 4 * i + k, 4 * i + j)
    layers = (i, j, k)
    wide_layers = ((wide >> 4) & 3, (wide >> 2) & 3, wide & 3)
    tiles = [None] * 3
    for a in range(3):
        first, last = x[64 * a : 64 * a + 32], turn(x[64 * a + 32 : 64 * a + 64], 64)
        pair = jnp.where(wide < 64, first, last)
        tail = jnp.where(wide < 16, last, first)
        ends = (wide_layers[a] == 0) | (wide_layers[a] == 3)
        for tile in range(3):
            v = 2 * tile + (lane >> 6)
            index = v * 16 + places[a]
            at_last = jnp.where(layers[a] == 3, 64, 0)
            if tile < 2:
                part = take(pair, index + at_last)
            else:
                part = take(tail, jnp.where(lane < 64, index - at_last, 80))
            part = jnp.where(ends, part, 0.0)
            tiles[tile] = part if tiles[tile] is None else tiles[tile] + part
    return tiles


def by_axis(function, *arrays):
    return jnp.concatenate(
        [function(a, *[x[64 * a : 64 * (a + 1)] for x in arrays]) for a in range(3)], axis=0)


def signed(x):
    return jnp.concatenate([-x[:32], x[32:]], axis=0)


class Faces:
    def __init__(self):
        lane = lanes()
        self.v = lane >> 4
        self.m = lane & 15
        self.ends = mask((self.v == 0) | (self.v == 4))
        self.last = mask(self.v == 4)
        self.normal = [mask(self.v == a + 1) for a in range(3)]
        self.normal_index = [(a + 1) * 16 + self.m for a in range(3)]
        self.pressure_index = 64 + self.m

    def normal_of(self, x):
        return by_axis(lambda a, x: take(x, self.normal_index[a]), x)

    def pressure_of(self, x):
        return take(x, self.pressure_index)

    def flux(self, x, u=None, p=None):
        u = self.normal_of(x) if u is None else u
        p = self.pressure_of(x) if p is None else p

        def along(a, x, u, p):
            c = u + mean_flow if a == 0 else u
            return signed(c * x + self.ends * u + self.normal[a] * p)

        return by_axis(along, x, u, p)

    def flux_back(self, x, u, w):
        def along(a, x, u, w):
            n = take(w, self.normal_index[a])
            c = u + mean_flow if a == 0 else u
            h = over_fields((x + self.ends) * w)
            return signed(c * w + self.last * n + self.normal[a] * h)

        return by_axis(along, x, u, w)

    def rest_back(self, w):
        def along(a, w):
            n = take(w, self.normal_index[a])
            h = over_fields(self.ends * w)
            part = self.last * n + self.normal[a] * h
            return signed(mean_flow * w + part if a == 0 else part)

        return by_axis(along, w)

    def state_back(self, x, u, w):
        def along(a, x, u, w):
            return signed(u * w + self.normal[a] * over_fields(x * w))

        return by_axis(along, x, u, w)

    def shifted(self, d):
        target = self.v + d
        target = jnp.where(target >= 5, target - 5, target)
        return target, jnp.where(self.v < 5, target * 16 + self.m, 16 * self.v + self.m)

    def hessian(self, d, y):
        target, index = self.shifted(d)

        def along(a, y):
            back = mask((self.v < 5) & (target == a + 1))
            return signed(-0.5 * (self.normal[a] * take(y, index) + back * y))

        return by_axis(along, y)

    def mirror(self, x):
        return by_axis(lambda a, x: x * (1.0 - 2.0 * self.normal[a]), x)


def over_fields(h):
    table = ((lax.broadcasted_iota(i32, (128, 128), 0) ^ lax.broadcasted_iota(i32, (128, 128), 1)) & 15) == 0
    table = mask(table).astype(bf16)
    hi, lo = halves(h)
    return dot(jnp.concatenate([hi, lo], axis=1), jnp.concatenate([table, table], axis=0))


def column_of(table_ref):
    x = table_ref[...].astype(f32)
    x = jnp.concatenate([x, jnp.zeros((2, E), f32)], axis=0)
    t = jnp.transpose(x)
    return jnp.concatenate([t[:, f : f + 1] for f in range(6)], axis=0).astype(i32)


def row_of(table_ref):
    return jnp.concatenate([table_ref[f : f + 1, :] for f in range(6)], axis=1)


def slot_column(send):
    x = jnp.broadcast_to(send.astype(f32), (8, S))
    return jnp.transpose(x)[:, :1].astype(i32)


def onehot(rows, columns, first, second):
    return jnp.where(first == second, 1.0, 0.0).astype(bf16)


def faces_from_columns(ext_col):
    return onehot(F, F, ext_col, lax.broadcasted_iota(i32, (F, F), 1))


def columns_from_faces(ext_row):
    return onehot(F, F, ext_row, lax.broadcasted_iota(i32, (F, F), 0))


def faces_from_slots(ext_col):
    return onehot(F, S, ext_col - F, lax.broadcasted_iota(i32, (F, S), 1))


def slots_from_faces(ext_row):
    return onehot(S, F, ext_row - F, lax.broadcasted_iota(i32, (S, F), 0))


def slots_from_columns(send_col):
    return onehot(S, F, send_col, lax.broadcasted_iota(i32, (S, F), 1))


def columns_from_slots(send_row):
    return onehot(F, S, send_row, lax.broadcasted_iota(i32, (F, S), 0))


def orientation(perm_col):
    lane = lanes(F)
    m = lane & 15
    crossed = lane - m + ((m & 3) * 4 + (m >> 2))
    k = jnp.broadcast_to(perm_col, (F, 128))
    flips = (k & 1) * 12 + ((k & 2) >> 1) * 3
    crossed_flips = (k & 1) * 3 + ((k & 2) >> 1) * 12
    swap = (k & 4) == 4
    place = jnp.where(swap, crossed, lane)
    return place ^ jnp.where(swap, crossed_flips, flips), place ^ flips


def peer_tables(send_ref, ext_ref):
    odd = (lax.axis_index("dom") & 1) == 1
    send = send_ref[...]
    swapped = jnp.concatenate([send[:, 2 * G :], send[:, G : 2 * G], send[:, :G]], axis=1)
    send = jnp.where(odd, send, swapped)

    def reordered(table):
        slot = table - F
        turned = jnp.where(slot < G, slot + 2 * G, jnp.where(slot >= 2 * G, slot - 2 * G, slot))
        turned = jnp.where((slot >= 0) & (slot < S), turned + F, table)
        return jnp.where(odd, turned, table)

    return send, reordered(column_of(ext_ref)), reordered(row_of(ext_ref))


def packed(x):
    tail = lanes(F) >= 80
    first = jnp.where(tail, turn(x, 80), 0.0)
    second = jnp.where(tail, turn(x, 32), 0.0)
    return jnp.concatenate([first, second], axis=1).astype(bf16)


def exterior(faces, wall, index, onehot_local, t, u):
    g = select_rows(onehot_local, t)
    node = index & 15
    x = jnp.where(wall, faces.mirror(t), take(g, index))
    v = by_axis(lambda a, g, node: take(g, (a + 1) * 16 + node), g, node)
    return x, jnp.where(wall, -u, v)


def places():
    own = jnp.where((lax.axis_index("dom") & 1) == 1, 0, 8)
    return own, 8 - own


def block_of(ref, row, start=0):
    return ref[pl.ds(start, 8), row : row + 16].reshape(G, 128)


def pack_kernel(state_hbm, final_hbm, send_hbm, ext_hbm, perm_hbm,
                out_ref, q_ref, w_ref, t_ref, lam_ref, send_slots_ref, back_slots_ref, inverse_ref,
                send_ref, ext_ref, perm_ref, state_ref, final_ref, sems):
    pairs = ((send_hbm, send_ref), (ext_hbm, ext_ref), (perm_hbm, perm_ref), (final_hbm, final_ref), (state_hbm, state_ref))
    copies = [pltpu.make_async_copy(a, b, sems.at[i]) for i, (a, b) in enumerate(pairs)]
    for copy in copies:
        copy.start()
    faces = Faces()
    for copy in copies[:3]:
        copy.wait()
    send, _, ext_row = peer_tables(send_ref, ext_ref)
    send_slots = slots_from_columns(slot_column(send))
    back_slots = slots_from_faces(ext_row)
    send_slots_ref[...] = send_slots
    back_slots_ref[...] = back_slots
    _, inverse = orientation(column_of(perm_ref))
    inverse_ref[...] = inverse
    for copy in copies[3:]:
        copy.wait()
    q = to_tiles(state_ref)
    w = to_tiles(final_ref)
    store_tiles(q_ref, q)
    store_tiles(w_ref, w)
    t = traces(q)
    lam = lift_factor * traces(w)
    t_ref[...] = t
    lam_ref[...] = lam
    y = take(lam, inverse)
    diagonal = by_axis(lambda a, y: signed(-faces.normal[a] * y), y)
    first = y - 0.5 * faces.rest_back(y) + turn(diagonal, 64)
    stack = jnp.concatenate([x.astype(bf16) for x in (first, faces.hessian(1, y), faces.hessian(2, y))], axis=1)
    back = dot(back_slots, stack)
    forward = dot(send_slots, packed(t))
    whole = jnp.concatenate([back[:, :128], back[:, 128:] + forward], axis=1).astype(bf16)
    own, other = places()
    for peer in range(8):
        for o, place, start in ((0, own, 48), (1, own, 0), (2, other, 0)):
            at = G * o + 16 * peer
            for j in range(3):
                row = start + 16 * j
                out_ref[place + peer, row : row + 16] = whole[at : at + 16, 128 * j : 128 * (j + 1)]
        out_ref[other + peer, 48:] = jnp.zeros((48, 128), bf16)


def first_local_kernel(q_ref, w_ref, t_ref, lam_ref, send_ref, ext_ref, perm_ref, forward_ref, backward_ref,
                       base_ref, z_ref, rest_ref, from_slots_ref, to_columns_ref, local_ref, local_back_ref,
                       index_ref, kind_ref):
    faces = Faces()
    send, ext_col, ext_row = peer_tables(send_ref, ext_ref)
    index, _ = orientation(column_of(perm_ref))
    index_ref[...] = index
    ext_wide = jnp.broadcast_to(ext_col, (F, 128))
    wall = ext_wide == F + S
    kind_ref[...] = jnp.where(wall, 2, jnp.where(ext_wide >= F, 1, 0))
    from_slots_ref[...] = faces_from_slots(ext_col)
    to_columns_ref[...] = columns_from_slots(send)
    local = faces_from_columns(ext_col)
    local_ref[...] = local
    local_back_ref[...] = columns_from_faces(ext_row)
    q = load_tiles(q_ref)
    t = t_ref[...]
    lam = lam_ref[...]
    rest_ref[...] = lam - 0.5 * faces.rest_back(lam)
    u = faces.normal_of(t)
    x, v = exterior(faces, wall, index, local, t, u)
    jump = 0.5 * (faces.flux(t, u) - faces.flux(x, v)) + (x - t)
    faced = lifted(lift_factor * jump)
    inner = volume(q, forward_ref[...])
    store_tiles(base_ref, [q[j] + step_size * (inner[j] + faced[j]) for j in range(3)])
    z_ref[...] = derivative_back(load_tiles(w_ref), backward_ref[...])


def middle_kernel(base_ref, w_ref, lam_ref, rest_ref, z_ref, chip_ref, arrived_ref,
                  from_slots_ref, to_columns_ref, local_ref, local_back_ref, send_slots_ref, back_slots_ref,
                  index_ref, inverse_ref, kind_ref,
                  out_ref, q1_ref, w1_ref, t1_ref, u1_ref, x1_ref, v1_ref, lam1_ref):
    faces = Faces()
    index = index_ref[...]
    inverse = inverse_ref[...]
    kind = kind_ref[...]
    wall = kind == 2
    wide = lanes(F)
    lane = lanes()
    node = index & 15
    own, other = places()
    arrived = jnp.concatenate(
        [jnp.concatenate([block_of(ref, 16 * j, start) for j in range(3)], axis=1)
         for ref, start in ((chip_ref, 0), (arrived_ref, own), (arrived_ref, other))], axis=0)
    g = dot(from_slots_ref[...], arrived[:, 128:])
    sums = dot(to_columns_ref[...], arrived)
    g0, g1 = g[:, :128], g[:, 128:]
    place = jnp.where(wide < 48, index + 80, jnp.where(wide < 80, index + 32, 112 + node))
    xr = jnp.where(wide < 48, take(g0, place), take(g1, place))
    ur = jnp.concatenate(
        [take(g0[:64], 96 + node[:64]), take(g0[64:128], 112 + node[64:128]), take(g1[128:], 80 + node[128:])], axis=0)
    pr = take(g1, 96 + node)
    faced = lifted((lift_factor * step_size) * (xr - 0.5 * faces.flux(xr, ur, pr)))
    base = load_tiles(base_ref)
    q1 = [base[j] + faced[j] for j in range(3)]
    store_tiles(q1_ref, q1)
    t1 = traces(q1)
    t1_ref[...] = t1
    t1_sent = t1.astype(bf16)
    forward = dot(send_slots_ref[...], t1_sent)
    lam = lam_ref[...]
    rest = rest_ref[...]
    u1 = faces.normal_of(t1)
    u1_ref[...] = u1
    x1, v1 = exterior(faces, wall, index, local_ref[...], t1, u1)
    x1_ref[...] = x1
    v1_ref[...] = v1
    bar = jnp.where(kind == 1, 0.0, rest - 0.5 * faces.state_back(x1, v1, lam))
    total = 0.5 * faces.state_back(t1, u1, lam) - rest + jnp.where(wall, faces.mirror(bar), 0.0)
    total = total + select_rows(local_back_ref[...], take(bar, inverse))
    sent = t1_sent.astype(f32)
    h0, h1, h2 = sums[:, :128], sums[:, 128:256], sums[:, 256:]
    ahead1, ahead2, behind2, behind1 = [faces.shifted(d)[1] for d in (1, 2, 3, 4)]
    through = h0 + h1 * take(sent, ahead1) + h2 * take(sent, ahead2)
    through = through + take(h1 * sent, behind1) + take(h2 * sent, behind2)
    through = through + mask((lane >= 16) & (lane < 64)) * turn(h0, 64) * sent
    total = total + mask(lane < 80) * through
    inner = volume_back(q1, z_ref[...])
    faced = lifted(total)
    w = load_tiles(w_ref)
    w1 = [0.5 * w[j] + (0.5 * step_size) * (inner[j] + faced[j]) for j in range(3)]
    store_tiles(w1_ref, w1)
    lam1 = lift_factor * traces(w1)
    lam1_ref[...] = lam1
    bar = lam1 - 0.5 * faces.flux_back(xr, ur, lam1)
    first = take(bar, jnp.where(wide >= 80, inverse - 80, 80))
    second = take(bar, jnp.where(wide < 32, inverse + 48, 80))
    back = dot(back_slots_ref[...], jnp.concatenate([first, second], axis=1).astype(bf16))
    main = (back[:, :128] + forward).astype(bf16)
    tail = [back[G * o : G * (o + 1), 128:] for o in range(3)]
    shared = (tail[0] + turn(tail[1], 32)).astype(bf16)
    last = turn(tail[2], 64).astype(bf16)
    for peer in range(8):
        at = 16 * peer
        out_ref[own + peer, :16] = main[G + at : G + at + 16]
        out_ref[own + peer, 16:32] = main[at : at + 16]
        out_ref[own + peer, 32:] = shared[at : at + 16]
        out_ref[other + peer, :16] = main[2 * G + at : 2 * G + at + 16]
        out_ref[other + peer, 16:32] = last[at : at + 16]
        out_ref[other + peer, 32:] = jnp.zeros((16, 128), bf16)


def second_local_kernel(q_ref, w_ref, t_ref, q1_ref, w1_ref, t1_ref, u1_ref, x1_ref, v1_ref, lam1_ref,
                        local_ref, local_back_ref, index_ref, inverse_ref, kind_ref,
                        forward_ref, backward_ref, end_ref, start_ref):
    faces = Faces()
    index = index_ref[...]
    inverse = inverse_ref[...]
    kind = kind_ref[...]
    wall = kind == 2
    q = load_tiles(q_ref)
    q1 = load_tiles(q1_ref)
    t1 = t1_ref[...]
    x1 = x1_ref[...]
    jump = 0.5 * (faces.flux(t1, u1_ref[...]) - faces.flux(x1, v1_ref[...])) + (x1 - t1)
    faced = lifted(lift_factor * jump)
    inner = volume(q1, forward_ref[...])
    store_tiles(end_ref, [0.5 * q[j] + 0.5 * (q1[j] + step_size * (inner[j] + faced[j])) for j in range(3)])
    t = t_ref[...]
    lam1 = lam1_ref[...]
    u = faces.normal_of(t)
    x, v = exterior(faces, wall, index, local_ref[...], t, u)
    rest = lam1 - 0.5 * faces.rest_back(lam1)
    bar = jnp.where(kind == 1, 0.0, rest - 0.5 * faces.state_back(x, v, lam1))
    total = 0.5 * faces.state_back(t, u, lam1) - rest + jnp.where(wall, faces.mirror(bar), 0.0)
    total = total + select_rows(local_back_ref[...], take(bar, inverse))
    w = load_tiles(w_ref)
    w1 = load_tiles(w1_ref)
    inner = volume_back(q, derivative_back(w1, backward_ref[...]))
    faced = lifted(total)
    store_tiles(start_ref, [0.5 * w[j] + w1[j] + step_size * (inner[j] + faced[j]) for j in range(3)])


def last_kernel(end_base_ref, start_base_ref, chip_ref, arrived_ref, from_slots_ref, to_columns_ref, index_ref,
                end_ref, start_ref):
    faces = Faces()
    own, other = places()
    main = jnp.concatenate([block_of(chip_ref, 0), block_of(arrived_ref, 0, own), block_of(arrived_ref, 0, other)], axis=0)
    lane = lanes(G)
    zero = jnp.zeros((G, 128), bf16)
    shared = jnp.concatenate([
        jnp.where(lane < 32, block_of(chip_ref, 16), zero),
        jnp.where((lane >= 32) & (lane < 64), block_of(arrived_ref, 32, own), zero),
        jnp.where((lane >= 64) & (lane < 96), block_of(arrived_ref, 16, other), zero)], axis=0)
    node = index_ref[...] & 15
    g = dot(from_slots_ref[...], main)
    b = dot(to_columns_ref[...], jnp.concatenate([main, shared], axis=1))
    lane = lanes()
    valid = mask(lane < 80)
    xr = valid * take(g, index_ref[...])
    ur = by_axis(lambda a, g, node: take(g, (a + 1) * 16 + node), g, node)
    pr = take(g, 64 + node)
    faced = lifted((0.5 * step_size * lift_factor) * (xr - 0.5 * faces.flux(xr, ur, pr)))
    base = load_tiles(end_base_ref)
    from_tiles([base[j] + faced[j] for j in range(3)], end_ref)
    high = turn(b[:, 128:], 48) + turn(b[:, 128:], 16) + turn(b[:, 128:], 112)
    bar = mask(lane < 48) * turn(b[:, :128], 48) + mask((lane >= 48) & (lane < 80)) * high
    faced = lifted(step_size * bar)
    base = load_tiles(start_base_ref)
    from_tiles([base[j] + faced[j] for j in range(3)], start_ref)


def shape(*dims, dtype=f32):
    return jax.ShapeDtypeStruct(dims, dtype)


def call(kernel, outs, *args, scratch=(), in_hbm=False):
    return pl.pallas_call(
        kernel,
        out_shape=outs,
        in_specs=[pl.BlockSpec(memory_space=pl.ANY if in_hbm else pltpu.VMEM)] * len(args),
        scratch_shapes=scratch,
        cost_estimate=pl.CostEstimate(flops=200_000_000, bytes_accessed=1_000_000, transcendentals=0),
        compiler_params=pltpu.CompilerParams(vmem_limit_bytes=32 * 1024 * 1024),
    )(*args)


def all_peers(whole):
    return lax.all_to_all(whole, "sub", split_axis=0, concat_axis=0, tiled=True)


def pair_peers(whole):
    count, peers = lax.axis_size("dom"), lax.axis_size("sub")
    groups = [[d % count * peers + peer for d in (first, first + 1) for peer in range(peers)]
              for first in range(1, count, 2)]
    return lax.all_to_all(
        whole, ("dom", "sub"), split_axis=0, concat_axis=0, tiled=True, axis_index_groups=groups)


def own_part(arrived):
    return jnp.where((lax.axis_index("dom") & 1) == 1, arrived[:8], arrived[8:])


def next_partner(value):
    count = lax.axis_size("dom")
    pairs = [(d, (d + 1) % count if d % 2 else (d - 1) % count) for d in range(count)]
    return lax.ppermute(value, "dom", pairs)


def chip_partner(value):
    return lax.ppermute(value, "dom", [(d, d ^ 1) for d in range(lax.axis_size("dom"))])


def shards(state, adjoint_final, send_slot, ext_index, ext_perm):
    forward, backward = derivative_operands()
    forward, backward = jnp.asarray(forward), jnp.asarray(backward)
    state, adjoint_final = jnp.swapaxes(state, 1, 2), jnp.swapaxes(adjoint_final, 1, 2)
    node = shape(E, 384)
    face = shape(F, 128)
    index_face = shape(F, 128, dtype=i32)

    out, q, w, t, lam, send_slots, back_slots, inverse, send_slot, ext_index, ext_perm = call(
        pack_kernel,
        (shape(16, 96, 128, dtype=bf16), node, node, face, face,
         shape(S, F, dtype=bf16), shape(S, F, dtype=bf16), index_face,
         shape(1, S, dtype=i32), shape(6, E, dtype=i32), shape(6, E, dtype=i32)),
        *[pltpu.with_memory_space_constraint(x, pltpu.HBM) for x in (state, adjoint_final, send_slot, ext_index, ext_perm)], in_hbm=True,
        scratch=[pltpu.VMEM((5, E, 64), f32), pltpu.VMEM((5, E, 64), f32), pltpu.SemaphoreType.DMA((5,))])
    arrived = pair_peers(out)
    base, z, rest, from_slots, to_columns, local, local_back, index, kind = call(
        first_local_kernel,
        (node, shape(96, 384), face, shape(F, S, dtype=bf16), shape(F, S, dtype=bf16),
         shape(F, F, dtype=bf16), shape(F, F, dtype=bf16), index_face, index_face),
        q, w, t, lam, send_slot, ext_index, ext_perm, forward, backward)
    from_chip = chip_partner(own_part(arrived[:, 48:]))
    out, q1, w1, t1, u1, x1, v1, lam1 = call(
        middle_kernel, (shape(16, 48, 128, dtype=bf16), node, node, face, face, face, face, face),
        base, w, lam, rest, z, from_chip, arrived,
        from_slots, to_columns, local, local_back, send_slots, back_slots, index, inverse, kind)
    arrived = pair_peers(out)
    end_base, start_base = call(
        second_local_kernel, (node, node),
        q, w, t, q1, w1, t1, u1, x1, v1, lam1, local, local_back, index, inverse, kind, forward, backward)
    from_chip = chip_partner(own_part(arrived[:, 16:]))
    out = shape(5, E, 64)
    end, start = call(
        last_kernel, (out, out),
        end_base, start_base, from_chip, arrived, from_slots, to_columns, index)
    return jnp.swapaxes(end, 1, 2), jnp.swapaxes(start, 1, 2)


def solution(mesh):
    return jax.shard_map(
        shards,
        mesh=mesh,
        in_specs=(
            P(None, None, ("dom", "sub")),
            P(None, None, ("dom", "sub")),
            P(("dom", "sub"), None),
            P(None, ("dom", "sub")),
            P(None, ("dom", "sub")),
        ),
        out_specs=(P(None, None, ("dom", "sub")), P(None, None, ("dom", "sub"))),
        check_vma=False,
    )
```

```python
import jax
import jax.numpy as jnp
import numpy as np
import ml_dtypes
from jax import lax
from jax.experimental import pallas as pl
from jax.experimental.pallas import tpu as pltpu
from jax.sharding import PartitionSpec as P

step_size = 0.02
mean_flow = 0.3
lift_factor = 12.0

E = 32
F = 192
S = 384
G = 128
f32 = jnp.float32
bf16 = jnp.bfloat16
i32 = jnp.int32


def derivative_table():
    points = np.array([-1.0, -1.0 / np.sqrt(5.0), 1.0 / np.sqrt(5.0), 1.0])
    products = np.array(
        [np.prod([points[t] - points[s] for s in range(4) if s != t]) for t in range(4)]
    )
    result = np.zeros((4, 4))
    for t in range(4):
        for s in range(4):
            if t != s:
                result[t, s] = products[t] / (products[s] * (points[t] - points[s]))
        result[t, t] = -np.sum(result[t])
    return result.astype(np.float32)


def halves_of(matrix):
    hi = matrix.astype(ml_dtypes.bfloat16)
    lo = (matrix - hi.astype(np.float32)).astype(ml_dtypes.bfloat16)
    return hi, lo


def derivative_operands():
    d = -2.0 * derivative_table()
    eye = np.eye(4, dtype=np.float32)
    along = [
        np.kron(d, np.kron(eye, eye)),
        np.kron(eye, np.kron(d, eye)),
        np.kron(eye, np.kron(eye, d)),
    ]
    two = [np.kron(np.eye(2, dtype=np.float32), a).astype(np.float32) for a in along]
    hi, lo = halves_of(np.concatenate([t.T for t in two], axis=0))
    forward = np.concatenate([hi, lo], axis=1)
    hi, lo = halves_of(np.concatenate(two, axis=1))
    backward = np.concatenate([hi, lo], axis=1)
    return forward, backward


def lanes(rows=1):
    return lax.broadcasted_iota(i32, (rows, 128), 1)


def take(x, index):
    return jnp.take_along_axis(x, jnp.broadcast_to(index, x.shape), axis=1)


def mask(condition):
    return jnp.where(condition, 1.0, 0.0).astype(f32)


def turn(x, shift):
    return pltpu.roll(x, shift, 1)


def halves(x):
    hi = x.astype(bf16)
    lo = (x - hi.astype(f32)).astype(bf16)
    return hi, lo


def dot(a, b):
    return jnp.dot(a, b, preferred_element_type=f32)


def select_rows(onehot, x):
    hi, lo = halves(x)
    r = dot(onehot, jnp.concatenate([hi, lo], axis=1))
    return r[:, :128] + r[:, 128:]


def to_tiles(ref):
    zero = jnp.zeros((E, 64), f32)
    tiles = []
    for j in range(3):
        high = ref[2 * j + 1] if j < 2 else zero
        tiles.append(jnp.concatenate([ref[2 * j], high], axis=1))
    return tiles


def from_tiles(tiles, ref):
    for j in range(3):
        ref[2 * j] = tiles[j][:, :64]
        if j < 2:
            ref[2 * j + 1] = tiles[j][:, 64:]


def load_tiles(ref):
    return [ref[:, 128 * j : 128 * (j + 1)] for j in range(3)]


def store_tiles(ref, tiles):
    for j in range(3):
        ref[:, 128 * j : 128 * (j + 1)] = tiles[j]


def spread(tiles):
    low = lanes(E) < 64
    back0, back1, back2 = turn(tiles[0], 64), turn(tiles[1], 64), turn(tiles[2], 64)
    ux = jnp.where(low, back0, tiles[0])
    uy = jnp.where(low, tiles[1], back1)
    uz = jnp.where(low, back1, tiles[1])
    p = tiles[2] + back2
    return low, (ux, uy, uz), p


def volume(tiles, table):
    low, speeds, p = spread(tiles)
    fluxes = []
    for a in range(3):
        u = speeds[a]
        c = u + mean_flow if a == 0 else u
        high0 = p if a == 0 else jnp.zeros_like(p)
        parts = [c * tiles[0] + jnp.where(low, u, high0), c * tiles[1], c * tiles[2] + jnp.where(low, u, 0.0)]
        if a == 1:
            parts[1] = parts[1] + jnp.where(low, p, 0.0)
        if a == 2:
            parts[1] = parts[1] + jnp.where(low, 0.0, p)
        fluxes.append(jnp.concatenate(parts, axis=0))
    hi, lo = halves(jnp.concatenate(fluxes, axis=1))
    r = dot(jnp.concatenate([hi, lo], axis=0), table)
    out = r[:96, :128] + (r[:96, 128:] + r[96:, :128])
    return [out[:32], out[32:64], out[64:96]]


def derivative_back(tiles, table):
    hi, lo = halves(jnp.concatenate(tiles, axis=0))
    r = dot(jnp.concatenate([hi, lo], axis=0), table)
    return r[:96, :384] + (r[:96, 384:] + r[96:, :384])


def volume_back(tiles, z):
    low, speeds, _ = spread(tiles)
    one = jnp.where(low, 1.0, 0.0).astype(f32)
    plus = [tiles[0] + one, tiles[1], tiles[2] + one]
    out = [jnp.zeros((E, 128), f32) for _ in range(3)]
    sums = []
    parts = []
    for a in range(3):
        c = speeds[a] + mean_flow if a == 0 else speeds[a]
        za = [z[32 * j : 32 * (j + 1), 128 * a : 128 * (a + 1)] for j in range(3)]
        total = plus[0] * za[0] + plus[1] * za[1] + plus[2] * za[2]
        sums.append(total + turn(total, 64))
        parts.append(za)
        out = [out[j] + c * za[j] for j in range(3)]
    pressure = turn(parts[0][0], 64) + parts[1][1] + turn(parts[2][1], 64)
    out[0] = out[0] + jnp.where(low, 0.0, sums[0])
    out[1] = out[1] + jnp.where(low, sums[1], sums[2])
    out[2] = out[2] + jnp.where(low, pressure, 0.0)
    return out


def traces(tiles):
    lane = lanes()
    wide = lanes(E)
    m = lane & 15
    r, s = m >> 2, m & 3
    base = ((lane >> 4) & 1) * 64
    rows = []
    for f in range(6):
        b = f % 2
        index = base + (48 * b + m, 16 * r + 12 * b + s, 4 * m + 3 * b)[f // 2]
        index = jnp.where(lane < 80, index, 64)
        t = jnp.where(
            wide < 32,
            take(tiles[0], index),
            jnp.where(wide < 64, take(tiles[1], index), take(tiles[2], index)),
        )
        rows.append(t)
    return jnp.concatenate(rows, axis=0)


def lifted(x):
    lane = lanes()
    wide = lanes(E)
    n = lane & 63
    i, j, k = n >> 4, (n >> 2) & 3, n & 3
    places = (4 * j + k, 4 * i + k, 4 * i + j)
    layers = (i, j, k)
    wide_layers = ((wide >> 4) & 3, (wide >> 2) & 3, wide & 3)
    tiles = [None] * 3
    for a in range(3):
        first, last = x[64 * a : 64 * a + 32], turn(x[64 * a + 32 : 64 * a + 64], 64)
        pair = jnp.where(wide < 64, first, last)
        tail = jnp.where(wide < 16, last, first)
        ends = (wide_layers[a] == 0) | (wide_layers[a] == 3)
        for tile in range(3):
            v = 2 * tile + (lane >> 6)
            index = v * 16 + places[a]
            at_last = jnp.where(layers[a] == 3, 64, 0)
            if tile < 2:
                part = take(pair, index + at_last)
            else:
                part = take(tail, jnp.where(lane < 64, index - at_last, 80))
            part = jnp.where(ends, part, 0.0)
            tiles[tile] = part if tiles[tile] is None else tiles[tile] + part
    return tiles


def lifted_traces(x):
    lane = lanes()
    wide = lanes(E)
    v16 = lane & 112
    r, s = (lane >> 2) & 3, lane & 3
    wide_r, wide_s = (wide >> 2) & 3, wide & 3
    rows = []
    for f in range(6):
        a, b = f // 2, f % 2
        total = x[32 * f : 32 * (f + 1)]
        for place, side in ((0, wide_r), (1, wide_s)):
            axis = [other for other in range(3) if other != a][place]
            free = (s, r)[place]
            node = 12 * b + free if a < [o for o in range(3) if o != axis and o != a][0] else 4 * free + 3 * b
            index = v16 + node
            first = take(x[64 * axis : 64 * axis + 32], index)
            last = take(x[64 * axis + 32 : 64 * axis + 64], index)
            total = total + jnp.where(side == 0, first, jnp.where(side == 3, last, 0.0))
        rows.append(total)
    return jnp.concatenate(rows, axis=0)


def by_axis(function, *arrays):
    return jnp.concatenate(
        [function(a, *[x[64 * a : 64 * (a + 1)] for x in arrays]) for a in range(3)], axis=0)


def signed(x):
    return jnp.concatenate([-x[:32], x[32:]], axis=0)


class Faces:
    def __init__(self):
        lane = lanes()
        self.v = lane >> 4
        self.m = lane & 15
        self.ends = mask((self.v == 0) | (self.v == 4))
        self.last = mask(self.v == 4)
        self.normal = [mask(self.v == a + 1) for a in range(3)]
        self.normal_index = [(a + 1) * 16 + self.m for a in range(3)]
        self.pressure_index = 64 + self.m

    def normal_of(self, x):
        return by_axis(lambda a, x: take(x, self.normal_index[a]), x)

    def pressure_of(self, x):
        return take(x, self.pressure_index)

    def flux(self, x, u=None, p=None):
        u = self.normal_of(x) if u is None else u
        p = self.pressure_of(x) if p is None else p

        def along(a, x, u, p):
            c = u + mean_flow if a == 0 else u
            return signed(c * x + self.ends * u + self.normal[a] * p)

        return by_axis(along, x, u, p)

    def flux_back(self, x, u, w):
        def along(a, x, u, w):
            n = take(w, self.normal_index[a])
            c = u + mean_flow if a == 0 else u
            h = over_fields((x + self.ends) * w)
            return signed(c * w + self.last * n + self.normal[a] * h)

        return by_axis(along, x, u, w)

    def rest_back(self, w):
        def along(a, w):
            n = take(w, self.normal_index[a])
            h = over_fields(self.ends * w)
            part = self.last * n + self.normal[a] * h
            return signed(mean_flow * w + part if a == 0 else part)

        return by_axis(along, w)

    def state_back(self, x, u, w):
        def along(a, x, u, w):
            return signed(u * w + self.normal[a] * over_fields(x * w))

        return by_axis(along, x, u, w)

    def shifted(self, d):
        target = self.v + d
        target = jnp.where(target >= 5, target - 5, target)
        return target, jnp.where(self.v < 5, target * 16 + self.m, 16 * self.v + self.m)

    def hessian(self, d, y):
        target, index = self.shifted(d)

        def along(a, y):
            back = mask((self.v < 5) & (target == a + 1))
            return signed(-0.5 * (self.normal[a] * take(y, index) + back * y))

        return by_axis(along, y)

    def mirror(self, x):
        return by_axis(lambda a, x: x * (1.0 - 2.0 * self.normal[a]), x)


def over_fields(h):
    table = ((lax.broadcasted_iota(i32, (128, 128), 0) ^ lax.broadcasted_iota(i32, (128, 128), 1)) & 15) == 0
    table = mask(table).astype(bf16)
    hi, lo = halves(h)
    return dot(jnp.concatenate([hi, lo], axis=1), jnp.concatenate([table, table], axis=0))


def column_of(table_ref):
    x = table_ref[...].astype(f32)
    x = jnp.concatenate([x, jnp.zeros((2, E), f32)], axis=0)
    t = jnp.transpose(x)
    return jnp.concatenate([t[:, f : f + 1] for f in range(6)], axis=0).astype(i32)


def row_of(table_ref):
    return jnp.concatenate([table_ref[f : f + 1, :] for f in range(6)], axis=1)


def slot_column(send):
    x = jnp.broadcast_to(send.astype(f32), (8, S))
    return jnp.transpose(x)[:, :1].astype(i32)


def onehot(rows, columns, first, second):
    return jnp.where(first == second, 1.0, 0.0).astype(bf16)


def faces_from_columns(ext_col):
    return onehot(F, F, ext_col, lax.broadcasted_iota(i32, (F, F), 1))


def columns_from_faces(ext_row):
    return onehot(F, F, ext_row, lax.broadcasted_iota(i32, (F, F), 0))


def faces_from_slots(ext_col):
    return onehot(F, S, ext_col - F, lax.broadcasted_iota(i32, (F, S), 1))


def slots_from_faces(ext_row):
    return onehot(S, F, ext_row - F, lax.broadcasted_iota(i32, (S, F), 0))


def slots_from_columns(send_col):
    return onehot(S, F, send_col, lax.broadcasted_iota(i32, (S, F), 1))


def columns_from_slots(send_row):
    return onehot(F, S, send_row, lax.broadcasted_iota(i32, (F, S), 0))


def orientation(perm_col):
    lane = lanes(F)
    m = lane & 15
    crossed = lane - m + ((m & 3) * 4 + (m >> 2))
    k = jnp.broadcast_to(perm_col, (F, 128))
    flips = (k & 1) * 12 + ((k & 2) >> 1) * 3
    crossed_flips = (k & 1) * 3 + ((k & 2) >> 1) * 12
    swap = (k & 4) == 4
    place = jnp.where(swap, crossed, lane)
    return place ^ jnp.where(swap, crossed_flips, flips), place ^ flips


def peer_tables(send_ref, ext_ref):
    odd = (lax.axis_index("dom") & 1) == 1
    send = send_ref[...]
    swapped = jnp.concatenate([send[:, 2 * G :], send[:, G : 2 * G], send[:, :G]], axis=1)
    send = jnp.where(odd, send, swapped)

    def reordered(table):
        slot = table - F
        turned = jnp.where(slot < G, slot + 2 * G, jnp.where(slot >= 2 * G, slot - 2 * G, slot))
        turned = jnp.where((slot >= 0) & (slot < S), turned + F, table)
        return jnp.where(odd, turned, table)

    return send, reordered(column_of(ext_ref)), reordered(row_of(ext_ref))


def packed(x):
    tail = lanes(F) >= 80
    first = jnp.where(tail, turn(x, 80), 0.0)
    second = jnp.where(tail, turn(x, 32), 0.0)
    return jnp.concatenate([first, second], axis=1).astype(bf16)


def exterior(faces, wall, index, onehot_local, t, u):
    g = select_rows(onehot_local, t)
    node = index & 15
    x = jnp.where(wall, faces.mirror(t), take(g, index))
    v = by_axis(lambda a, g, node: take(g, (a + 1) * 16 + node), g, node)
    return x, jnp.where(wall, -u, v)


def places():
    own = jnp.where((lax.axis_index("dom") & 1) == 1, 0, 8)
    return own, 8 - own


def block_of(ref, row, start=0):
    return ref[pl.ds(start, 8), row : row + 16].reshape(G, 128)


def pack_kernel(state_hbm, final_hbm, send_hbm, ext_hbm, perm_hbm,
                out_ref, q_ref, w_ref, t_ref, lam_ref, send_slots_ref, back_slots_ref, inverse_ref,
                send_ref, ext_ref, perm_ref, state_ref, final_ref, sems):
    pairs = ((send_hbm, send_ref), (ext_hbm, ext_ref), (perm_hbm, perm_ref), (final_hbm, final_ref), (state_hbm, state_ref))
    copies = [pltpu.make_async_copy(a, b, sems.at[i]) for i, (a, b) in enumerate(pairs)]
    for copy in copies:
        copy.start()
    faces = Faces()
    for copy in copies[:3]:
        copy.wait()
    send, _, ext_row = peer_tables(send_ref, ext_ref)
    send_slots = slots_from_columns(slot_column(send))
    back_slots = slots_from_faces(ext_row)
    send_slots_ref[...] = send_slots
    back_slots_ref[...] = back_slots
    _, inverse = orientation(column_of(perm_ref))
    inverse_ref[...] = inverse
    for copy in copies[3:]:
        copy.wait()
    q = to_tiles(state_ref)
    w = to_tiles(final_ref)
    store_tiles(q_ref, q)
    store_tiles(w_ref, w)
    t = traces(q)
    lam = lift_factor * traces(w)
    t_ref[...] = t
    lam_ref[...] = lam
    y = take(lam, inverse)
    diagonal = by_axis(lambda a, y: signed(-faces.normal[a] * y), y)
    first = y - 0.5 * faces.rest_back(y) + turn(diagonal, 64)
    stack = jnp.concatenate([x.astype(bf16) for x in (first, faces.hessian(1, y), faces.hessian(2, y))], axis=1)
    back = dot(back_slots, stack)
    forward = dot(send_slots, packed(t))
    whole = jnp.concatenate([back[:, :128], back[:, 128:] + forward], axis=1).astype(bf16)
    own, other = places()
    for peer in range(8):
        for o, place, start in ((0, own, 48), (1, own, 0), (2, other, 0)):
            at = G * o + 16 * peer
            for j in range(3):
                row = start + 16 * j
                out_ref[place + peer, row : row + 16] = whole[at : at + 16, 128 * j : 128 * (j + 1)]
        out_ref[other + peer, 48:] = jnp.zeros((48, 128), bf16)


def first_local_kernel(q_ref, w_ref, t_ref, lam_ref, send_ref, ext_ref, perm_ref, forward_ref, backward_ref,
                       base_ref, t_base_ref, z_ref, rest_ref, u_ref, x_ref, v_ref,
                       from_slots_ref, to_columns_ref, local_ref, local_back_ref, index_ref, kind_ref):
    faces = Faces()
    send, ext_col, ext_row = peer_tables(send_ref, ext_ref)
    index, _ = orientation(column_of(perm_ref))
    index_ref[...] = index
    ext_wide = jnp.broadcast_to(ext_col, (F, 128))
    wall = ext_wide == F + S
    kind_ref[...] = jnp.where(wall, 2, jnp.where(ext_wide >= F, 1, 0))
    from_slots_ref[...] = faces_from_slots(ext_col)
    to_columns_ref[...] = columns_from_slots(send)
    local = faces_from_columns(ext_col)
    local_ref[...] = local
    local_back_ref[...] = columns_from_faces(ext_row)
    q = load_tiles(q_ref)
    t = t_ref[...]
    lam = lam_ref[...]
    rest_ref[...] = lam - 0.5 * faces.rest_back(lam)
    u = faces.normal_of(t)
    x, v = exterior(faces, wall, index, local, t, u)
    u_ref[...] = u
    x_ref[...] = x
    v_ref[...] = v
    jump = 0.5 * (faces.flux(t, u) - faces.flux(x, v)) + (x - t)
    faced = lifted(lift_factor * jump)
    inner = volume(q, forward_ref[...])
    base = [q[j] + step_size * (inner[j] + faced[j]) for j in range(3)]
    store_tiles(base_ref, base)
    t_base_ref[...] = traces(base)
    z_ref[...] = derivative_back(load_tiles(w_ref), backward_ref[...])


def middle_kernel(base_ref, t_base_ref, w_ref, lam_ref, rest_ref, z_ref, chip_ref, arrived_ref,
                  from_slots_ref, to_columns_ref, local_ref, local_back_ref, send_slots_ref, back_slots_ref,
                  index_ref, inverse_ref, kind_ref,
                  out_ref, q1_ref, w1_ref, t1_ref, u1_ref, x1_ref, v1_ref, lam1_ref):
    faces = Faces()
    index = index_ref[...]
    inverse = inverse_ref[...]
    kind = kind_ref[...]
    wall = kind == 2
    wide = lanes(F)
    lane = lanes()
    node = index & 15
    own, other = places()
    arrived = jnp.concatenate(
        [jnp.concatenate([block_of(ref, 16 * j, start) for j in range(3)], axis=1)
         for ref, start in ((chip_ref, 0), (arrived_ref, own), (arrived_ref, other))], axis=0)
    g = dot(from_slots_ref[...], arrived[:, 128:])
    sums = dot(to_columns_ref[...], arrived)
    g0, g1 = g[:, :128], g[:, 128:]
    place = jnp.where(wide < 48, index + 80, jnp.where(wide < 80, index + 32, 112 + node))
    xr = jnp.where(wide < 48, take(g0, place), take(g1, place))
    ur = jnp.concatenate(
        [take(g0[:64], 96 + node[:64]), take(g0[64:128], 112 + node[64:128]), take(g1[128:], 80 + node[128:])], axis=0)
    pr = take(g1, 96 + node)
    jump = (lift_factor * step_size) * (xr - 0.5 * faces.flux(xr, ur, pr))
    t1 = t_base_ref[...] + lifted_traces(jump)
    faced = lifted(jump)
    base = load_tiles(base_ref)
    q1 = [base[j] + faced[j] for j in range(3)]
    store_tiles(q1_ref, q1)
    t1_ref[...] = t1
    t1_sent = t1.astype(bf16)
    forward = dot(send_slots_ref[...], t1_sent)
    lam = lam_ref[...]
    rest = rest_ref[...]
    u1 = faces.normal_of(t1)
    u1_ref[...] = u1
    x1, v1 = exterior(faces, wall, index, local_ref[...], t1, u1)
    x1_ref[...] = x1
    v1_ref[...] = v1
    bar = jnp.where(kind == 1, 0.0, rest - 0.5 * faces.state_back(x1, v1, lam))
    total = 0.5 * faces.state_back(t1, u1, lam) - rest + jnp.where(wall, faces.mirror(bar), 0.0)
    total = total + select_rows(local_back_ref[...], take(bar, inverse))
    sent = t1_sent.astype(f32)
    h0, h1, h2 = sums[:, :128], sums[:, 128:256], sums[:, 256:]
    ahead1, ahead2, behind2, behind1 = [faces.shifted(d)[1] for d in (1, 2, 3, 4)]
    through = h0 + h1 * take(sent, ahead1) + h2 * take(sent, ahead2)
    through = through + take(h1 * sent, behind1) + take(h2 * sent, behind2)
    through = through + mask((lane >= 16) & (lane < 64)) * turn(h0, 64) * sent
    total = total + mask(lane < 80) * through
    inner = volume_back(q1, z_ref[...])
    w = load_tiles(w_ref)
    half = [0.5 * w[j] + (0.5 * step_size) * inner[j] for j in range(3)]
    lam1 = lift_factor * traces(half) + (0.5 * step_size * lift_factor) * lifted_traces(total)
    faced = lifted(total)
    store_tiles(w1_ref, [half[j] + (0.5 * step_size) * faced[j] for j in range(3)])
    lam1_ref[...] = lam1
    bar = lam1 - 0.5 * faces.flux_back(xr, ur, lam1)
    first = take(bar, jnp.where(wide >= 80, inverse - 80, 80))
    second = take(bar, jnp.where(wide < 32, inverse + 48, 80))
    back = dot(back_slots_ref[...], jnp.concatenate([first, second], axis=1).astype(bf16))
    main = (back[:, :128] + forward).astype(bf16)
    tail = [back[G * o : G * (o + 1), 128:] for o in range(3)]
    shared = (tail[0] + turn(tail[1], 32)).astype(bf16)
    last = turn(tail[2], 64).astype(bf16)
    for peer in range(8):
        at = 16 * peer
        out_ref[own + peer, :16] = main[G + at : G + at + 16]
        out_ref[own + peer, 16:32] = main[at : at + 16]
        out_ref[own + peer, 32:] = shared[at : at + 16]
        out_ref[other + peer, :16] = main[2 * G + at : 2 * G + at + 16]
        out_ref[other + peer, 16:32] = jnp.zeros((16, 128), bf16)
        out_ref[other + peer, 32:] = last[at : at + 16]


def second_local_kernel(q_ref, w_ref, t_ref, u_ref, x_ref, v_ref, q1_ref, w1_ref, t1_ref, u1_ref, x1_ref, v1_ref,
                        lam1_ref, local_back_ref, inverse_ref, kind_ref,
                        forward_ref, backward_ref, end_ref, start_ref):
    faces = Faces()
    inverse = inverse_ref[...]
    kind = kind_ref[...]
    wall = kind == 2
    q = load_tiles(q_ref)
    q1 = load_tiles(q1_ref)
    t1 = t1_ref[...]
    x1 = x1_ref[...]
    jump = 0.5 * (faces.flux(t1, u1_ref[...]) - faces.flux(x1, v1_ref[...])) + (x1 - t1)
    faced = lifted(lift_factor * jump)
    inner = volume(q1, forward_ref[...])
    store_tiles(end_ref, [0.5 * q[j] + 0.5 * (q1[j] + step_size * (inner[j] + faced[j])) for j in range(3)])
    t = t_ref[...]
    lam1 = lam1_ref[...]
    u, x, v = u_ref[...], x_ref[...], v_ref[...]
    rest = lam1 - 0.5 * faces.rest_back(lam1)
    bar = jnp.where(kind == 1, 0.0, rest - 0.5 * faces.state_back(x, v, lam1))
    total = 0.5 * faces.state_back(t, u, lam1) - rest + jnp.where(wall, faces.mirror(bar), 0.0)
    total = total + select_rows(local_back_ref[...], take(bar, inverse))
    w = load_tiles(w_ref)
    w1 = load_tiles(w1_ref)
    inner = volume_back(q, derivative_back(w1, backward_ref[...]))
    faced = lifted(total)
    store_tiles(start_ref, [0.5 * w[j] + w1[j] + step_size * (inner[j] + faced[j]) for j in range(3)])


def last_kernel(end_base_ref, start_base_ref, chip_ref, arrived_ref, from_slots_ref, to_columns_ref, index_ref,
                end_ref, start_ref):
    faces = Faces()
    own, other = places()
    main = jnp.concatenate([block_of(chip_ref, 0), block_of(arrived_ref, 0, own), block_of(arrived_ref, 0, other)], axis=0)
    lane = lanes(G)
    zero = jnp.zeros((G, 128), bf16)
    shared = jnp.concatenate([
        jnp.where(lane < 32, block_of(chip_ref, 16), zero),
        jnp.where((lane >= 32) & (lane < 64), block_of(arrived_ref, 32, own), zero),
        jnp.where((lane >= 64) & (lane < 96), block_of(arrived_ref, 32, other), zero)], axis=0)
    node = index_ref[...] & 15
    g = dot(from_slots_ref[...], main)
    b = dot(to_columns_ref[...], jnp.concatenate([main, shared], axis=1))
    lane = lanes()
    valid = mask(lane < 80)
    xr = valid * take(g, index_ref[...])
    ur = by_axis(lambda a, g, node: take(g, (a + 1) * 16 + node), g, node)
    pr = take(g, 64 + node)
    faced = lifted((0.5 * step_size * lift_factor) * (xr - 0.5 * faces.flux(xr, ur, pr)))
    base = load_tiles(end_base_ref)
    from_tiles([base[j] + faced[j] for j in range(3)], end_ref)
    high = turn(b[:, 128:], 48) + turn(b[:, 128:], 16) + turn(b[:, 128:], 112)
    bar = mask(lane < 48) * turn(b[:, :128], 48) + mask((lane >= 48) & (lane < 80)) * high
    faced = lifted(step_size * bar)
    base = load_tiles(start_base_ref)
    from_tiles([base[j] + faced[j] for j in range(3)], start_ref)


def shape(*dims, dtype=f32):
    return jax.ShapeDtypeStruct(dims, dtype)


def call(kernel, outs, *args, scratch=(), in_hbm=False):
    return pl.pallas_call(
        kernel,
        out_shape=outs,
        in_specs=[pl.BlockSpec(memory_space=pl.ANY if in_hbm else pltpu.VMEM)] * len(args),
        scratch_shapes=scratch,
        cost_estimate=pl.CostEstimate(flops=200_000_000, bytes_accessed=1_000_000, transcendentals=0),
        compiler_params=pltpu.CompilerParams(vmem_limit_bytes=32 * 1024 * 1024),
    )(*args)


def pair_peers(whole):
    count, peers = lax.axis_size("dom"), lax.axis_size("sub")
    groups = [[d % count * peers + peer for d in (first, first + 1) for peer in range(peers)]
              for first in range(1, count, 2)]
    return lax.all_to_all(
        whole, ("dom", "sub"), split_axis=0, concat_axis=0, tiled=True, axis_index_groups=groups)


def for_chip(arrived):
    return arrived[:8] + arrived[8:]


def chip_partner(value):
    return lax.ppermute(value, "dom", [(d, d ^ 1) for d in range(lax.axis_size("dom"))])


def shards(state, adjoint_final, send_slot, ext_index, ext_perm):
    forward, backward = derivative_operands()
    forward, backward = jnp.asarray(forward), jnp.asarray(backward)
    state, adjoint_final = jnp.swapaxes(state, 1, 2), jnp.swapaxes(adjoint_final, 1, 2)
    node = shape(E, 384)
    face = shape(F, 128)
    index_face = shape(F, 128, dtype=i32)

    out, q, w, t, lam, send_slots, back_slots, inverse, send_slot, ext_index, ext_perm = call(
        pack_kernel,
        (shape(16, 96, 128, dtype=bf16), node, node, face, face,
         shape(S, F, dtype=bf16), shape(S, F, dtype=bf16), index_face,
         shape(1, S, dtype=i32), shape(6, E, dtype=i32), shape(6, E, dtype=i32)),
        *[pltpu.with_memory_space_constraint(x, pltpu.HBM) for x in (state, adjoint_final, send_slot, ext_index, ext_perm)], in_hbm=True,
        scratch=[pltpu.VMEM((5, E, 64), f32), pltpu.VMEM((5, E, 64), f32), pltpu.SemaphoreType.DMA((5,))])
    arrived = pair_peers(out)
    base, t_base, z, rest, u, x, v, from_slots, to_columns, local, local_back, index, kind = call(
        first_local_kernel,
        (node, face, shape(96, 384), face, face, face, face, shape(F, S, dtype=bf16), shape(F, S, dtype=bf16),
         shape(F, F, dtype=bf16), shape(F, F, dtype=bf16), index_face, index_face),
        q, w, t, lam, send_slot, ext_index, ext_perm, forward, backward)
    from_chip = chip_partner(for_chip(arrived[:, 48:]))
    out, q1, w1, t1, u1, x1, v1, lam1 = call(
        middle_kernel, (shape(16, 48, 128, dtype=bf16), node, node, face, face, face, face, face),
        base, t_base, w, lam, rest, z, from_chip, arrived,
        from_slots, to_columns, local, local_back, send_slots, back_slots, index, inverse, kind)
    arrived = pair_peers(out)
    end_base, start_base = call(
        second_local_kernel, (node, node),
        q, w, t, u, x, v, q1, w1, t1, u1, x1, v1, lam1, local_back, inverse, kind, forward, backward)
    from_chip = chip_partner(for_chip(arrived[:, 16:]))
    out = shape(5, E, 64)
    end, start = call(
        last_kernel, (out, out),
        end_base, start_base, from_chip, arrived, from_slots, to_columns, index)
    return jnp.swapaxes(end, 1, 2), jnp.swapaxes(start, 1, 2)


def solution(mesh):
    return jax.shard_map(
        shards,
        mesh=mesh,
        in_specs=(
            P(None, None, ("dom", "sub")),
            P(None, None, ("dom", "sub")),
            P(("dom", "sub"), None),
            P(None, ("dom", "sub")),
            P(None, ("dom", "sub")),
        ),
        out_specs=(P(None, None, ("dom", "sub")), P(None, None, ("dom", "sub"))),
        check_vma=False,
    )
```

```python
import jax
import jax.numpy as jnp
import numpy as np
import ml_dtypes
from jax import lax
from jax.experimental import pallas as pl
from jax.experimental.pallas import tpu as pltpu
from jax.sharding import PartitionSpec as P

step_size = 0.02
mean_flow = 0.3
lift_factor = 12.0

E = 32
F = 192
S = 384
G = 128
f32 = jnp.float32
bf16 = jnp.bfloat16
i32 = jnp.int32


def derivative_table():
    points = np.array([-1.0, -1.0 / np.sqrt(5.0), 1.0 / np.sqrt(5.0), 1.0])
    products = np.array(
        [np.prod([points[t] - points[s] for s in range(4) if s != t]) for t in range(4)]
    )
    result = np.zeros((4, 4))
    for t in range(4):
        for s in range(4):
            if t != s:
                result[t, s] = products[t] / (products[s] * (points[t] - points[s]))
        result[t, t] = -np.sum(result[t])
    return result.astype(np.float32)


def halves_of(matrix):
    hi = matrix.astype(ml_dtypes.bfloat16)
    lo = (matrix - hi.astype(np.float32)).astype(ml_dtypes.bfloat16)
    return hi, lo


def derivative_operands():
    d = -2.0 * derivative_table()
    eye = np.eye(4, dtype=np.float32)
    along = [
        np.kron(d, np.kron(eye, eye)),
        np.kron(eye, np.kron(d, eye)),
        np.kron(eye, np.kron(eye, d)),
    ]
    two = [np.kron(np.eye(2, dtype=np.float32), a).astype(np.float32) for a in along]
    hi, lo = halves_of(np.concatenate([t.T for t in two], axis=0))
    forward = np.concatenate([hi, lo], axis=1)
    hi, lo = halves_of(np.concatenate(two, axis=1))
    backward = np.concatenate([hi, lo], axis=1)
    return forward, backward


def lanes(rows=1):
    return lax.broadcasted_iota(i32, (rows, 128), 1)


def take(x, index):
    return jnp.take_along_axis(x, jnp.broadcast_to(index, x.shape), axis=1)


def mask(condition):
    return jnp.where(condition, 1.0, 0.0).astype(f32)


def turn(x, shift):
    return pltpu.roll(x, shift, 1)


def halves(x):
    hi = x.astype(bf16)
    lo = (x - hi.astype(f32)).astype(bf16)
    return hi, lo


def dot(a, b):
    return jnp.dot(a, b, preferred_element_type=f32)


def select_rows(onehot, x):
    hi, lo = halves(x)
    r = dot(onehot, jnp.concatenate([hi, lo], axis=1))
    return r[:, :128] + r[:, 128:]


def to_tiles(ref):
    zero = jnp.zeros((E, 64), f32)
    tiles = []
    for j in range(3):
        high = ref[2 * j + 1] if j < 2 else zero
        tiles.append(jnp.concatenate([ref[2 * j], high], axis=1))
    return tiles


def from_tiles(tiles, ref):
    for j in range(3):
        ref[2 * j] = tiles[j][:, :64]
        if j < 2:
            ref[2 * j + 1] = tiles[j][:, 64:]


def load_tiles(ref):
    return [ref[:, 128 * j : 128 * (j + 1)] for j in range(3)]


def store_tiles(ref, tiles):
    for j in range(3):
        ref[:, 128 * j : 128 * (j + 1)] = tiles[j]


def spread(tiles):
    low = lanes(E) < 64
    back0, back1, back2 = turn(tiles[0], 64), turn(tiles[1], 64), turn(tiles[2], 64)
    ux = jnp.where(low, back0, tiles[0])
    uy = jnp.where(low, tiles[1], back1)
    uz = jnp.where(low, back1, tiles[1])
    p = tiles[2] + back2
    return low, (ux, uy, uz), p


def volume(tiles, table):
    low, speeds, p = spread(tiles)
    fluxes = []
    for a in range(3):
        u = speeds[a]
        c = u + mean_flow if a == 0 else u
        high0 = p if a == 0 else jnp.zeros_like(p)
        parts = [c * tiles[0] + jnp.where(low, u, high0), c * tiles[1], c * tiles[2] + jnp.where(low, u, 0.0)]
        if a == 1:
            parts[1] = parts[1] + jnp.where(low, p, 0.0)
        if a == 2:
            parts[1] = parts[1] + jnp.where(low, 0.0, p)
        fluxes.append(jnp.concatenate(parts, axis=0))
    hi, lo = halves(jnp.concatenate(fluxes, axis=1))
    r = dot(jnp.concatenate([hi, lo], axis=0), table)
    out = r[:96, :128] + (r[:96, 128:] + r[96:, :128])
    return [out[:32], out[32:64], out[64:96]]


def derivative_back(tiles, table):
    hi, lo = halves(jnp.concatenate(tiles, axis=0))
    r = dot(jnp.concatenate([hi, lo], axis=0), table)
    return r[:96, :384] + (r[:96, 384:] + r[96:, :384])


def volume_back(tiles, z):
    low, speeds, _ = spread(tiles)
    one = jnp.where(low, 1.0, 0.0).astype(f32)
    plus = [tiles[0] + one, tiles[1], tiles[2] + one]
    out = [jnp.zeros((E, 128), f32) for _ in range(3)]
    sums = []
    parts = []
    for a in range(3):
        c = speeds[a] + mean_flow if a == 0 else speeds[a]
        za = [z[32 * j : 32 * (j + 1), 128 * a : 128 * (a + 1)] for j in range(3)]
        total = plus[0] * za[0] + plus[1] * za[1] + plus[2] * za[2]
        sums.append(total + turn(total, 64))
        parts.append(za)
        out = [out[j] + c * za[j] for j in range(3)]
    pressure = turn(parts[0][0], 64) + parts[1][1] + turn(parts[2][1], 64)
    out[0] = out[0] + jnp.where(low, 0.0, sums[0])
    out[1] = out[1] + jnp.where(low, sums[1], sums[2])
    out[2] = out[2] + jnp.where(low, pressure, 0.0)
    return out


def traces(tiles):
    lane = lanes()
    wide = lanes(E)
    m = lane & 15
    r, s = m >> 2, m & 3
    base = ((lane >> 4) & 1) * 64
    rows = []
    for f in range(6):
        b = f % 2
        index = base + (48 * b + m, 16 * r + 12 * b + s, 4 * m + 3 * b)[f // 2]
        index = jnp.where(lane < 80, index, 64)
        t = jnp.where(
            wide < 32,
            take(tiles[0], index),
            jnp.where(wide < 64, take(tiles[1], index), take(tiles[2], index)),
        )
        rows.append(t)
    return jnp.concatenate(rows, axis=0)


def lifted(x):
    lane = lanes()
    wide = lanes(E)
    n = lane & 63
    i, j, k = n >> 4, (n >> 2) & 3, n & 3
    places = (4 * j + k, 4 * i + k, 4 * i + j)
    layers = (i, j, k)
    wide_layers = ((wide >> 4) & 3, (wide >> 2) & 3, wide & 3)
    tiles = [None] * 3
    for a in range(3):
        first, last = x[64 * a : 64 * a + 32], turn(x[64 * a + 32 : 64 * a + 64], 64)
        pair = jnp.where(wide < 64, first, last)
        tail = jnp.where(wide < 16, last, first)
        ends = (wide_layers[a] == 0) | (wide_layers[a] == 3)
        for tile in range(3):
            v = 2 * tile + (lane >> 6)
            index = v * 16 + places[a]
            at_last = jnp.where(layers[a] == 3, 64, 0)
            if tile < 2:
                part = take(pair, index + at_last)
            else:
                part = take(tail, jnp.where(lane < 64, index - at_last, 80))
            part = jnp.where(ends, part, 0.0)
            tiles[tile] = part if tiles[tile] is None else tiles[tile] + part
    return tiles


def lifted_traces(x):
    lane = lanes()
    wide = lanes(E)
    v16 = lane & 112
    r, s = (lane >> 2) & 3, lane & 3
    wide_r, wide_s = (wide >> 2) & 3, wide & 3
    rows = []
    for f in range(6):
        a, b = f // 2, f % 2
        total = x[32 * f : 32 * (f + 1)]
        for place, side in ((0, wide_r), (1, wide_s)):
            axis = [other for other in range(3) if other != a][place]
            free = (s, r)[place]
            node = 12 * b + free if a < [o for o in range(3) if o != axis and o != a][0] else 4 * free + 3 * b
            index = v16 + node
            first = take(x[64 * axis : 64 * axis + 32], index)
            last = take(x[64 * axis + 32 : 64 * axis + 64], index)
            total = total + jnp.where(side == 0, first, jnp.where(side == 3, last, 0.0))
        rows.append(total)
    return jnp.concatenate(rows, axis=0)


def by_axis(function, *arrays):
    return jnp.concatenate(
        [function(a, *[x[64 * a : 64 * (a + 1)] for x in arrays]) for a in range(3)], axis=0)


def signed(x):
    return jnp.concatenate([-x[:32], x[32:]], axis=0)


class Faces:
    def __init__(self):
        lane = lanes()
        self.v = lane >> 4
        self.m = lane & 15
        self.ends = mask((self.v == 0) | (self.v == 4))
        self.last = mask(self.v == 4)
        self.normal = [mask(self.v == a + 1) for a in range(3)]
        self.normal_index = [(a + 1) * 16 + self.m for a in range(3)]
        self.pressure_index = 64 + self.m

    def normal_of(self, x):
        return by_axis(lambda a, x: take(x, self.normal_index[a]), x)

    def pressure_of(self, x):
        return take(x, self.pressure_index)

    def flux(self, x, u=None, p=None):
        u = self.normal_of(x) if u is None else u
        p = self.pressure_of(x) if p is None else p

        def along(a, x, u, p):
            c = u + mean_flow if a == 0 else u
            return signed(c * x + self.ends * u + self.normal[a] * p)

        return by_axis(along, x, u, p)

    def flux_back(self, x, u, w):
        def along(a, x, u, w, h):
            n = take(w, self.normal_index[a])
            c = u + mean_flow if a == 0 else u
            return signed(c * w + self.last * n + self.normal[a] * h)

        return by_axis(along, x, u, w, over_fields((x + self.ends) * w))

    def rest_back(self, w):
        def along(a, w, h):
            n = take(w, self.normal_index[a])
            part = self.last * n + self.normal[a] * h
            return signed(mean_flow * w + part if a == 0 else part)

        return by_axis(along, w, over_fields(self.ends * w))

    def state_back(self, x, u, w):
        def along(a, u, w, h):
            return signed(u * w + self.normal[a] * h)

        return by_axis(along, u, w, over_fields(x * w))

    def shifted(self, d):
        target = self.v + d
        target = jnp.where(target >= 5, target - 5, target)
        return target, jnp.where(self.v < 5, target * 16 + self.m, 16 * self.v + self.m)

    def hessian(self, d, y):
        target, index = self.shifted(d)

        def along(a, y):
            back = mask((self.v < 5) & (target == a + 1))
            return signed(-0.5 * (self.normal[a] * take(y, index) + back * y))

        return by_axis(along, y)

    def mirror(self, x):
        return by_axis(lambda a, x: x * (1.0 - 2.0 * self.normal[a]), x)


def over_fields(h):
    table = ((lax.broadcasted_iota(i32, (128, 128), 0) ^ lax.broadcasted_iota(i32, (128, 128), 1)) & 15) == 0
    table = mask(table).astype(bf16)
    hi, lo = halves(h)
    return dot(jnp.concatenate([hi, lo], axis=1), jnp.concatenate([table, table], axis=0))


def column_of(table_ref):
    x = table_ref[...].astype(f32)
    x = jnp.concatenate([x, jnp.zeros((2, E), f32)], axis=0)
    t = jnp.transpose(x)
    return jnp.concatenate([t[:, f : f + 1] for f in range(6)], axis=0).astype(i32)


def row_of(table_ref):
    return jnp.concatenate([table_ref[f : f + 1, :] for f in range(6)], axis=1)


def slot_column(send):
    x = jnp.broadcast_to(send.astype(f32), (8, S))
    return jnp.transpose(x)[:, :1].astype(i32)


def onehot(rows, columns, first, second):
    return jnp.where(first == second, 1.0, 0.0).astype(bf16)


def faces_from_columns(ext_col):
    return onehot(F, F, ext_col, lax.broadcasted_iota(i32, (F, F), 1))


def columns_from_faces(ext_row):
    return onehot(F, F, ext_row, lax.broadcasted_iota(i32, (F, F), 0))


def faces_from_slots(ext_col):
    return onehot(F, S, ext_col - F, lax.broadcasted_iota(i32, (F, S), 1))


def slots_from_faces(ext_row):
    return onehot(S, F, ext_row - F, lax.broadcasted_iota(i32, (S, F), 0))


def slots_from_columns(send_col):
    return onehot(S, F, send_col, lax.broadcasted_iota(i32, (S, F), 1))


def columns_from_slots(send_row):
    return onehot(F, S, send_row, lax.broadcasted_iota(i32, (F, S), 0))


def orientation(perm_col):
    lane = lanes(F)
    m = lane & 15
    crossed = lane - m + ((m & 3) * 4 + (m >> 2))
    k = jnp.broadcast_to(perm_col, (F, 128))
    flips = (k & 1) * 12 + ((k & 2) >> 1) * 3
    crossed_flips = (k & 1) * 3 + ((k & 2) >> 1) * 12
    swap = (k & 4) == 4
    place = jnp.where(swap, crossed, lane)
    return place ^ jnp.where(swap, crossed_flips, flips), place ^ flips


def peer_tables(send_ref, ext_ref):
    odd = (lax.axis_index("dom") & 1) == 1
    send = send_ref[...]
    swapped = jnp.concatenate([send[:, 2 * G :], send[:, G : 2 * G], send[:, :G]], axis=1)
    send = jnp.where(odd, send, swapped)

    def reordered(table):
        slot = table - F
        turned = jnp.where(slot < G, slot + 2 * G, jnp.where(slot >= 2 * G, slot - 2 * G, slot))
        turned = jnp.where((slot >= 0) & (slot < S), turned + F, table)
        return jnp.where(odd, turned, table)

    return send, reordered(column_of(ext_ref)), reordered(row_of(ext_ref))


def packed(x):
    tail = lanes(F) >= 80
    first = jnp.where(tail, turn(x, 80), 0.0)
    second = jnp.where(tail, turn(x, 32), 0.0)
    return jnp.concatenate([first, second], axis=1).astype(bf16)


def exterior(faces, wall, index, onehot_local, t, u):
    g = select_rows(onehot_local, t)
    node = index & 15
    x = jnp.where(wall, faces.mirror(t), take(g, index))
    v = by_axis(lambda a, g, node: take(g, (a + 1) * 16 + node), g, node)
    return x, jnp.where(wall, -u, v)


def places():
    own = jnp.where((lax.axis_index("dom") & 1) == 1, 0, 8)
    return own, 8 - own


def block_of(ref, row, start=0):
    return ref[pl.ds(start, 8), row : row + 16].reshape(G, 128)


def pack_kernel(state_hbm, final_hbm, send_hbm, ext_hbm, perm_hbm,
                chip_ref, out_ref, q_ref, w_ref, t_ref, lam_ref, send_slots_ref, back_slots_ref, inverse_ref,
                send_ref, ext_ref, perm_ref, state_ref, final_ref, sems):
    pairs = ((send_hbm, send_ref), (ext_hbm, ext_ref), (perm_hbm, perm_ref), (final_hbm, final_ref), (state_hbm, state_ref))
    copies = [pltpu.make_async_copy(a, b, sems.at[i]) for i, (a, b) in enumerate(pairs)]
    for copy in copies:
        copy.start()
    faces = Faces()
    for copy in copies[:3]:
        copy.wait()
    send, _, ext_row = peer_tables(send_ref, ext_ref)
    send_slots = slots_from_columns(slot_column(send))
    back_slots = slots_from_faces(ext_row)
    send_slots_ref[...] = send_slots
    back_slots_ref[...] = back_slots
    _, inverse = orientation(column_of(perm_ref))
    inverse_ref[...] = inverse
    for copy in copies[3:]:
        copy.wait()
    q = to_tiles(state_ref)
    w = to_tiles(final_ref)
    store_tiles(q_ref, q)
    store_tiles(w_ref, w)
    t = traces(q)
    lam = lift_factor * traces(w)
    t_ref[...] = t
    lam_ref[...] = lam
    y = take(lam, inverse)
    diagonal = by_axis(lambda a, y: signed(-faces.normal[a] * y), y)
    first = y - 0.5 * faces.rest_back(y) + turn(diagonal, 64)
    stack = jnp.concatenate([x.astype(bf16) for x in (first, faces.hessian(1, y), faces.hessian(2, y))], axis=1)
    back = dot(back_slots, stack)
    forward = dot(send_slots, packed(t))
    whole = jnp.concatenate([back[:, :128], back[:, 128:] + forward], axis=1).astype(bf16)
    own, other = places()
    for peer in range(8):
        for o, ref, place in ((0, chip_ref, 0), (1, out_ref, own), (2, out_ref, other)):
            at = G * o + 16 * peer
            for j in range(3):
                ref[place + peer, 16 * j : 16 * (j + 1)] = whole[at : at + 16, 128 * j : 128 * (j + 1)]


def first_local_kernel(q_ref, w_ref, t_ref, lam_ref, send_ref, ext_ref, perm_ref, forward_ref, backward_ref,
                       base_ref, t_base_ref, z_ref, rest_ref, u_ref, x_ref, v_ref,
                       from_slots_ref, to_columns_ref, local_ref, local_back_ref, index_ref, kind_ref):
    faces = Faces()
    send, ext_col, ext_row = peer_tables(send_ref, ext_ref)
    index, _ = orientation(column_of(perm_ref))
    index_ref[...] = index
    ext_wide = jnp.broadcast_to(ext_col, (F, 128))
    wall = ext_wide == F + S
    kind_ref[...] = jnp.where(wall, 2, jnp.where(ext_wide >= F, 1, 0))
    from_slots_ref[...] = faces_from_slots(ext_col)
    to_columns_ref[...] = columns_from_slots(send)
    local = faces_from_columns(ext_col)
    local_ref[...] = local
    local_back_ref[...] = columns_from_faces(ext_row)
    q = load_tiles(q_ref)
    t = t_ref[...]
    lam = lam_ref[...]
    rest_ref[...] = lam - 0.5 * faces.rest_back(lam)
    u = faces.normal_of(t)
    x, v = exterior(faces, wall, index, local, t, u)
    u_ref[...] = u
    x_ref[...] = x
    v_ref[...] = v
    jump = 0.5 * (faces.flux(t, u) - faces.flux(x, v)) + (x - t)
    faced = lifted(lift_factor * jump)
    inner = volume(q, forward_ref[...])
    base = [q[j] + step_size * (inner[j] + faced[j]) for j in range(3)]
    store_tiles(base_ref, base)
    t_base_ref[...] = traces(base)
    z_ref[...] = derivative_back(load_tiles(w_ref), backward_ref[...])


def middle_kernel(base_ref, t_base_ref, w_ref, lam_ref, rest_ref, z_ref, arrived_ref,
                  from_slots_ref, to_columns_ref, local_ref, local_back_ref, send_slots_ref, back_slots_ref,
                  index_ref, inverse_ref, kind_ref,
                  out_ref, q1_ref, w1_ref, t1_ref, u1_ref, x1_ref, v1_ref, lam1_ref):
    faces = Faces()
    index = index_ref[...]
    inverse = inverse_ref[...]
    kind = kind_ref[...]
    wall = kind == 2
    wide = lanes(F)
    lane = lanes()
    node = index & 15
    own, other = places()
    arrived = jnp.concatenate(
        [jnp.concatenate([block_of(arrived_ref, row + 16 * j, start) for j in range(3)], axis=1)
         for row, start in ((48, own), (0, own), (0, other))], axis=0)
    g = dot(from_slots_ref[...], arrived[:, 128:])
    sums = dot(to_columns_ref[...], arrived)
    g0, g1 = g[:, :128], g[:, 128:]
    place = jnp.where(wide < 48, index + 80, jnp.where(wide < 80, index + 32, 112 + node))
    xr = jnp.where(wide < 48, take(g0, place), take(g1, place))
    ur = jnp.concatenate(
        [take(g0[:64], 96 + node[:64]), take(g0[64:128], 112 + node[64:128]), take(g1[128:], 80 + node[128:])], axis=0)
    pr = take(g1, 96 + node)
    jump = (lift_factor * step_size) * (xr - 0.5 * faces.flux(xr, ur, pr))
    t1 = t_base_ref[...] + lifted_traces(jump)
    faced = lifted(jump)
    base = load_tiles(base_ref)
    q1 = [base[j] + faced[j] for j in range(3)]
    store_tiles(q1_ref, q1)
    t1_ref[...] = t1
    t1_sent = t1.astype(bf16)
    forward = dot(send_slots_ref[...], t1_sent)
    lam = lam_ref[...]
    rest = rest_ref[...]
    u1 = faces.normal_of(t1)
    u1_ref[...] = u1
    x1, v1 = exterior(faces, wall, index, local_ref[...], t1, u1)
    x1_ref[...] = x1
    v1_ref[...] = v1
    bar = jnp.where(kind == 1, 0.0, rest - 0.5 * faces.state_back(x1, v1, lam))
    total = 0.5 * faces.state_back(t1, u1, lam) - rest + jnp.where(wall, faces.mirror(bar), 0.0)
    total = total + select_rows(local_back_ref[...], take(bar, inverse))
    sent = t1_sent.astype(f32)
    h0, h1, h2 = sums[:, :128], sums[:, 128:256], sums[:, 256:]
    ahead1, ahead2, behind2, behind1 = [faces.shifted(d)[1] for d in (1, 2, 3, 4)]
    through = h0 + h1 * take(sent, ahead1) + h2 * take(sent, ahead2)
    through = through + take(h1 * sent, behind1) + take(h2 * sent, behind2)
    through = through + mask((lane >= 16) & (lane < 64)) * turn(h0, 64) * sent
    total = total + mask(lane < 80) * through
    inner = volume_back(q1, z_ref[...])
    w = load_tiles(w_ref)
    half = [0.5 * w[j] + (0.5 * step_size) * inner[j] for j in range(3)]
    lam1 = lift_factor * traces(half) + (0.5 * step_size * lift_factor) * lifted_traces(total)
    faced = lifted(total)
    store_tiles(w1_ref, [half[j] + (0.5 * step_size) * faced[j] for j in range(3)])
    lam1_ref[...] = lam1
    bar = lam1 - 0.5 * faces.flux_back(xr, ur, lam1)
    first = take(bar, jnp.where(wide >= 80, inverse - 80, 80))
    second = take(bar, jnp.where(wide < 32, inverse + 48, 80))
    back = dot(back_slots_ref[...], jnp.concatenate([first, second], axis=1).astype(bf16))
    main = (back[:, :128] + forward).astype(bf16)
    tail = [back[G * o : G * (o + 1), 128:] for o in range(3)]
    shared = (tail[0] + turn(tail[1], 32)).astype(bf16)
    last = turn(tail[2], 64).astype(bf16)
    for peer in range(8):
        at = 16 * peer
        out_ref[own + peer, :16] = main[G + at : G + at + 16]
        out_ref[own + peer, 16:32] = main[at : at + 16]
        out_ref[own + peer, 32:] = shared[at : at + 16]
        out_ref[other + peer, :16] = main[2 * G + at : 2 * G + at + 16]
        out_ref[other + peer, 16:32] = jnp.zeros((16, 128), bf16)
        out_ref[other + peer, 32:] = last[at : at + 16]


def second_local_kernel(q_ref, w_ref, t_ref, u_ref, x_ref, v_ref, q1_ref, w1_ref, t1_ref, u1_ref, x1_ref, v1_ref,
                        lam1_ref, local_back_ref, inverse_ref, kind_ref,
                        forward_ref, backward_ref, end_ref, start_ref):
    faces = Faces()
    inverse = inverse_ref[...]
    kind = kind_ref[...]
    wall = kind == 2
    q = load_tiles(q_ref)
    q1 = load_tiles(q1_ref)
    t1 = t1_ref[...]
    x1 = x1_ref[...]
    jump = 0.5 * (faces.flux(t1, u1_ref[...]) - faces.flux(x1, v1_ref[...])) + (x1 - t1)
    faced = lifted(lift_factor * jump)
    inner = volume(q1, forward_ref[...])
    store_tiles(end_ref, [0.5 * q[j] + 0.5 * (q1[j] + step_size * (inner[j] + faced[j])) for j in range(3)])
    t = t_ref[...]
    lam1 = lam1_ref[...]
    u, x, v = u_ref[...], x_ref[...], v_ref[...]
    rest = lam1 - 0.5 * faces.rest_back(lam1)
    bar = jnp.where(kind == 1, 0.0, rest - 0.5 * faces.state_back(x, v, lam1))
    total = 0.5 * faces.state_back(t, u, lam1) - rest + jnp.where(wall, faces.mirror(bar), 0.0)
    total = total + select_rows(local_back_ref[...], take(bar, inverse))
    w = load_tiles(w_ref)
    w1 = load_tiles(w1_ref)
    inner = volume_back(q, derivative_back(w1, backward_ref[...]))
    faced = lifted(total)
    store_tiles(start_ref, [0.5 * w[j] + w1[j] + step_size * (inner[j] + faced[j]) for j in range(3)])


def last_kernel(end_base_ref, start_base_ref, chip_ref, arrived_ref, from_slots_ref, to_columns_ref, index_ref,
                end_ref, start_ref):
    faces = Faces()
    own, other = places()
    main = jnp.concatenate([block_of(chip_ref, 0), block_of(arrived_ref, 0, own), block_of(arrived_ref, 0, other)], axis=0)
    lane = lanes(G)
    zero = jnp.zeros((G, 128), bf16)
    shared = jnp.concatenate([
        jnp.where(lane < 32, block_of(chip_ref, 16), zero),
        jnp.where((lane >= 32) & (lane < 64), block_of(arrived_ref, 32, own), zero),
        jnp.where((lane >= 64) & (lane < 96), block_of(arrived_ref, 32, other), zero)], axis=0)
    node = index_ref[...] & 15
    g = dot(from_slots_ref[...], main)
    b = dot(to_columns_ref[...], jnp.concatenate([main, shared], axis=1))
    lane = lanes()
    valid = mask(lane < 80)
    xr = valid * take(g, index_ref[...])
    ur = by_axis(lambda a, g, node: take(g, (a + 1) * 16 + node), g, node)
    pr = take(g, 64 + node)
    faced = lifted((0.5 * step_size * lift_factor) * (xr - 0.5 * faces.flux(xr, ur, pr)))
    base = load_tiles(end_base_ref)
    from_tiles([base[j] + faced[j] for j in range(3)], end_ref)
    high = turn(b[:, 128:], 48) + turn(b[:, 128:], 16) + turn(b[:, 128:], 112)
    bar = mask(lane < 48) * turn(b[:, :128], 48) + mask((lane >= 48) & (lane < 80)) * high
    faced = lifted(step_size * bar)
    base = load_tiles(start_base_ref)
    from_tiles([base[j] + faced[j] for j in range(3)], start_ref)


def shape(*dims, dtype=f32):
    return jax.ShapeDtypeStruct(dims, dtype)


def call(kernel, outs, *args, scratch=(), in_hbm=False):
    return pl.pallas_call(
        kernel,
        out_shape=outs,
        in_specs=[pl.BlockSpec(memory_space=pl.ANY if in_hbm else pltpu.VMEM)] * len(args),
        scratch_shapes=scratch,
        cost_estimate=pl.CostEstimate(flops=200_000_000, bytes_accessed=1_000_000, transcendentals=0),
        compiler_params=pltpu.CompilerParams(vmem_limit_bytes=32 * 1024 * 1024),
    )(*args)


def pair_peers(whole):
    count, peers = lax.axis_size("dom"), lax.axis_size("sub")
    groups = [[d % count * peers + peer for d in (first, first + 1) for peer in range(peers)]
              for first in range(1, count, 2)]
    return lax.all_to_all(
        whole, ("dom", "sub"), split_axis=0, concat_axis=0, tiled=True, axis_index_groups=groups)


def for_chip(arrived):
    return arrived[:8] + arrived[8:]


def chip_partner(value):
    return lax.ppermute(value, "dom", [(d, d ^ 1) for d in range(lax.axis_size("dom"))])


def shards(state, adjoint_final, send_slot, ext_index, ext_perm):
    forward, backward = derivative_operands()
    forward, backward = jnp.asarray(forward), jnp.asarray(backward)
    state, adjoint_final = jnp.swapaxes(state, 1, 2), jnp.swapaxes(adjoint_final, 1, 2)
    node = shape(E, 384)
    face = shape(F, 128)
    index_face = shape(F, 128, dtype=i32)

    to_chip, out, q, w, t, lam, send_slots, back_slots, inverse, send_slot, ext_index, ext_perm = call(
        pack_kernel,
        (shape(8, 48, 128, dtype=bf16), shape(16, 96, 128, dtype=bf16), node, node, face, face,
         shape(S, F, dtype=bf16), shape(S, F, dtype=bf16), index_face,
         shape(1, S, dtype=i32), shape(6, E, dtype=i32), shape(6, E, dtype=i32)),
        *[pltpu.with_memory_space_constraint(x, pltpu.HBM) for x in (state, adjoint_final, send_slot, ext_index, ext_perm)], in_hbm=True,
        scratch=[pltpu.VMEM((5, E, 64), f32), pltpu.VMEM((5, E, 64), f32), pltpu.SemaphoreType.DMA((5,))])
    from_chip = chip_partner(to_chip)
    base, t_base, z, rest, u, x, v, from_slots, to_columns, local, local_back, index, kind = call(
        first_local_kernel,
        (node, face, shape(96, 384), face, face, face, face, shape(F, S, dtype=bf16), shape(F, S, dtype=bf16),
         shape(F, F, dtype=bf16), shape(F, F, dtype=bf16), index_face, index_face),
        q, w, t, lam, send_slot, ext_index, ext_perm, forward, backward)
    out = lax.dynamic_update_slice(out, from_chip, (0, 48, 0))
    out = lax.dynamic_update_slice(out, from_chip, (8, 48, 0))
    out, z = lax.optimization_barrier((out, z))
    arrived = pair_peers(out)
    out, q1, w1, t1, u1, x1, v1, lam1 = call(
        middle_kernel, (shape(16, 48, 128, dtype=bf16), node, node, face, face, face, face, face),
        base, t_base, w, lam, rest, z, arrived,
        from_slots, to_columns, local, local_back, send_slots, back_slots, index, inverse, kind)
    arrived = pair_peers(out)
    end_base, start_base = call(
        second_local_kernel, (node, node),
        q, w, t, u, x, v, q1, w1, t1, u1, x1, v1, lam1, local_back, inverse, kind, forward, backward)
    from_chip = chip_partner(for_chip(arrived[:, 16:]))
    out = shape(5, E, 64)
    end, start = call(
        last_kernel, (out, out),
        end_base, start_base, from_chip, arrived, from_slots, to_columns, index)
    return jnp.swapaxes(end, 1, 2), jnp.swapaxes(start, 1, 2)


def solution(mesh):
    return jax.shard_map(
        shards,
        mesh=mesh,
        in_specs=(
            P(None, None, ("dom", "sub")),
            P(None, None, ("dom", "sub")),
            P(("dom", "sub"), None),
            P(None, ("dom", "sub")),
            P(None, ("dom", "sub")),
        ),
        out_specs=(P(None, None, ("dom", "sub")), P(None, None, ("dom", "sub"))),
        check_vma=False,
    )
```

```python
import jax
import jax.numpy as jnp
import numpy as np
import ml_dtypes
from jax import lax
from jax.experimental import pallas as pl
from jax.experimental.pallas import tpu as pltpu
from jax.sharding import PartitionSpec as P

step_size = 0.02
mean_flow = 0.3
lift_factor = 12.0

E = 32
F = 192
S = 384
G = 128
f32 = jnp.float32
bf16 = jnp.bfloat16
i32 = jnp.int32


def derivative_table():
    points = np.array([-1.0, -1.0 / np.sqrt(5.0), 1.0 / np.sqrt(5.0), 1.0])
    products = np.array(
        [np.prod([points[t] - points[s] for s in range(4) if s != t]) for t in range(4)]
    )
    result = np.zeros((4, 4))
    for t in range(4):
        for s in range(4):
            if t != s:
                result[t, s] = products[t] / (products[s] * (points[t] - points[s]))
        result[t, t] = -np.sum(result[t])
    return result.astype(np.float32)


def halves_of(matrix):
    hi = matrix.astype(ml_dtypes.bfloat16)
    lo = (matrix - hi.astype(np.float32)).astype(ml_dtypes.bfloat16)
    return hi, lo


def derivative_operands():
    d = -2.0 * derivative_table()
    eye = np.eye(4, dtype=np.float32)
    along = [
        np.kron(d, np.kron(eye, eye)),
        np.kron(eye, np.kron(d, eye)),
        np.kron(eye, np.kron(eye, d)),
    ]
    two = [np.kron(np.eye(2, dtype=np.float32), a).astype(np.float32) for a in along]
    hi, lo = halves_of(np.concatenate([t.T for t in two], axis=0))
    forward = np.concatenate([hi, lo], axis=1)
    hi, lo = halves_of(np.concatenate(two, axis=1))
    backward = np.concatenate([hi, lo], axis=1)
    return forward, backward


def lanes(rows=1):
    return lax.broadcasted_iota(i32, (rows, 128), 1)


def take(x, index):
    return jnp.take_along_axis(x, jnp.broadcast_to(index, x.shape), axis=1)


def mask(condition):
    return jnp.where(condition, 1.0, 0.0).astype(f32)


def turn(x, shift):
    return pltpu.roll(x, shift, 1)


def halves(x):
    hi = x.astype(bf16)
    lo = (x - hi.astype(f32)).astype(bf16)
    return hi, lo


def dot(a, b):
    return jnp.dot(a, b, preferred_element_type=f32)


def select_rows(onehot, x):
    hi, lo = halves(x)
    r = dot(onehot, jnp.concatenate([hi, lo], axis=1))
    return r[:, :128] + r[:, 128:]


def to_tiles(ref):
    zero = jnp.zeros((E, 64), f32)
    tiles = []
    for j in range(3):
        high = ref[2 * j + 1] if j < 2 else zero
        tiles.append(jnp.concatenate([ref[2 * j], high], axis=1))
    return tiles


def from_tiles(tiles, ref):
    for j in range(3):
        ref[2 * j] = tiles[j][:, :64]
        if j < 2:
            ref[2 * j + 1] = tiles[j][:, 64:]


def load_tiles(ref):
    return [ref[:, 128 * j : 128 * (j + 1)] for j in range(3)]


def store_tiles(ref, tiles):
    for j in range(3):
        ref[:, 128 * j : 128 * (j + 1)] = tiles[j]


def spread(tiles):
    low = lanes(E) < 64
    back0, back1, back2 = turn(tiles[0], 64), turn(tiles[1], 64), turn(tiles[2], 64)
    ux = jnp.where(low, back0, tiles[0])
    uy = jnp.where(low, tiles[1], back1)
    uz = jnp.where(low, back1, tiles[1])
    p = tiles[2] + back2
    return low, (ux, uy, uz), p


def volume(tiles, table):
    low, speeds, p = spread(tiles)
    fluxes = []
    for a in range(3):
        u = speeds[a]
        c = u + mean_flow if a == 0 else u
        high0 = p if a == 0 else jnp.zeros_like(p)
        parts = [c * tiles[0] + jnp.where(low, u, high0), c * tiles[1], c * tiles[2] + jnp.where(low, u, 0.0)]
        if a == 1:
            parts[1] = parts[1] + jnp.where(low, p, 0.0)
        if a == 2:
            parts[1] = parts[1] + jnp.where(low, 0.0, p)
        fluxes.append(jnp.concatenate(parts, axis=0))
    hi, lo = halves(jnp.concatenate(fluxes, axis=1))
    r = dot(jnp.concatenate([hi, lo], axis=0), table)
    out = r[:96, :128] + (r[:96, 128:] + r[96:, :128])
    return [out[:32], out[32:64], out[64:96]]


def derivative_back(tiles, table):
    hi, lo = halves(jnp.concatenate(tiles, axis=0))
    r = dot(jnp.concatenate([hi, lo], axis=0), table)
    return r[:96, :384] + (r[:96, 384:] + r[96:, :384])


def volume_back(tiles, z):
    low, speeds, _ = spread(tiles)
    one = jnp.where(low, 1.0, 0.0).astype(f32)
    plus = [tiles[0] + one, tiles[1], tiles[2] + one]
    out = [jnp.zeros((E, 128), f32) for _ in range(3)]
    sums = []
    parts = []
    for a in range(3):
        c = speeds[a] + mean_flow if a == 0 else speeds[a]
        za = [z[32 * j : 32 * (j + 1), 128 * a : 128 * (a + 1)] for j in range(3)]
        total = plus[0] * za[0] + plus[1] * za[1] + plus[2] * za[2]
        sums.append(total + turn(total, 64))
        parts.append(za)
        out = [out[j] + c * za[j] for j in range(3)]
    pressure = turn(parts[0][0], 64) + parts[1][1] + turn(parts[2][1], 64)
    out[0] = out[0] + jnp.where(low, 0.0, sums[0])
    out[1] = out[1] + jnp.where(low, sums[1], sums[2])
    out[2] = out[2] + jnp.where(low, pressure, 0.0)
    return out


def traces(tiles):
    lane = lanes()
    wide = lanes(E)
    m = lane & 15
    r, s = m >> 2, m & 3
    base = ((lane >> 4) & 1) * 64
    rows = []
    for f in range(6):
        b = f % 2
        index = base + (48 * b + m, 16 * r + 12 * b + s, 4 * m + 3 * b)[f // 2]
        index = jnp.where(lane < 80, index, 64)
        t = jnp.where(
            wide < 32,
            take(tiles[0], index),
            jnp.where(wide < 64, take(tiles[1], index), take(tiles[2], index)),
        )
        rows.append(t)
    return jnp.concatenate(rows, axis=0)


def lifted(x):
    lane = lanes()
    wide = lanes(E)
    n = lane & 63
    i, j, k = n >> 4, (n >> 2) & 3, n & 3
    places = (4 * j + k, 4 * i + k, 4 * i + j)
    layers = (i, j, k)
    wide_layers = ((wide >> 4) & 3, (wide >> 2) & 3, wide & 3)
    tiles = [None] * 3
    for a in range(3):
        first, last = x[64 * a : 64 * a + 32], turn(x[64 * a + 32 : 64 * a + 64], 64)
        pair = jnp.where(wide < 64, first, last)
        tail = jnp.where(wide < 16, last, first)
        ends = (wide_layers[a] == 0) | (wide_layers[a] == 3)
        for tile in range(3):
            v = 2 * tile + (lane >> 6)
            index = v * 16 + places[a]
            at_last = jnp.where(layers[a] == 3, 64, 0)
            if tile < 2:
                part = take(pair, index + at_last)
            else:
                part = take(tail, jnp.where(lane < 64, index - at_last, 80))
            part = jnp.where(ends, part, 0.0)
            tiles[tile] = part if tiles[tile] is None else tiles[tile] + part
    return tiles


def lifted_traces(x):
    lane = lanes()
    wide = lanes(E)
    v16 = lane & 112
    r, s = (lane >> 2) & 3, lane & 3
    wide_r, wide_s = (wide >> 2) & 3, wide & 3
    rows = []
    for f in range(6):
        a, b = f // 2, f % 2
        total = x[32 * f : 32 * (f + 1)]
        for place, side in ((0, wide_r), (1, wide_s)):
            axis = [other for other in range(3) if other != a][place]
            free = (s, r)[place]
            node = 12 * b + free if a < [o for o in range(3) if o != axis and o != a][0] else 4 * free + 3 * b
            index = v16 + node
            first = take(x[64 * axis : 64 * axis + 32], index)
            last = take(x[64 * axis + 32 : 64 * axis + 64], index)
            total = total + jnp.where(side == 0, first, jnp.where(side == 3, last, 0.0))
        rows.append(total)
    return jnp.concatenate(rows, axis=0)


def by_axis(function, *arrays):
    return jnp.concatenate(
        [function(a, *[x[64 * a : 64 * (a + 1)] for x in arrays]) for a in range(3)], axis=0)


def signed(x):
    return jnp.concatenate([-x[:32], x[32:]], axis=0)


class Faces:
    def __init__(self):
        lane = lanes()
        self.v = lane >> 4
        self.m = lane & 15
        self.ends = mask((self.v == 0) | (self.v == 4))
        self.last = mask(self.v == 4)
        self.normal = [mask(self.v == a + 1) for a in range(3)]
        self.normal_index = [(a + 1) * 16 + self.m for a in range(3)]
        self.pressure_index = 64 + self.m

    def normal_of(self, x):
        return by_axis(lambda a, x: take(x, self.normal_index[a]), x)

    def pressure_of(self, x):
        return take(x, self.pressure_index)

    def flux(self, x, u=None, p=None):
        u = self.normal_of(x) if u is None else u
        p = self.pressure_of(x) if p is None else p

        def along(a, x, u, p):
            c = u + mean_flow if a == 0 else u
            return signed(c * x + self.ends * u + self.normal[a] * p)

        return by_axis(along, x, u, p)

    def flux_back(self, x, u, w):
        def along(a, x, u, w, h):
            n = take(w, self.normal_index[a])
            c = u + mean_flow if a == 0 else u
            return signed(c * w + self.last * n + self.normal[a] * h)

        return by_axis(along, x, u, w, over_fields((x + self.ends) * w))

    def rest_back(self, w):
        def along(a, w, h):
            n = take(w, self.normal_index[a])
            part = self.last * n + self.normal[a] * h
            return signed(mean_flow * w + part if a == 0 else part)

        return by_axis(along, w, over_fields(self.ends * w))

    def state_back(self, x, u, w):
        def along(a, u, w, h):
            return signed(u * w + self.normal[a] * h)

        return by_axis(along, u, w, over_fields(x * w))

    def shifted(self, d):
        target = self.v + d
        target = jnp.where(target >= 5, target - 5, target)
        return target, jnp.where(self.v < 5, target * 16 + self.m, 16 * self.v + self.m)

    def hessian(self, d, y):
        target, index = self.shifted(d)

        def along(a, y):
            back = mask((self.v < 5) & (target == a + 1))
            return signed(-0.5 * (self.normal[a] * take(y, index) + back * y))

        return by_axis(along, y)

    def mirror(self, x):
        return by_axis(lambda a, x: x * (1.0 - 2.0 * self.normal[a]), x)


def over_fields(h):
    table = ((lax.broadcasted_iota(i32, (128, 128), 0) ^ lax.broadcasted_iota(i32, (128, 128), 1)) & 15) == 0
    table = mask(table).astype(bf16)
    hi, lo = halves(h)
    return dot(jnp.concatenate([hi, lo], axis=1), jnp.concatenate([table, table], axis=0))


def column_of(table_ref):
    x = table_ref[...].astype(f32)
    x = jnp.concatenate([x, jnp.zeros((2, E), f32)], axis=0)
    t = jnp.transpose(x)
    return jnp.concatenate([t[:, f : f + 1] for f in range(6)], axis=0).astype(i32)


def row_of(table_ref):
    return jnp.concatenate([table_ref[f : f + 1, :] for f in range(6)], axis=1)


def slot_column(send):
    x = jnp.broadcast_to(send.astype(f32), (8, S))
    return jnp.transpose(x)[:, :1].astype(i32)


def onehot(rows, columns, first, second):
    return jnp.where(first == second, 1.0, 0.0).astype(bf16)


def faces_from_columns(ext_col):
    return onehot(F, F, ext_col, lax.broadcasted_iota(i32, (F, F), 1))


def columns_from_faces(ext_row):
    return onehot(F, F, ext_row, lax.broadcasted_iota(i32, (F, F), 0))


def faces_from_slots(ext_col):
    return onehot(F, S, ext_col - F, lax.broadcasted_iota(i32, (F, S), 1))


def slots_from_faces(ext_row):
    return onehot(S, F, ext_row - F, lax.broadcasted_iota(i32, (S, F), 0))


def slots_from_columns(send_col):
    return onehot(S, F, send_col, lax.broadcasted_iota(i32, (S, F), 1))


def columns_from_slots(send_row):
    return onehot(F, S, send_row, lax.broadcasted_iota(i32, (F, S), 0))


def orientation(perm_col):
    lane = lanes(F)
    m = lane & 15
    crossed = lane - m + ((m & 3) * 4 + (m >> 2))
    k = jnp.broadcast_to(perm_col, (F, 128))
    flips = (k & 1) * 12 + ((k & 2) >> 1) * 3
    crossed_flips = (k & 1) * 3 + ((k & 2) >> 1) * 12
    swap = (k & 4) == 4
    place = jnp.where(swap, crossed, lane)
    return place ^ jnp.where(swap, crossed_flips, flips), place ^ flips


def peer_tables(send_ref, ext_ref):
    odd = (lax.axis_index("dom") & 1) == 1
    send = send_ref[...]
    swapped = jnp.concatenate([send[:, 2 * G :], send[:, G : 2 * G], send[:, :G]], axis=1)
    send = jnp.where(odd, send, swapped)

    def reordered(table):
        slot = table - F
        turned = jnp.where(slot < G, slot + 2 * G, jnp.where(slot >= 2 * G, slot - 2 * G, slot))
        turned = jnp.where((slot >= 0) & (slot < S), turned + F, table)
        return jnp.where(odd, turned, table)

    return send, reordered(column_of(ext_ref)), reordered(row_of(ext_ref))


def packed(x):
    tail = lanes(F) >= 80
    first = jnp.where(tail, turn(x, 80), 0.0)
    second = jnp.where(tail, turn(x, 32), 0.0)
    return jnp.concatenate([first, second], axis=1).astype(bf16)


def exterior(faces, wall, index, onehot_local, t, u):
    g = select_rows(onehot_local, t)
    node = index & 15
    x = jnp.where(wall, faces.mirror(t), take(g, index))
    v = by_axis(lambda a, g, node: take(g, (a + 1) * 16 + node), g, node)
    return x, jnp.where(wall, -u, v)


def places():
    own = jnp.where((lax.axis_index("dom") & 1) == 1, 0, 8)
    return own, 8 - own


def block_of(ref, row, start=0):
    return ref[pl.ds(start, 8), row : row + 16].reshape(G, 128)


def pack_kernel(state_hbm, final_hbm, send_hbm, ext_hbm, perm_hbm,
                chip_ref, out_ref, q_ref, w_ref, t_ref, lam_ref, send_slots_ref, back_slots_ref, inverse_ref,
                send_ref, ext_ref, perm_ref, state_ref, final_ref, sems):
    pairs = ((send_hbm, send_ref), (ext_hbm, ext_ref), (perm_hbm, perm_ref), (final_hbm, final_ref), (state_hbm, state_ref))
    copies = [pltpu.make_async_copy(a, b, sems.at[i]) for i, (a, b) in enumerate(pairs)]
    for copy in copies:
        copy.start()
    faces = Faces()
    for copy in copies[:3]:
        copy.wait()
    send, _, ext_row = peer_tables(send_ref, ext_ref)
    send_slots = slots_from_columns(slot_column(send))
    back_slots = slots_from_faces(ext_row)
    send_slots_ref[...] = send_slots
    back_slots_ref[...] = back_slots
    _, inverse = orientation(column_of(perm_ref))
    inverse_ref[...] = inverse
    for copy in copies[3:]:
        copy.wait()
    q = to_tiles(state_ref)
    w = to_tiles(final_ref)
    store_tiles(q_ref, q)
    store_tiles(w_ref, w)
    t = traces(q)
    lam = lift_factor * traces(w)
    t_ref[...] = t
    lam_ref[...] = lam
    y = take(lam, inverse)
    diagonal = by_axis(lambda a, y: signed(-faces.normal[a] * y), y)
    first = y - 0.5 * faces.rest_back(y) + turn(diagonal, 64)
    stack = jnp.concatenate([x.astype(bf16) for x in (first, faces.hessian(1, y), faces.hessian(2, y))], axis=1)
    back = dot(back_slots, stack)
    forward = dot(send_slots, packed(t))
    whole = jnp.concatenate([back[:, :128], back[:, 128:] + forward], axis=1).astype(bf16)
    own, other = places()
    for peer in range(8):
        for o, ref, place in ((0, chip_ref, 0), (1, out_ref, own), (2, out_ref, other)):
            at = G * o + 16 * peer
            for j in range(3):
                ref[place + peer, 16 * j : 16 * (j + 1)] = whole[at : at + 16, 128 * j : 128 * (j + 1)]


def first_local_kernel(q_ref, w_ref, t_ref, lam_ref, send_ref, ext_ref, perm_ref, forward_ref, backward_ref,
                       base_ref, t_base_ref, z_ref, rest_ref, u_ref, x_ref, v_ref,
                       from_slots_ref, to_columns_ref, local_ref, local_back_ref, index_ref, kind_ref):
    faces = Faces()
    send, ext_col, ext_row = peer_tables(send_ref, ext_ref)
    index, _ = orientation(column_of(perm_ref))
    index_ref[...] = index
    ext_wide = jnp.broadcast_to(ext_col, (F, 128))
    wall = ext_wide == F + S
    kind_ref[...] = jnp.where(wall, 2, jnp.where(ext_wide >= F, 1, 0))
    from_slots_ref[...] = faces_from_slots(ext_col)
    to_columns_ref[...] = columns_from_slots(send)
    local = faces_from_columns(ext_col)
    local_ref[...] = local
    local_back_ref[...] = columns_from_faces(ext_row)
    q = load_tiles(q_ref)
    t = t_ref[...]
    lam = lam_ref[...]
    rest_ref[...] = lam - 0.5 * faces.rest_back(lam)
    u = faces.normal_of(t)
    x, v = exterior(faces, wall, index, local, t, u)
    u_ref[...] = u
    x_ref[...] = x
    v_ref[...] = v
    jump = 0.5 * (faces.flux(t, u) - faces.flux(x, v)) + (x - t)
    faced = lifted(lift_factor * jump)
    inner = volume(q, forward_ref[...])
    base = [q[j] + step_size * (inner[j] + faced[j]) for j in range(3)]
    store_tiles(base_ref, base)
    t_base_ref[...] = traces(base)
    z_ref[...] = derivative_back(load_tiles(w_ref), backward_ref[...])


def middle_kernel(base_ref, t_base_ref, w_ref, lam_ref, rest_ref, z_ref, arrived_ref,
                  from_slots_ref, to_columns_ref, local_ref, local_back_ref, send_slots_ref, back_slots_ref,
                  index_ref, inverse_ref, kind_ref,
                  chip_ref, out_ref, q1_ref, w1_ref, t1_ref, u1_ref, x1_ref, v1_ref, lam1_ref):
    faces = Faces()
    index = index_ref[...]
    inverse = inverse_ref[...]
    kind = kind_ref[...]
    wall = kind == 2
    wide = lanes(F)
    lane = lanes()
    node = index & 15
    own, other = places()
    arrived = jnp.concatenate(
        [jnp.concatenate([block_of(arrived_ref, row + 16 * j, start) for j in range(3)], axis=1)
         for row, start in ((48, own), (0, own), (0, other))], axis=0)
    g = dot(from_slots_ref[...], arrived[:, 128:])
    sums = dot(to_columns_ref[...], arrived)
    g0, g1 = g[:, :128], g[:, 128:]
    place = jnp.where(wide < 48, index + 80, jnp.where(wide < 80, index + 32, 112 + node))
    xr = jnp.where(wide < 48, take(g0, place), take(g1, place))
    ur = jnp.concatenate(
        [take(g0[:64], 96 + node[:64]), take(g0[64:128], 112 + node[64:128]), take(g1[128:], 80 + node[128:])], axis=0)
    pr = take(g1, 96 + node)
    jump = (lift_factor * step_size) * (xr - 0.5 * faces.flux(xr, ur, pr))
    t1 = t_base_ref[...] + lifted_traces(jump)
    faced = lifted(jump)
    base = load_tiles(base_ref)
    q1 = [base[j] + faced[j] for j in range(3)]
    store_tiles(q1_ref, q1)
    t1_ref[...] = t1
    t1_sent = t1.astype(bf16)
    forward = dot(send_slots_ref[...], t1_sent)
    lam = lam_ref[...]
    rest = rest_ref[...]
    u1 = faces.normal_of(t1)
    u1_ref[...] = u1
    x1, v1 = exterior(faces, wall, index, local_ref[...], t1, u1)
    x1_ref[...] = x1
    v1_ref[...] = v1
    bar = jnp.where(kind == 1, 0.0, rest - 0.5 * faces.state_back(x1, v1, lam))
    total = 0.5 * faces.state_back(t1, u1, lam) - rest + jnp.where(wall, faces.mirror(bar), 0.0)
    total = total + select_rows(local_back_ref[...], take(bar, inverse))
    sent = t1_sent.astype(f32)
    h0, h1, h2 = sums[:, :128], sums[:, 128:256], sums[:, 256:]
    ahead1, ahead2, behind2, behind1 = [faces.shifted(d)[1] for d in (1, 2, 3, 4)]
    through = h0 + h1 * take(sent, ahead1) + h2 * take(sent, ahead2)
    through = through + take(h1 * sent, behind1) + take(h2 * sent, behind2)
    through = through + mask((lane >= 16) & (lane < 64)) * turn(h0, 64) * sent
    total = total + mask(lane < 80) * through
    inner = volume_back(q1, z_ref[...])
    w = load_tiles(w_ref)
    half = [0.5 * w[j] + (0.5 * step_size) * inner[j] for j in range(3)]
    lam1 = lift_factor * traces(half) + (0.5 * step_size * lift_factor) * lifted_traces(total)
    faced = lifted(total)
    store_tiles(w1_ref, [half[j] + (0.5 * step_size) * faced[j] for j in range(3)])
    lam1_ref[...] = lam1
    bar = lam1 - 0.5 * faces.flux_back(xr, ur, lam1)
    first = take(bar, jnp.where(wide >= 80, inverse - 80, 80))
    second = take(bar, jnp.where(wide < 32, inverse + 48, 80))
    back = dot(back_slots_ref[...], jnp.concatenate([first, second], axis=1).astype(bf16))
    main = (back[:, :128] + forward).astype(bf16)
    tail = [back[G * o : G * (o + 1), 128:] for o in range(3)]
    tail = [tail[0].astype(bf16), turn(tail[1], 32).astype(bf16), turn(tail[2], 64).astype(bf16)]
    zero = jnp.zeros((16, 128), bf16)
    for peer in range(8):
        at = 16 * peer
        chip_ref[peer, :16] = main[at : at + 16]
        chip_ref[peer, 16:] = tail[0][at : at + 16]
        for o, place in ((1, own), (2, other)):
            out_ref[place + peer, :16] = main[G * o + at : G * o + at + 16]
            out_ref[place + peer, 16:32] = zero
            out_ref[place + peer, 32:] = tail[o][at : at + 16]


def second_local_kernel(q_ref, w_ref, t_ref, u_ref, x_ref, v_ref, q1_ref, w1_ref, t1_ref, u1_ref, x1_ref, v1_ref,
                        lam1_ref, local_back_ref, inverse_ref, kind_ref,
                        forward_ref, backward_ref, end_ref, start_ref):
    faces = Faces()
    inverse = inverse_ref[...]
    kind = kind_ref[...]
    wall = kind == 2
    q = load_tiles(q_ref)
    q1 = load_tiles(q1_ref)
    t1 = t1_ref[...]
    x1 = x1_ref[...]
    jump = 0.5 * (faces.flux(t1, u1_ref[...]) - faces.flux(x1, v1_ref[...])) + (x1 - t1)
    faced = lifted(lift_factor * jump)
    inner = volume(q1, forward_ref[...])
    store_tiles(end_ref, [0.5 * q[j] + 0.5 * (q1[j] + step_size * (inner[j] + faced[j])) for j in range(3)])
    t = t_ref[...]
    lam1 = lam1_ref[...]
    u, x, v = u_ref[...], x_ref[...], v_ref[...]
    rest = lam1 - 0.5 * faces.rest_back(lam1)
    bar = jnp.where(kind == 1, 0.0, rest - 0.5 * faces.state_back(x, v, lam1))
    total = 0.5 * faces.state_back(t, u, lam1) - rest + jnp.where(wall, faces.mirror(bar), 0.0)
    total = total + select_rows(local_back_ref[...], take(bar, inverse))
    w = load_tiles(w_ref)
    w1 = load_tiles(w1_ref)
    inner = volume_back(q, derivative_back(w1, backward_ref[...]))
    faced = lifted(total)
    store_tiles(start_ref, [0.5 * w[j] + w1[j] + step_size * (inner[j] + faced[j]) for j in range(3)])


def last_kernel(end_base_ref, start_base_ref, arrived_ref, from_slots_ref, to_columns_ref, index_ref,
                end_ref, start_ref):
    faces = Faces()
    own, other = places()
    main = jnp.concatenate(
        [block_of(arrived_ref, 16, own), block_of(arrived_ref, 0, own), block_of(arrived_ref, 0, other)], axis=0)
    lane = lanes(G)
    zero = jnp.zeros((G, 128), bf16)
    shared = jnp.concatenate([
        jnp.where(lane < 32, block_of(arrived_ref, 32, own), zero),
        jnp.where((lane >= 32) & (lane < 64), block_of(arrived_ref, 32, own), zero),
        jnp.where((lane >= 64) & (lane < 96), block_of(arrived_ref, 32, other), zero)], axis=0)
    node = index_ref[...] & 15
    g = dot(from_slots_ref[...], main)
    b = dot(to_columns_ref[...], jnp.concatenate([main, shared], axis=1))
    lane = lanes()
    valid = mask(lane < 80)
    xr = valid * take(g, index_ref[...])
    ur = by_axis(lambda a, g, node: take(g, (a + 1) * 16 + node), g, node)
    pr = take(g, 64 + node)
    faced = lifted((0.5 * step_size * lift_factor) * (xr - 0.5 * faces.flux(xr, ur, pr)))
    base = load_tiles(end_base_ref)
    from_tiles([base[j] + faced[j] for j in range(3)], end_ref)
    high = turn(b[:, 128:], 48) + turn(b[:, 128:], 16) + turn(b[:, 128:], 112)
    bar = mask(lane < 48) * turn(b[:, :128], 48) + mask((lane >= 48) & (lane < 80)) * high
    faced = lifted(step_size * bar)
    base = load_tiles(start_base_ref)
    from_tiles([base[j] + faced[j] for j in range(3)], start_ref)


def shape(*dims, dtype=f32):
    return jax.ShapeDtypeStruct(dims, dtype)


def call(kernel, outs, *args, scratch=(), in_hbm=False):
    return pl.pallas_call(
        kernel,
        out_shape=outs,
        in_specs=[pl.BlockSpec(memory_space=pl.ANY if in_hbm else pltpu.VMEM)] * len(args),
        scratch_shapes=scratch,
        cost_estimate=pl.CostEstimate(flops=200_000_000, bytes_accessed=1_000_000, transcendentals=0),
        compiler_params=pltpu.CompilerParams(vmem_limit_bytes=32 * 1024 * 1024),
    )(*args)


def pair_peers(whole):
    count, peers = lax.axis_size("dom"), lax.axis_size("sub")
    groups = [[d % count * peers + peer for d in (first, first + 1) for peer in range(peers)]
              for first in range(1, count, 2)]
    return lax.all_to_all(
        whole, ("dom", "sub"), split_axis=0, concat_axis=0, tiled=True, axis_index_groups=groups)


def chip_partner(value):
    return lax.ppermute(value, "dom", [(d, d ^ 1) for d in range(lax.axis_size("dom"))])


def shards(state, adjoint_final, send_slot, ext_index, ext_perm):
    forward, backward = derivative_operands()
    forward, backward = jnp.asarray(forward), jnp.asarray(backward)
    state, adjoint_final = jnp.swapaxes(state, 1, 2), jnp.swapaxes(adjoint_final, 1, 2)
    node = shape(E, 384)
    face = shape(F, 128)
    index_face = shape(F, 128, dtype=i32)

    to_chip, out, q, w, t, lam, send_slots, back_slots, inverse, send_slot, ext_index, ext_perm = call(
        pack_kernel,
        (shape(8, 48, 128, dtype=bf16), shape(16, 96, 128, dtype=bf16), node, node, face, face,
         shape(S, F, dtype=bf16), shape(S, F, dtype=bf16), index_face,
         shape(1, S, dtype=i32), shape(6, E, dtype=i32), shape(6, E, dtype=i32)),
        *[pltpu.with_memory_space_constraint(x, pltpu.HBM) for x in (state, adjoint_final, send_slot, ext_index, ext_perm)], in_hbm=True,
        scratch=[pltpu.VMEM((5, E, 64), f32), pltpu.VMEM((5, E, 64), f32), pltpu.SemaphoreType.DMA((5,))])
    from_chip = chip_partner(to_chip)
    base, t_base, z, rest, u, x, v, from_slots, to_columns, local, local_back, index, kind = call(
        first_local_kernel,
        (node, face, shape(96, 384), face, face, face, face, shape(F, S, dtype=bf16), shape(F, S, dtype=bf16),
         shape(F, F, dtype=bf16), shape(F, F, dtype=bf16), index_face, index_face),
        q, w, t, lam, send_slot, ext_index, ext_perm, forward, backward)
    out = lax.dynamic_update_slice(out, from_chip, (0, 48, 0))
    out = lax.dynamic_update_slice(out, from_chip, (8, 48, 0))
    out, z = lax.optimization_barrier((out, z))
    arrived = pair_peers(out)
    to_chip, out, q1, w1, t1, u1, x1, v1, lam1 = call(
        middle_kernel, (shape(8, 32, 128, dtype=bf16), shape(16, 48, 128, dtype=bf16), node, node, face, face, face, face, face),
        base, t_base, w, lam, rest, z, arrived,
        from_slots, to_columns, local, local_back, send_slots, back_slots, index, inverse, kind)
    from_chip = chip_partner(to_chip)
    end_base, start_base = call(
        second_local_kernel, (node, node),
        q, w, t, u, x, v, q1, w1, t1, u1, x1, v1, lam1, local_back, inverse, kind, forward, backward)
    out = lax.dynamic_update_slice(out, out[:8, 16:] + from_chip, (0, 16, 0))
    out = lax.dynamic_update_slice(out, out[8:, 16:] + from_chip, (8, 16, 0))
    out, end_base = lax.optimization_barrier((out, end_base))
    arrived = pair_peers(out)
    out = shape(5, E, 64)
    end, start = call(
        last_kernel, (out, out),
        end_base, start_base, arrived, from_slots, to_columns, index)
    return jnp.swapaxes(end, 1, 2), jnp.swapaxes(start, 1, 2)


def solution(mesh):
    return jax.shard_map(
        shards,
        mesh=mesh,
        in_specs=(
            P(None, None, ("dom", "sub")),
            P(None, None, ("dom", "sub")),
            P(("dom", "sub"), None),
            P(None, ("dom", "sub")),
            P(None, ("dom", "sub")),
        ),
        out_specs=(P(None, None, ("dom", "sub")), P(None, None, ("dom", "sub"))),
        check_vma=False,
    )
```

```python
import jax
import jax.numpy as jnp
import numpy as np
import ml_dtypes
from jax import lax
from jax.experimental import pallas as pl
from jax.experimental.pallas import tpu as pltpu
from jax.sharding import PartitionSpec as P

step_size = 0.02
mean_flow = 0.3
lift_factor = 12.0

E = 32
F = 192
S = 384
G = 128
f32 = jnp.float32
bf16 = jnp.bfloat16
i32 = jnp.int32


def derivative_table():
    points = np.array([-1.0, -1.0 / np.sqrt(5.0), 1.0 / np.sqrt(5.0), 1.0])
    products = np.array(
        [np.prod([points[t] - points[s] for s in range(4) if s != t]) for t in range(4)]
    )
    result = np.zeros((4, 4))
    for t in range(4):
        for s in range(4):
            if t != s:
                result[t, s] = products[t] / (products[s] * (points[t] - points[s]))
        result[t, t] = -np.sum(result[t])
    return result.astype(np.float32)


def halves_of(matrix):
    hi = matrix.astype(ml_dtypes.bfloat16)
    lo = (matrix - hi.astype(np.float32)).astype(ml_dtypes.bfloat16)
    return hi, lo


def derivative_operands():
    d = -2.0 * derivative_table()
    eye = np.eye(4, dtype=np.float32)
    along = [
        np.kron(d, np.kron(eye, eye)),
        np.kron(eye, np.kron(d, eye)),
        np.kron(eye, np.kron(eye, d)),
    ]
    two = [np.kron(np.eye(2, dtype=np.float32), a).astype(np.float32) for a in along]
    hi, lo = halves_of(np.concatenate([t.T for t in two], axis=0))
    forward = np.concatenate([hi, lo], axis=1)
    hi, lo = halves_of(np.concatenate(two, axis=1))
    backward = np.concatenate([hi, lo], axis=1)
    return forward, backward


def lanes(rows=1):
    return lax.broadcasted_iota(i32, (rows, 128), 1)


def take(x, index):
    return jnp.take_along_axis(x, jnp.broadcast_to(index, x.shape), axis=1)


def mask(condition):
    return jnp.where(condition, 1.0, 0.0).astype(f32)


def turn(x, shift):
    return pltpu.roll(x, shift, 1)


def halves(x):
    hi = x.astype(bf16)
    lo = (x - hi.astype(f32)).astype(bf16)
    return hi, lo


def dot(a, b):
    return jnp.dot(a, b, preferred_element_type=f32)


def select_rows(onehot, x):
    hi, lo = halves(x)
    r = dot(onehot, jnp.concatenate([hi, lo], axis=1))
    return r[:, :128] + r[:, 128:]


def to_tiles(ref):
    zero = jnp.zeros((E, 64), f32)
    tiles = []
    for j in range(3):
        high = ref[2 * j + 1] if j < 2 else zero
        tiles.append(jnp.concatenate([ref[2 * j], high], axis=1))
    return tiles


def from_tiles(tiles, ref):
    for j in range(3):
        ref[2 * j] = tiles[j][:, :64]
        if j < 2:
            ref[2 * j + 1] = tiles[j][:, 64:]


def load_tiles(ref):
    return [ref[:, 128 * j : 128 * (j + 1)] for j in range(3)]


def store_tiles(ref, tiles):
    for j in range(3):
        ref[:, 128 * j : 128 * (j + 1)] = tiles[j]


def spread(tiles):
    low = lanes(E) < 64
    back0, back1, back2 = turn(tiles[0], 64), turn(tiles[1], 64), turn(tiles[2], 64)
    ux = jnp.where(low, back0, tiles[0])
    uy = jnp.where(low, tiles[1], back1)
    uz = jnp.where(low, back1, tiles[1])
    p = tiles[2] + back2
    return low, (ux, uy, uz), p


def volume(tiles, table):
    low, speeds, p = spread(tiles)
    fluxes = []
    for a in range(3):
        u = speeds[a]
        c = u + mean_flow if a == 0 else u
        high0 = p if a == 0 else jnp.zeros_like(p)
        parts = [c * tiles[0] + jnp.where(low, u, high0), c * tiles[1], c * tiles[2] + jnp.where(low, u, 0.0)]
        if a == 1:
            parts[1] = parts[1] + jnp.where(low, p, 0.0)
        if a == 2:
            parts[1] = parts[1] + jnp.where(low, 0.0, p)
        fluxes.append(jnp.concatenate(parts, axis=0))
    hi, lo = halves(jnp.concatenate(fluxes, axis=1))
    r = dot(jnp.concatenate([hi, lo], axis=0), table)
    out = r[:96, :128] + (r[:96, 128:] + r[96:, :128])
    return [out[:32], out[32:64], out[64:96]]


def derivative_back(tiles, table):
    hi, lo = halves(jnp.concatenate(tiles, axis=0))
    r = dot(jnp.concatenate([hi, lo], axis=0), table)
    return r[:96, :384] + (r[:96, 384:] + r[96:, :384])


def volume_back(tiles, z):
    low, speeds, _ = spread(tiles)
    one = jnp.where(low, 1.0, 0.0).astype(f32)
    plus = [tiles[0] + one, tiles[1], tiles[2] + one]
    out = [jnp.zeros((E, 128), f32) for _ in range(3)]
    sums = []
    parts = []
    for a in range(3):
        c = speeds[a] + mean_flow if a == 0 else speeds[a]
        za = [z[32 * j : 32 * (j + 1), 128 * a : 128 * (a + 1)] for j in range(3)]
        total = plus[0] * za[0] + plus[1] * za[1] + plus[2] * za[2]
        sums.append(total + turn(total, 64))
        parts.append(za)
        out = [out[j] + c * za[j] for j in range(3)]
    pressure = turn(parts[0][0], 64) + parts[1][1] + turn(parts[2][1], 64)
    out[0] = out[0] + jnp.where(low, 0.0, sums[0])
    out[1] = out[1] + jnp.where(low, sums[1], sums[2])
    out[2] = out[2] + jnp.where(low, pressure, 0.0)
    return out


def traces(tiles):
    lane = lanes()
    wide = lanes(E)
    m = lane & 15
    r, s = m >> 2, m & 3
    base = ((lane >> 4) & 1) * 64
    rows = []
    for f in range(6):
        b = f % 2
        index = base + (48 * b + m, 16 * r + 12 * b + s, 4 * m + 3 * b)[f // 2]
        index = jnp.where(lane < 80, index, 64)
        t = jnp.where(
            wide < 32,
            take(tiles[0], index),
            jnp.where(wide < 64, take(tiles[1], index), take(tiles[2], index)),
        )
        rows.append(t)
    return jnp.concatenate(rows, axis=0)


def lifted(x):
    lane = lanes()
    wide = lanes(E)
    n = lane & 63
    i, j, k = n >> 4, (n >> 2) & 3, n & 3
    places = (4 * j + k, 4 * i + k, 4 * i + j)
    layers = (i, j, k)
    wide_layers = ((wide >> 4) & 3, (wide >> 2) & 3, wide & 3)
    tiles = [None] * 3
    for a in range(3):
        first, last = x[64 * a : 64 * a + 32], turn(x[64 * a + 32 : 64 * a + 64], 64)
        pair = jnp.where(wide < 64, first, last)
        tail = jnp.where(wide < 16, last, first)
        ends = (wide_layers[a] == 0) | (wide_layers[a] == 3)
        for tile in range(3):
            v = 2 * tile + (lane >> 6)
            index = v * 16 + places[a]
            at_last = jnp.where(layers[a] == 3, 64, 0)
            if tile < 2:
                part = take(pair, index + at_last)
            else:
                part = take(tail, jnp.where(lane < 64, index - at_last, 80))
            part = jnp.where(ends, part, 0.0)
            tiles[tile] = part if tiles[tile] is None else tiles[tile] + part
    return tiles


def lifted_traces(x):
    lane = lanes()
    wide = lanes(E)
    v16 = lane & 112
    r, s = (lane >> 2) & 3, lane & 3
    wide_r, wide_s = (wide >> 2) & 3, wide & 3
    rows = []
    for f in range(6):
        a, b = f // 2, f % 2
        total = x[32 * f : 32 * (f + 1)]
        for place, side in ((0, wide_r), (1, wide_s)):
            axis = [other for other in range(3) if other != a][place]
            free = (s, r)[place]
            node = 12 * b + free if a < [o for o in range(3) if o != axis and o != a][0] else 4 * free + 3 * b
            index = v16 + node
            first = take(x[64 * axis : 64 * axis + 32], index)
            last = take(x[64 * axis + 32 : 64 * axis + 64], index)
            total = total + jnp.where(side == 0, first, jnp.where(side == 3, last, 0.0))
        rows.append(total)
    return jnp.concatenate(rows, axis=0)


def by_axis(function, *arrays):
    return jnp.concatenate(
        [function(a, *[x[64 * a : 64 * (a + 1)] for x in arrays]) for a in range(3)], axis=0)


def signed(x):
    return jnp.concatenate([-x[:32], x[32:]], axis=0)


class Faces:
    def __init__(self):
        lane = lanes()
        self.v = lane >> 4
        self.m = lane & 15
        self.ends = mask((self.v == 0) | (self.v == 4))
        self.last = mask(self.v == 4)
        self.normal = [mask(self.v == a + 1) for a in range(3)]
        self.normal_index = [(a + 1) * 16 + self.m for a in range(3)]
        self.pressure_index = 64 + self.m

    def normal_of(self, x):
        return by_axis(lambda a, x: take(x, self.normal_index[a]), x)

    def pressure_of(self, x):
        return take(x, self.pressure_index)

    def flux(self, x, u=None, p=None):
        u = self.normal_of(x) if u is None else u
        p = self.pressure_of(x) if p is None else p

        def along(a, x, u, p):
            c = u + mean_flow if a == 0 else u
            return signed(c * x + self.ends * u + self.normal[a] * p)

        return by_axis(along, x, u, p)

    def flux_back(self, x, u, w):
        def along(a, x, u, w, h):
            n = take(w, self.normal_index[a])
            c = u + mean_flow if a == 0 else u
            return signed(c * w + self.last * n + self.normal[a] * h)

        return by_axis(along, x, u, w, over_fields((x + self.ends) * w))

    def rest_back(self, w):
        def along(a, w, h):
            n = take(w, self.normal_index[a])
            part = self.last * n + self.normal[a] * h
            return signed(mean_flow * w + part if a == 0 else part)

        return by_axis(along, w, over_fields(self.ends * w))

    def state_back(self, x, u, w):
        def along(a, u, w, h):
            return signed(u * w + self.normal[a] * h)

        return by_axis(along, u, w, over_fields(x * w))

    def shifted(self, d):
        target = self.v + d
        target = jnp.where(target >= 5, target - 5, target)
        return target, jnp.where(self.v < 5, target * 16 + self.m, 16 * self.v + self.m)

    def hessian(self, d, y):
        target, index = self.shifted(d)

        def along(a, y):
            back = mask((self.v < 5) & (target == a + 1))
            return signed(-0.5 * (self.normal[a] * take(y, index) + back * y))

        return by_axis(along, y)

    def mirror(self, x):
        return by_axis(lambda a, x: x * (1.0 - 2.0 * self.normal[a]), x)


def over_fields(h):
    table = ((lax.broadcasted_iota(i32, (128, 128), 0) ^ lax.broadcasted_iota(i32, (128, 128), 1)) & 15) == 0
    table = mask(table).astype(bf16)
    hi, lo = halves(h)
    return dot(jnp.concatenate([hi, lo], axis=1), jnp.concatenate([table, table], axis=0))


def column_of(table_ref):
    x = table_ref[...].astype(f32)
    x = jnp.concatenate([x, jnp.zeros((2, E), f32)], axis=0)
    t = jnp.transpose(x)
    return jnp.concatenate([t[:, f : f + 1] for f in range(6)], axis=0).astype(i32)


def row_of(table_ref):
    return jnp.concatenate([table_ref[f : f + 1, :] for f in range(6)], axis=1)


def slot_column(send):
    x = jnp.broadcast_to(send.astype(f32), (8, S))
    return jnp.transpose(x)[:, :1].astype(i32)


def onehot(rows, columns, first, second):
    return jnp.where(first == second, 1.0, 0.0).astype(bf16)


def faces_from_columns(ext_col):
    return onehot(F, F, ext_col, lax.broadcasted_iota(i32, (F, F), 1))


def columns_from_faces(ext_row):
    return onehot(F, F, ext_row, lax.broadcasted_iota(i32, (F, F), 0))


def faces_from_slots(ext_col):
    return onehot(F, S, ext_col - F, lax.broadcasted_iota(i32, (F, S), 1))


def slots_from_faces(ext_row):
    return onehot(S, F, ext_row - F, lax.broadcasted_iota(i32, (S, F), 0))


def slots_from_columns(send_col):
    return onehot(S, F, send_col, lax.broadcasted_iota(i32, (S, F), 1))


def columns_from_slots(send_row):
    return onehot(F, S, send_row, lax.broadcasted_iota(i32, (F, S), 0))


def orientation(perm_col):
    lane = lanes(F)
    m = lane & 15
    crossed = lane - m + ((m & 3) * 4 + (m >> 2))
    k = jnp.broadcast_to(perm_col, (F, 128))
    flips = (k & 1) * 12 + ((k & 2) >> 1) * 3
    crossed_flips = (k & 1) * 3 + ((k & 2) >> 1) * 12
    swap = (k & 4) == 4
    place = jnp.where(swap, crossed, lane)
    return place ^ jnp.where(swap, crossed_flips, flips), place ^ flips


def peer_tables(send_ref, ext_ref):
    odd = (lax.axis_index("dom") & 1) == 1
    send = send_ref[...]
    swapped = jnp.concatenate([send[:, 2 * G :], send[:, G : 2 * G], send[:, :G]], axis=1)
    send = jnp.where(odd, send, swapped)

    def reordered(table):
        slot = table - F
        turned = jnp.where(slot < G, slot + 2 * G, jnp.where(slot >= 2 * G, slot - 2 * G, slot))
        turned = jnp.where((slot >= 0) & (slot < S), turned + F, table)
        return jnp.where(odd, turned, table)

    return send, reordered(column_of(ext_ref)), reordered(row_of(ext_ref))


def packed(x):
    lane = lanes(F)
    first = jnp.where(lane >= 64, turn(x, 64), 0.0)
    second = jnp.where((lane >= 80) & (lane < 96), turn(x, 16), 0.0)
    return jnp.concatenate([first, second], axis=1).astype(bf16)


def exterior(faces, wall, index, onehot_local, t, u):
    g = select_rows(onehot_local, t)
    node = index & 15
    x = jnp.where(wall, faces.mirror(t), take(g, index))
    v = by_axis(lambda a, g, node: take(g, (a + 1) * 16 + node), g, node)
    return x, jnp.where(wall, -u, v)


def folded(x):
    y = x.reshape(8, 16, 128)
    return (y[:, :8].reshape(64, 128) + turn(y[:, 8:].reshape(64, 128), 64)).reshape(8, 8, 128)


def unfolded(z):
    z = z.reshape(64, 128)
    low = mask(lanes() < 64)
    halves = [(low * part).reshape(8, 8, 128) for part in (z, turn(z, 64))]
    return jnp.concatenate(halves, axis=1).reshape(G, 128)


def places():
    own = jnp.where((lax.axis_index("dom") & 1) == 1, 0, 8)
    return own, 8 - own


def pack_kernel(state_hbm, final_hbm, send_hbm, ext_hbm, perm_hbm,
                chip_ref, out_ref, q_ref, w_ref, t_ref, lam_ref, send_slots_ref, back_slots_ref, inverse_ref,
                send_ref, ext_ref, perm_ref, state_ref, final_ref, sems):
    pairs = ((send_hbm, send_ref), (ext_hbm, ext_ref), (perm_hbm, perm_ref), (final_hbm, final_ref), (state_hbm, state_ref))
    copies = [pltpu.make_async_copy(a, b, sems.at[i]) for i, (a, b) in enumerate(pairs)]
    for copy in copies:
        copy.start()
    faces = Faces()
    for copy in copies[:3]:
        copy.wait()
    send, _, ext_row = peer_tables(send_ref, ext_ref)
    send_slots = slots_from_columns(slot_column(send))
    back_slots = slots_from_faces(ext_row)
    send_slots_ref[...] = send_slots
    back_slots_ref[...] = back_slots
    _, inverse = orientation(column_of(perm_ref))
    inverse_ref[...] = inverse
    for copy in copies[3:]:
        copy.wait()
    q = to_tiles(state_ref)
    w = to_tiles(final_ref)
    store_tiles(q_ref, q)
    store_tiles(w_ref, w)
    t = traces(q)
    lam = lift_factor * traces(w)
    t_ref[...] = t
    lam_ref[...] = lam
    y = take(lam, inverse)
    diagonal = by_axis(lambda a, y: signed(-faces.normal[a] * y), y)
    first = y - 0.5 * faces.rest_back(y) + turn(diagonal, 64)
    stack = jnp.concatenate([x.astype(bf16) for x in (first, faces.hessian(1, y), faces.hessian(2, y))], axis=1)
    back = dot(back_slots, stack)
    forward = dot(send_slots, packed(t))
    parts = [back[:, :128], back[:, 128:256] + forward[:, :128], back[:, 256:] + forward[:, 128:]]
    own, other = places()
    lane = lanes()
    guest = mask(lane >= 96) * turn(parts[2][:G], 32)
    rest = folded(mask(lane < 64) * parts[2][:G])
    for peer in range(8):
        at = 16 * peer
        chip_ref[peer] = jnp.concatenate(
            [guest[at : at + 16], parts[0][at : at + 16], parts[1][at : at + 16], rest[peer]], axis=0).astype(bf16)
        for o, place in ((1, own), (2, other)):
            at = G * o + 16 * peer
            for j in range(3):
                out_ref[place + peer, 16 * j : 16 * (j + 1)] = parts[j][at : at + 16].astype(bf16)


def first_local_kernel(q_ref, w_ref, t_ref, lam_ref, send_ref, ext_ref, perm_ref, forward_ref, backward_ref,
                       base_ref, t_base_ref, z_ref, rest_ref, u_ref, x_ref, v_ref,
                       from_slots_ref, to_columns_ref, local_ref, local_back_ref, index_ref, kind_ref):
    faces = Faces()
    send, ext_col, ext_row = peer_tables(send_ref, ext_ref)
    index, _ = orientation(column_of(perm_ref))
    index_ref[...] = index
    ext_wide = jnp.broadcast_to(ext_col, (F, 128))
    wall = ext_wide == F + S
    kind_ref[...] = jnp.where(wall, 2, jnp.where(ext_wide >= F, 1, 0))
    from_slots_ref[...] = faces_from_slots(ext_col)
    to_columns_ref[...] = columns_from_slots(send)
    local = faces_from_columns(ext_col)
    local_ref[...] = local
    local_back_ref[...] = columns_from_faces(ext_row)
    q = load_tiles(q_ref)
    t = t_ref[...]
    lam = lam_ref[...]
    rest_ref[...] = lam - 0.5 * faces.rest_back(lam)
    u = faces.normal_of(t)
    x, v = exterior(faces, wall, index, local, t, u)
    u_ref[...] = u
    x_ref[...] = x
    v_ref[...] = v
    jump = 0.5 * (faces.flux(t, u) - faces.flux(x, v)) + (x - t)
    faced = lifted(lift_factor * jump)
    inner = volume(q, forward_ref[...])
    base = [q[j] + step_size * (inner[j] + faced[j]) for j in range(3)]
    store_tiles(base_ref, base)
    t_base_ref[...] = traces(base)
    z_ref[...] = derivative_back(load_tiles(w_ref), backward_ref[...])


def middle_kernel(base_ref, t_base_ref, w_ref, lam_ref, rest_ref, z_ref, arrived_ref,
                  from_slots_ref, to_columns_ref, local_ref, local_back_ref, send_slots_ref, back_slots_ref,
                  index_ref, inverse_ref, kind_ref,
                  chip_ref, out_ref, q1_ref, w1_ref, t1_ref, u1_ref, x1_ref, v1_ref, lam1_ref):
    faces = Faces()
    index = index_ref[...]
    inverse = inverse_ref[...]
    kind = kind_ref[...]
    wall = kind == 2
    wide = lanes(F)
    lane = lanes()
    node = index & 15
    own, other = places()
    mine, theirs = arrived_ref[pl.ds(own, 8)], arrived_ref[pl.ds(other, 8)]
    third = mine[:, 32:48].reshape(G, 128)
    guest = mask((lane >= 64) & (lane < 96)) * turn(third.astype(f32), 96)
    rest = unfolded(mine[:, 80:].astype(f32))
    kept = lanes(G) < 96
    zero = jnp.zeros((G, 128), bf16)
    third = jnp.concatenate(
        [jnp.where(kept, third, zero), jnp.where(kept, theirs[:, 32:48].reshape(G, 128), zero)], axis=0)
    tiles = [jnp.concatenate([x.reshape(G, 128) for x in blocks], axis=0) for blocks in (
        (mine[:, 48:64], mine[:, :16], theirs[:, :16]), (mine[:, 64:80], mine[:, 16:32], theirs[:, 16:32]))]
    g = dot(from_slots_ref[...], jnp.concatenate(
        [tiles[1], jnp.concatenate([guest.astype(bf16), third], axis=0)], axis=1))
    sums = dot(to_columns_ref[...], jnp.concatenate(
        tiles + [jnp.concatenate([(guest + rest).astype(bf16), third], axis=0)], axis=1))
    g0, g1 = g[:, :128], g[:, 128:]
    place = jnp.where(wide < 64, index + 64, jnp.where(wide < 80, index + 16, 96 + node))
    xr = jnp.where(wide < 64, take(g0, place), take(g1, place))
    ur = by_axis(lambda a, g, node: take(g, 80 + 16 * a + node), g0, node)
    pr = take(g1, 80 + node)
    jump = (lift_factor * step_size) * (xr - 0.5 * faces.flux(xr, ur, pr))
    t1 = t_base_ref[...] + lifted_traces(jump)
    faced = lifted(jump)
    base = load_tiles(base_ref)
    q1 = [base[j] + faced[j] for j in range(3)]
    store_tiles(q1_ref, q1)
    t1_ref[...] = t1
    t1_sent = t1.astype(bf16)
    forward = dot(send_slots_ref[...], t1_sent)
    lam = lam_ref[...]
    rest = rest_ref[...]
    u1 = faces.normal_of(t1)
    u1_ref[...] = u1
    x1, v1 = exterior(faces, wall, index, local_ref[...], t1, u1)
    x1_ref[...] = x1
    v1_ref[...] = v1
    bar = jnp.where(kind == 1, 0.0, rest - 0.5 * faces.state_back(x1, v1, lam))
    total = 0.5 * faces.state_back(t1, u1, lam) - rest + jnp.where(wall, faces.mirror(bar), 0.0)
    total = total + select_rows(local_back_ref[...], take(bar, inverse))
    sent = t1_sent.astype(f32)
    h0, h1, h2 = sums[:, :128], mask(lane < 64) * sums[:, 128:256], sums[:, 256:]
    ahead1, ahead2, behind2, behind1 = [faces.shifted(d)[1] for d in (1, 2, 3, 4)]
    through = h0 + h1 * take(sent, ahead1) + h2 * take(sent, ahead2)
    through = through + take(h1 * sent, behind1) + take(h2 * sent, behind2)
    through = through + mask((lane >= 16) & (lane < 64)) * turn(h0, 64) * sent
    total = total + mask(lane < 80) * through
    inner = volume_back(q1, z_ref[...])
    w = load_tiles(w_ref)
    half = [0.5 * w[j] + (0.5 * step_size) * inner[j] for j in range(3)]
    lam1 = lift_factor * traces(half) + (0.5 * step_size * lift_factor) * lifted_traces(total)
    faced = lifted(total)
    store_tiles(w1_ref, [half[j] + (0.5 * step_size) * faced[j] for j in range(3)])
    lam1_ref[...] = lam1
    bar = lam1 - 0.5 * faces.flux_back(xr, ur, lam1)
    first = take(bar, jnp.where(wide >= 80, inverse - 80, 80))
    second = take(bar, jnp.where(wide < 32, inverse + 48, 80))
    back = dot(back_slots_ref[...], jnp.concatenate([first, second], axis=1).astype(bf16))
    main = back[:, :128] + forward
    tail = [folded(back[:G, 128:])] + [folded(turn(back[G * o : G * (o + 1), 128:], 32)) for o in (1, 2)]
    zero = jnp.zeros((16, 128), f32)
    for peer in range(8):
        at = 16 * peer
        chip_ref[peer] = jnp.concatenate([main[at : at + 16], tail[0][peer]], axis=0).astype(bf16)
        for o, place in ((1, own), (2, other)):
            at = G * o + 16 * peer
            out_ref[place + peer] = jnp.concatenate([main[at : at + 16], zero, tail[o][peer]], axis=0).astype(bf16)


def second_local_kernel(q_ref, w_ref, t_ref, u_ref, x_ref, v_ref, q1_ref, w1_ref, t1_ref, u1_ref, x1_ref, v1_ref,
                        lam1_ref, local_back_ref, inverse_ref, kind_ref,
                        forward_ref, backward_ref, end_ref, start_ref):
    faces = Faces()
    inverse = inverse_ref[...]
    kind = kind_ref[...]
    wall = kind == 2
    q = load_tiles(q_ref)
    q1 = load_tiles(q1_ref)
    t1 = t1_ref[...]
    x1 = x1_ref[...]
    jump = 0.5 * (faces.flux(t1, u1_ref[...]) - faces.flux(x1, v1_ref[...])) + (x1 - t1)
    faced = lifted(lift_factor * jump)
    inner = volume(q1, forward_ref[...])
    store_tiles(end_ref, [0.5 * q[j] + 0.5 * (q1[j] + step_size * (inner[j] + faced[j])) for j in range(3)])
    t = t_ref[...]
    lam1 = lam1_ref[...]
    u, x, v = u_ref[...], x_ref[...], v_ref[...]
    rest = lam1 - 0.5 * faces.rest_back(lam1)
    bar = jnp.where(kind == 1, 0.0, rest - 0.5 * faces.state_back(x, v, lam1))
    total = 0.5 * faces.state_back(t, u, lam1) - rest + jnp.where(wall, faces.mirror(bar), 0.0)
    total = total + select_rows(local_back_ref[...], take(bar, inverse))
    w = load_tiles(w_ref)
    w1 = load_tiles(w1_ref)
    inner = volume_back(q, derivative_back(w1, backward_ref[...]))
    faced = lifted(total)
    store_tiles(start_ref, [0.5 * w[j] + w1[j] + step_size * (inner[j] + faced[j]) for j in range(3)])


def last_kernel(end_base_ref, start_base_ref, arrived_ref, from_slots_ref, to_columns_ref, index_ref,
                end_ref, start_ref):
    faces = Faces()
    own, other = places()
    mine, theirs = arrived_ref[pl.ds(own, 8)], arrived_ref[pl.ds(other, 8)]
    main = jnp.concatenate(
        [mine[:, 16:32].reshape(G, 128), mine[:, :16].reshape(G, 128), theirs[:, :16].reshape(G, 128)], axis=0)
    lane = lanes()
    tail, next_tail = unfolded(mine[:, 32:].astype(f32)), unfolded(theirs[:, 32:].astype(f32))
    late = mask(lane >= 32)
    shared = jnp.concatenate([mask(lane < 32) * tail, late * tail, late * next_tail], axis=0).astype(bf16)
    node = index_ref[...] & 15
    g = dot(from_slots_ref[...], main)
    b = dot(to_columns_ref[...], jnp.concatenate([main, shared], axis=1))
    lane = lanes()
    valid = mask(lane < 80)
    xr = valid * take(g, index_ref[...])
    ur = by_axis(lambda a, g, node: take(g, (a + 1) * 16 + node), g, node)
    pr = take(g, 64 + node)
    faced = lifted((0.5 * step_size * lift_factor) * (xr - 0.5 * faces.flux(xr, ur, pr)))
    base = load_tiles(end_base_ref)
    from_tiles([base[j] + faced[j] for j in range(3)], end_ref)
    high = turn(b[:, 128:], 48) + turn(b[:, 128:], 16)
    bar = mask(lane < 48) * turn(b[:, :128], 48) + mask((lane >= 48) & (lane < 80)) * high
    faced = lifted(step_size * bar)
    base = load_tiles(start_base_ref)
    from_tiles([base[j] + faced[j] for j in range(3)], start_ref)


def shape(*dims, dtype=f32):
    return jax.ShapeDtypeStruct(dims, dtype)


def call(kernel, outs, *args, scratch=(), in_hbm=False):
    return pl.pallas_call(
        kernel,
        out_shape=outs,
        in_specs=[pl.BlockSpec(memory_space=pl.ANY if in_hbm else pltpu.VMEM)] * len(args),
        scratch_shapes=scratch,
        cost_estimate=pl.CostEstimate(flops=200_000_000, bytes_accessed=1_000_000, transcendentals=0),
        compiler_params=pltpu.CompilerParams(vmem_limit_bytes=32 * 1024 * 1024),
    )(*args)


def pair_peers(whole):
    count, peers = lax.axis_size("dom"), lax.axis_size("sub")
    groups = [[d % count * peers + peer for d in (first, first + 1) for peer in range(peers)]
              for first in range(1, count, 2)]
    return lax.all_to_all(
        whole, ("dom", "sub"), split_axis=0, concat_axis=0, tiled=True, axis_index_groups=groups)


def chip_partner(value):
    return lax.ppermute(value, "dom", [(d, d ^ 1) for d in range(lax.axis_size("dom"))])


def shards(state, adjoint_final, send_slot, ext_index, ext_perm):
    forward, backward = derivative_operands()
    forward, backward = jnp.asarray(forward), jnp.asarray(backward)
    state, adjoint_final = jnp.swapaxes(state, 1, 2), jnp.swapaxes(adjoint_final, 1, 2)
    node = shape(E, 384)
    face = shape(F, 128)
    index_face = shape(F, 128, dtype=i32)

    to_chip, out, q, w, t, lam, send_slots, back_slots, inverse, send_slot, ext_index, ext_perm = call(
        pack_kernel,
        (shape(8, 56, 128, dtype=bf16), shape(16, 88, 128, dtype=bf16), node, node, face, face,
         shape(S, F, dtype=bf16), shape(S, F, dtype=bf16), index_face,
         shape(1, S, dtype=i32), shape(6, E, dtype=i32), shape(6, E, dtype=i32)),
        *[pltpu.with_memory_space_constraint(x, pltpu.HBM) for x in (state, adjoint_final, send_slot, ext_index, ext_perm)], in_hbm=True,
        scratch=[pltpu.VMEM((5, E, 64), f32), pltpu.VMEM((5, E, 64), f32), pltpu.SemaphoreType.DMA((5,))])
    from_chip = chip_partner(to_chip)
    base, t_base, z, rest, u, x, v, from_slots, to_columns, local, local_back, index, kind = call(
        first_local_kernel,
        (node, face, shape(96, 384), face, face, face, face, shape(F, S, dtype=bf16), shape(F, S, dtype=bf16),
         shape(F, F, dtype=bf16), shape(F, F, dtype=bf16), index_face, index_face),
        q, w, t, lam, send_slot, ext_index, ext_perm, forward, backward)
    for start in (0, 8):
        out = lax.dynamic_update_slice(out, from_chip[:, 16:], (start, 48, 0))
        out = lax.dynamic_update_slice(out, out[start : start + 8, 32:48] + from_chip[:, :16], (start, 32, 0))
    out, z = lax.optimization_barrier((out, z))
    arrived = pair_peers(out)
    to_chip, out, q1, w1, t1, u1, x1, v1, lam1 = call(
        middle_kernel, (shape(8, 24, 128, dtype=bf16), shape(16, 40, 128, dtype=bf16), node, node, face, face, face, face, face),
        base, t_base, w, lam, rest, z, arrived,
        from_slots, to_columns, local, local_back, send_slots, back_slots, index, inverse, kind)
    from_chip = chip_partner(to_chip)
    end_base, start_base = call(
        second_local_kernel, (node, node),
        q, w, t, u, x, v, q1, w1, t1, u1, x1, v1, lam1, local_back, inverse, kind, forward, backward)
    out = lax.dynamic_update_slice(out, out[:8, 16:] + from_chip, (0, 16, 0))
    out = lax.dynamic_update_slice(out, out[8:, 16:] + from_chip, (8, 16, 0))
    out, end_base = lax.optimization_barrier((out, end_base))
    arrived = pair_peers(out)
    out = shape(5, E, 64)
    end, start = call(
        last_kernel, (out, out),
        end_base, start_base, arrived, from_slots, to_columns, index)
    return jnp.swapaxes(end, 1, 2), jnp.swapaxes(start, 1, 2)


def solution(mesh):
    return jax.shard_map(
        shards,
        mesh=mesh,
        in_specs=(
            P(None, None, ("dom", "sub")),
            P(None, None, ("dom", "sub")),
            P(("dom", "sub"), None),
            P(None, ("dom", "sub")),
            P(None, ("dom", "sub")),
        ),
        out_specs=(P(None, None, ("dom", "sub")), P(None, None, ("dom", "sub"))),
        check_vma=False,
    )
```

```python
import jax
import jax.numpy as jnp
import numpy as np
import ml_dtypes
from jax import lax
from jax.experimental import pallas as pl
from jax.experimental.pallas import tpu as pltpu
from jax.sharding import PartitionSpec as P

step_size = 0.02
mean_flow = 0.3
lift_factor = 12.0

E = 32
F = 192
S = 384
G = 128
f32 = jnp.float32
bf16 = jnp.bfloat16
i32 = jnp.int32


def derivative_table():
    points = np.array([-1.0, -1.0 / np.sqrt(5.0), 1.0 / np.sqrt(5.0), 1.0])
    products = np.array(
        [np.prod([points[t] - points[s] for s in range(4) if s != t]) for t in range(4)]
    )
    result = np.zeros((4, 4))
    for t in range(4):
        for s in range(4):
            if t != s:
                result[t, s] = products[t] / (products[s] * (points[t] - points[s]))
        result[t, t] = -np.sum(result[t])
    return result.astype(np.float32)


def halves_of(matrix):
    hi = matrix.astype(ml_dtypes.bfloat16)
    lo = (matrix - hi.astype(np.float32)).astype(ml_dtypes.bfloat16)
    return hi, lo


def derivative_operands():
    d = -2.0 * derivative_table()
    eye = np.eye(4, dtype=np.float32)
    along = [
        np.kron(d, np.kron(eye, eye)),
        np.kron(eye, np.kron(d, eye)),
        np.kron(eye, np.kron(eye, d)),
    ]
    two = [np.kron(np.eye(2, dtype=np.float32), a).astype(np.float32) for a in along]
    hi, lo = halves_of(np.concatenate([t.T for t in two], axis=0))
    forward = np.concatenate([hi, lo], axis=1)
    hi, lo = halves_of(np.concatenate(two, axis=1))
    backward = np.concatenate([hi, lo], axis=1)
    return forward, backward


def lanes(rows=1):
    return lax.broadcasted_iota(i32, (rows, 128), 1)


def take(x, index):
    return jnp.take_along_axis(x, jnp.broadcast_to(index, x.shape), axis=1)


def mask(condition):
    return jnp.where(condition, 1.0, 0.0).astype(f32)


def turn(x, shift):
    return pltpu.roll(x, shift, 1)


def halves(x):
    hi = x.astype(bf16)
    lo = (x - hi.astype(f32)).astype(bf16)
    return hi, lo


def dot(a, b):
    return jnp.dot(a, b, preferred_element_type=f32)


def select_rows(onehot, x):
    hi, lo = halves(x)
    r = dot(onehot, jnp.concatenate([hi, lo], axis=1))
    return r[:, :128] + r[:, 128:]


def to_tiles(ref):
    zero = jnp.zeros((E, 64), f32)
    tiles = []
    for j in range(3):
        high = ref[2 * j + 1] if j < 2 else zero
        tiles.append(jnp.concatenate([ref[2 * j], high], axis=1))
    return tiles


def from_tiles(tiles, ref):
    for j in range(3):
        ref[2 * j] = tiles[j][:, :64]
        if j < 2:
            ref[2 * j + 1] = tiles[j][:, 64:]


def load_tiles(ref):
    return [ref[:, 128 * j : 128 * (j + 1)] for j in range(3)]


def store_tiles(ref, tiles):
    for j in range(3):
        ref[:, 128 * j : 128 * (j + 1)] = tiles[j]


def spread(tiles):
    low = lanes(E) < 64
    back0, back1, back2 = turn(tiles[0], 64), turn(tiles[1], 64), turn(tiles[2], 64)
    ux = jnp.where(low, back0, tiles[0])
    uy = jnp.where(low, tiles[1], back1)
    uz = jnp.where(low, back1, tiles[1])
    p = tiles[2] + back2
    return low, (ux, uy, uz), p


def volume(tiles, table):
    low, speeds, p = spread(tiles)
    fluxes = []
    for a in range(3):
        u = speeds[a]
        c = u + mean_flow if a == 0 else u
        high0 = p if a == 0 else jnp.zeros_like(p)
        parts = [c * tiles[0] + jnp.where(low, u, high0), c * tiles[1], c * tiles[2] + jnp.where(low, u, 0.0)]
        if a == 1:
            parts[1] = parts[1] + jnp.where(low, p, 0.0)
        if a == 2:
            parts[1] = parts[1] + jnp.where(low, 0.0, p)
        fluxes.append(jnp.concatenate(parts, axis=0))
    hi, lo = halves(jnp.concatenate(fluxes, axis=1))
    r = dot(jnp.concatenate([hi, lo], axis=0), table)
    out = r[:96, :128] + (r[:96, 128:] + r[96:, :128])
    return [out[:32], out[32:64], out[64:96]]


def derivative_back(tiles, table):
    hi, lo = halves(jnp.concatenate(tiles, axis=0))
    r = dot(jnp.concatenate([hi, lo], axis=0), table)
    return r[:96, :384] + (r[:96, 384:] + r[96:, :384])


def volume_back(tiles, z):
    low, speeds, _ = spread(tiles)
    one = jnp.where(low, 1.0, 0.0).astype(f32)
    plus = [tiles[0] + one, tiles[1], tiles[2] + one]
    out = [jnp.zeros((E, 128), f32) for _ in range(3)]
    sums = []
    parts = []
    for a in range(3):
        c = speeds[a] + mean_flow if a == 0 else speeds[a]
        za = [z[32 * j : 32 * (j + 1), 128 * a : 128 * (a + 1)] for j in range(3)]
        total = plus[0] * za[0] + plus[1] * za[1] + plus[2] * za[2]
        sums.append(total + turn(total, 64))
        parts.append(za)
        out = [out[j] + c * za[j] for j in range(3)]
    pressure = turn(parts[0][0], 64) + parts[1][1] + turn(parts[2][1], 64)
    out[0] = out[0] + jnp.where(low, 0.0, sums[0])
    out[1] = out[1] + jnp.where(low, sums[1], sums[2])
    out[2] = out[2] + jnp.where(low, pressure, 0.0)
    return out


def traces(tiles):
    lane = lanes()
    wide = lanes(E)
    m = lane & 15
    r, s = m >> 2, m & 3
    base = ((lane >> 4) & 1) * 64
    rows = []
    for f in range(6):
        b = f % 2
        index = base + (48 * b + m, 16 * r + 12 * b + s, 4 * m + 3 * b)[f // 2]
        index = jnp.where(lane < 80, index, 64)
        t = jnp.where(
            wide < 32,
            take(tiles[0], index),
            jnp.where(wide < 64, take(tiles[1], index), take(tiles[2], index)),
        )
        rows.append(t)
    return jnp.concatenate(rows, axis=0)


def lifted(x):
    lane = lanes()
    wide = lanes(E)
    n = lane & 63
    i, j, k = n >> 4, (n >> 2) & 3, n & 3
    places = (4 * j + k, 4 * i + k, 4 * i + j)
    layers = (i, j, k)
    wide_layers = ((wide >> 4) & 3, (wide >> 2) & 3, wide & 3)
    tiles = [None] * 3
    for a in range(3):
        first, last = x[64 * a : 64 * a + 32], turn(x[64 * a + 32 : 64 * a + 64], 64)
        pair = jnp.where(wide < 64, first, last)
        tail = jnp.where(wide < 16, last, first)
        ends = (wide_layers[a] == 0) | (wide_layers[a] == 3)
        for tile in range(3):
            v = 2 * tile + (lane >> 6)
            index = v * 16 + places[a]
            at_last = jnp.where(layers[a] == 3, 64, 0)
            if tile < 2:
                part = take(pair, index + at_last)
            else:
                part = take(tail, jnp.where(lane < 64, index - at_last, 80))
            part = jnp.where(ends, part, 0.0)
            tiles[tile] = part if tiles[tile] is None else tiles[tile] + part
    return tiles


def lifted_traces(x):
    lane = lanes()
    wide = lanes(E)
    v16 = lane & 112
    r, s = (lane >> 2) & 3, lane & 3
    wide_r, wide_s = (wide >> 2) & 3, wide & 3
    rows = []
    for f in range(6):
        a, b = f // 2, f % 2
        total = x[32 * f : 32 * (f + 1)]
        for place, side in ((0, wide_r), (1, wide_s)):
            axis = [other for other in range(3) if other != a][place]
            free = (s, r)[place]
            node = 12 * b + free if a < [o for o in range(3) if o != axis and o != a][0] else 4 * free + 3 * b
            index = v16 + node
            first = take(x[64 * axis : 64 * axis + 32], index)
            last = take(x[64 * axis + 32 : 64 * axis + 64], index)
            total = total + jnp.where(side == 0, first, jnp.where(side == 3, last, 0.0))
        rows.append(total)
    return jnp.concatenate(rows, axis=0)


def by_axis(function, *arrays):
    return jnp.concatenate(
        [function(a, *[x[64 * a : 64 * (a + 1)] for x in arrays]) for a in range(3)], axis=0)


def signed(x):
    return jnp.concatenate([-x[:32], x[32:]], axis=0)


class Faces:
    def __init__(self):
        lane = lanes()
        self.v = lane >> 4
        self.m = lane & 15
        self.ends = mask((self.v == 0) | (self.v == 4))
        self.last = mask(self.v == 4)
        self.normal = [mask(self.v == a + 1) for a in range(3)]
        self.normal_index = [(a + 1) * 16 + self.m for a in range(3)]
        self.pressure_index = 64 + self.m

    def normal_of(self, x):
        return by_axis(lambda a, x: take(x, self.normal_index[a]), x)

    def pressure_of(self, x):
        return take(x, self.pressure_index)

    def flux(self, x, u=None, p=None):
        u = self.normal_of(x) if u is None else u
        p = self.pressure_of(x) if p is None else p

        def along(a, x, u, p):
            c = u + mean_flow if a == 0 else u
            return signed(c * x + self.ends * u + self.normal[a] * p)

        return by_axis(along, x, u, p)

    def flux_back(self, x, u, w):
        def along(a, x, u, w, h):
            n = take(w, self.normal_index[a])
            c = u + mean_flow if a == 0 else u
            return signed(c * w + self.last * n + self.normal[a] * h)

        return by_axis(along, x, u, w, over_fields((x + self.ends) * w))

    def rest_back(self, w):
        def along(a, w, h):
            n = take(w, self.normal_index[a])
            part = self.last * n + self.normal[a] * h
            return signed(mean_flow * w + part if a == 0 else part)

        return by_axis(along, w, over_fields(self.ends * w))

    def state_back(self, x, u, w):
        def along(a, u, w, h):
            return signed(u * w + self.normal[a] * h)

        return by_axis(along, u, w, over_fields(x * w))

    def shifted(self, d):
        target = self.v + d
        target = jnp.where(target >= 5, target - 5, target)
        return target, jnp.where(self.v < 5, target * 16 + self.m, 16 * self.v + self.m)

    def hessian(self, d, y):
        target, index = self.shifted(d)

        def along(a, y):
            back = mask((self.v < 5) & (target == a + 1))
            return signed(-0.5 * (self.normal[a] * take(y, index) + back * y))

        return by_axis(along, y)

    def mirror(self, x):
        return by_axis(lambda a, x: x * (1.0 - 2.0 * self.normal[a]), x)


def over_fields(h):
    table = ((lax.broadcasted_iota(i32, (128, 128), 0) ^ lax.broadcasted_iota(i32, (128, 128), 1)) & 15) == 0
    table = mask(table).astype(bf16)
    hi, lo = halves(h)
    return dot(jnp.concatenate([hi, lo], axis=1), jnp.concatenate([table, table], axis=0))


def column_of(table_ref):
    x = table_ref[...].astype(f32)
    x = jnp.concatenate([x, jnp.zeros((2, E), f32)], axis=0)
    t = jnp.transpose(x)
    return jnp.concatenate([t[:, f : f + 1] for f in range(6)], axis=0).astype(i32)


def row_of(table_ref):
    return jnp.concatenate([table_ref[f : f + 1, :] for f in range(6)], axis=1)


def slot_column(send):
    x = jnp.broadcast_to(send.astype(f32), (8, S))
    return jnp.transpose(x)[:, :1].astype(i32)


def onehot(rows, columns, first, second):
    return jnp.where(first == second, 1.0, 0.0).astype(bf16)


def faces_from_columns(ext_col):
    return onehot(F, F, ext_col, lax.broadcasted_iota(i32, (F, F), 1))


def columns_from_faces(ext_row):
    return onehot(F, F, ext_row, lax.broadcasted_iota(i32, (F, F), 0))


def faces_from_slots(ext_col):
    return onehot(F, S, ext_col - F, lax.broadcasted_iota(i32, (F, S), 1))


def slots_from_faces(ext_row):
    return onehot(S, F, ext_row - F, lax.broadcasted_iota(i32, (S, F), 0))


def slots_from_columns(send_col):
    return onehot(S, F, send_col, lax.broadcasted_iota(i32, (S, F), 1))


def columns_from_slots(send_row):
    return onehot(F, S, send_row, lax.broadcasted_iota(i32, (F, S), 0))


def orientation(perm_col):
    lane = lanes(F)
    m = lane & 15
    crossed = lane - m + ((m & 3) * 4 + (m >> 2))
    k = jnp.broadcast_to(perm_col, (F, 128))
    flips = (k & 1) * 12 + ((k & 2) >> 1) * 3
    crossed_flips = (k & 1) * 3 + ((k & 2) >> 1) * 12
    swap = (k & 4) == 4
    place = jnp.where(swap, crossed, lane)
    return place ^ jnp.where(swap, crossed_flips, flips), place ^ flips


def peer_tables(send_ref, ext_ref):
    odd = (lax.axis_index("dom") & 1) == 1
    send = send_ref[...]
    swapped = jnp.concatenate([send[:, 2 * G :], send[:, G : 2 * G], send[:, :G]], axis=1)
    send = jnp.where(odd, send, swapped)

    def reordered(table):
        slot = table - F
        turned = jnp.where(slot < G, slot + 2 * G, jnp.where(slot >= 2 * G, slot - 2 * G, slot))
        turned = jnp.where((slot >= 0) & (slot < S), turned + F, table)
        return jnp.where(odd, turned, table)

    return send, reordered(column_of(ext_ref)), reordered(row_of(ext_ref))


def packed(x):
    lane = lanes(F)
    first = jnp.where(lane >= 64, turn(x, 64), 0.0)
    second = jnp.where((lane >= 80) & (lane < 96), turn(x, 16), 0.0)
    return jnp.concatenate([first, second], axis=1).astype(bf16)


def exterior(faces, wall, index, onehot_local, t, u):
    g = select_rows(onehot_local, t)
    node = index & 15
    x = jnp.where(wall, faces.mirror(t), take(g, index))
    v = by_axis(lambda a, g, node: take(g, (a + 1) * 16 + node), g, node)
    return x, jnp.where(wall, -u, v)


def folded(x):
    y = x.reshape(8, 16, 128)
    return (y[:, :8].reshape(64, 128) + turn(y[:, 8:].reshape(64, 128), 64)).reshape(8, 8, 128)


def folded_copies(x, at):
    y = x.reshape(8, 16, 128)
    group = lanes() >> 5
    low, high = mask(group == at), mask(group == at + 2)
    return (low * y[:, :8].reshape(64, 128) + high * y[:, 8:].reshape(64, 128)).reshape(8, 8, 128)


def unfolded(z):
    z = z.reshape(64, 128)
    low = mask(lanes() < 64)
    halves = [(low * part).reshape(8, 8, 128) for part in (z, turn(z, 64))]
    return jnp.concatenate(halves, axis=1).reshape(G, 128)


def places():
    own = jnp.where((lax.axis_index("dom") & 1) == 1, 0, 8)
    return own, 8 - own


def pack_kernel(state_hbm, final_hbm, send_hbm, ext_hbm, perm_hbm,
                chip_ref, out_ref, q_ref, w_ref, t_ref, lam_ref, send_slots_ref, back_slots_ref, inverse_ref,
                send_ref, ext_ref, perm_ref, state_ref, final_ref, sems):
    pairs = ((send_hbm, send_ref), (ext_hbm, ext_ref), (perm_hbm, perm_ref), (final_hbm, final_ref), (state_hbm, state_ref))
    copies = [pltpu.make_async_copy(a, b, sems.at[i]) for i, (a, b) in enumerate(pairs)]
    for copy in copies:
        copy.start()
    faces = Faces()
    for copy in copies[:3]:
        copy.wait()
    send, _, ext_row = peer_tables(send_ref, ext_ref)
    send_slots = slots_from_columns(slot_column(send))
    back_slots = slots_from_faces(ext_row)
    send_slots_ref[...] = send_slots
    back_slots_ref[...] = back_slots
    _, inverse = orientation(column_of(perm_ref))
    inverse_ref[...] = inverse
    for copy in copies[3:]:
        copy.wait()
    q = to_tiles(state_ref)
    w = to_tiles(final_ref)
    store_tiles(q_ref, q)
    store_tiles(w_ref, w)
    t = traces(q)
    lam = lift_factor * traces(w)
    t_ref[...] = t
    lam_ref[...] = lam
    y = take(lam, inverse)
    diagonal = by_axis(lambda a, y: signed(-faces.normal[a] * y), y)
    first = y - 0.5 * faces.rest_back(y) + turn(diagonal, 64)
    stack = jnp.concatenate([x.astype(bf16) for x in (first, faces.hessian(1, y), faces.hessian(2, y))], axis=1)
    back = dot(back_slots, stack)
    forward = dot(send_slots, packed(t))
    parts = [back[:, :128], back[:, 128:256] + forward[:, :128], back[:, 256:] + forward[:, 128:]]
    own, other = places()
    lane = lanes()
    guest = mask(lane >= 96) * turn(parts[2][:G], 32)
    rest = folded(mask(lane < 64) * parts[2][:G])
    for peer in range(8):
        at = 16 * peer
        chip_ref[peer] = jnp.concatenate(
            [guest[at : at + 16], parts[0][at : at + 16], parts[1][at : at + 16], rest[peer]], axis=0).astype(bf16)
        for o, place in ((1, own), (2, other)):
            at = G * o + 16 * peer
            for j in range(3):
                out_ref[place + peer, 16 * j : 16 * (j + 1)] = parts[j][at : at + 16].astype(bf16)


def first_local_kernel(q_ref, w_ref, t_ref, lam_ref, send_ref, ext_ref, perm_ref, forward_ref, backward_ref,
                       base_ref, t_base_ref, z_ref, rest_ref, u_ref, x_ref, v_ref,
                       from_slots_ref, to_columns_ref, local_ref, local_back_ref, index_ref, kind_ref):
    faces = Faces()
    send, ext_col, ext_row = peer_tables(send_ref, ext_ref)
    index, _ = orientation(column_of(perm_ref))
    index_ref[...] = index
    ext_wide = jnp.broadcast_to(ext_col, (F, 128))
    wall = ext_wide == F + S
    kind_ref[...] = jnp.where(wall, 2, jnp.where(ext_wide >= F, 1, 0))
    from_slots_ref[...] = faces_from_slots(ext_col)
    to_columns_ref[...] = columns_from_slots(send)
    local = faces_from_columns(ext_col)
    local_ref[...] = local
    local_back_ref[...] = columns_from_faces(ext_row)
    q = load_tiles(q_ref)
    t = t_ref[...]
    lam = lam_ref[...]
    rest_ref[...] = lam - 0.5 * faces.rest_back(lam)
    u = faces.normal_of(t)
    x, v = exterior(faces, wall, index, local, t, u)
    u_ref[...] = u
    x_ref[...] = x
    v_ref[...] = v
    jump = 0.5 * (faces.flux(t, u) - faces.flux(x, v)) + (x - t)
    faced = lifted(lift_factor * jump)
    inner = volume(q, forward_ref[...])
    base = [q[j] + step_size * (inner[j] + faced[j]) for j in range(3)]
    store_tiles(base_ref, base)
    t_base_ref[...] = traces(base)
    z_ref[...] = derivative_back(load_tiles(w_ref), backward_ref[...])


def middle_kernel(base_ref, t_base_ref, w_ref, lam_ref, rest_ref, z_ref, arrived_ref,
                  from_slots_ref, to_columns_ref, local_ref, local_back_ref, send_slots_ref, back_slots_ref,
                  index_ref, inverse_ref, kind_ref,
                  chip_ref, out_ref, q1_ref, w1_ref, t1_ref, u1_ref, x1_ref, v1_ref, lam1_ref):
    faces = Faces()
    index = index_ref[...]
    inverse = inverse_ref[...]
    kind = kind_ref[...]
    wall = kind == 2
    wide = lanes(F)
    lane = lanes()
    node = index & 15
    own, other = places()
    mine, theirs = arrived_ref[pl.ds(own, 8)], arrived_ref[pl.ds(other, 8)]
    third = mine[:, 32:48].reshape(G, 128)
    guest = mask((lane >= 64) & (lane < 96)) * turn(third.astype(f32), 96)
    rest = unfolded(mine[:, 80:].astype(f32))
    kept = lanes(G) < 96
    zero = jnp.zeros((G, 128), bf16)
    third = jnp.concatenate(
        [jnp.where(kept, third, zero), jnp.where(kept, theirs[:, 32:48].reshape(G, 128), zero)], axis=0)
    tiles = [jnp.concatenate([x.reshape(G, 128) for x in blocks], axis=0) for blocks in (
        (mine[:, 48:64], mine[:, :16], theirs[:, :16]), (mine[:, 64:80], mine[:, 16:32], theirs[:, 16:32]))]
    g = dot(from_slots_ref[...], jnp.concatenate(
        [tiles[1], jnp.concatenate([guest.astype(bf16), third], axis=0)], axis=1))
    sums = dot(to_columns_ref[...], jnp.concatenate(
        tiles + [jnp.concatenate([(guest + rest).astype(bf16), third], axis=0)], axis=1))
    g0, g1 = g[:, :128], g[:, 128:]
    place = jnp.where(wide < 64, index + 64, jnp.where(wide < 80, index + 16, 96 + node))
    xr = jnp.where(wide < 64, take(g0, place), take(g1, place))
    ur = by_axis(lambda a, g, node: take(g, 80 + 16 * a + node), g0, node)
    pr = take(g1, 80 + node)
    jump = (lift_factor * step_size) * (xr - 0.5 * faces.flux(xr, ur, pr))
    t1 = t_base_ref[...] + lifted_traces(jump)
    faced = lifted(jump)
    base = load_tiles(base_ref)
    q1 = [base[j] + faced[j] for j in range(3)]
    store_tiles(q1_ref, q1)
    t1_ref[...] = t1
    t1_sent = t1.astype(bf16)
    forward = dot(send_slots_ref[...], t1_sent)
    lam = lam_ref[...]
    rest = rest_ref[...]
    u1 = faces.normal_of(t1)
    u1_ref[...] = u1
    x1, v1 = exterior(faces, wall, index, local_ref[...], t1, u1)
    x1_ref[...] = x1
    v1_ref[...] = v1
    bar = jnp.where(kind == 1, 0.0, rest - 0.5 * faces.state_back(x1, v1, lam))
    total = 0.5 * faces.state_back(t1, u1, lam) - rest + jnp.where(wall, faces.mirror(bar), 0.0)
    total = total + select_rows(local_back_ref[...], take(bar, inverse))
    sent = t1_sent.astype(f32)
    h0, h1, h2 = sums[:, :128], mask(lane < 64) * sums[:, 128:256], sums[:, 256:]
    ahead1, ahead2, behind2, behind1 = [faces.shifted(d)[1] for d in (1, 2, 3, 4)]
    through = h0 + h1 * take(sent, ahead1) + h2 * take(sent, ahead2)
    through = through + take(h1 * sent, behind1) + take(h2 * sent, behind2)
    through = through + mask((lane >= 16) & (lane < 64)) * turn(h0, 64) * sent
    total = total + mask(lane < 80) * through
    inner = volume_back(q1, z_ref[...])
    w = load_tiles(w_ref)
    half = [0.5 * w[j] + (0.5 * step_size) * inner[j] for j in range(3)]
    lam1 = lift_factor * traces(half) + (0.5 * step_size * lift_factor) * lifted_traces(total)
    faced = lifted(total)
    store_tiles(w1_ref, [half[j] + (0.5 * step_size) * faced[j] for j in range(3)])
    lam1_ref[...] = lam1
    bar = lam1 - 0.5 * faces.flux_back(xr, ur, lam1)
    first = take(bar, jnp.where(wide >= 80, inverse - 80, 80))
    second = take(bar, (inverse & 15) + 48 + (wide & 16))
    back = dot(back_slots_ref[...], jnp.concatenate([first, second], axis=1).astype(bf16))
    main = back[:, :128] + forward
    tail = [folded_copies(back[G * o : G * (o + 1), 128:], min(o, 1)) for o in range(3)]
    zero = jnp.zeros((16, 128), f32)
    for peer in range(8):
        at = 16 * peer
        chip_ref[peer] = jnp.concatenate([main[at : at + 16], tail[0][peer]], axis=0).astype(bf16)
        for o, place in ((1, own), (2, other)):
            at = G * o + 16 * peer
            out_ref[place + peer] = jnp.concatenate([main[at : at + 16], zero, tail[o][peer]], axis=0).astype(bf16)


def second_local_kernel(q_ref, w_ref, t_ref, u_ref, x_ref, v_ref, q1_ref, w1_ref, t1_ref, u1_ref, x1_ref, v1_ref,
                        lam1_ref, local_back_ref, inverse_ref, kind_ref,
                        forward_ref, backward_ref, end_ref, start_ref):
    faces = Faces()
    inverse = inverse_ref[...]
    kind = kind_ref[...]
    wall = kind == 2
    q = load_tiles(q_ref)
    q1 = load_tiles(q1_ref)
    t1 = t1_ref[...]
    x1 = x1_ref[...]
    jump = 0.5 * (faces.flux(t1, u1_ref[...]) - faces.flux(x1, v1_ref[...])) + (x1 - t1)
    faced = lifted(lift_factor * jump)
    inner = volume(q1, forward_ref[...])
    store_tiles(end_ref, [0.5 * q[j] + 0.5 * (q1[j] + step_size * (inner[j] + faced[j])) for j in range(3)])
    t = t_ref[...]
    lam1 = lam1_ref[...]
    u, x, v = u_ref[...], x_ref[...], v_ref[...]
    rest = lam1 - 0.5 * faces.rest_back(lam1)
    bar = jnp.where(kind == 1, 0.0, rest - 0.5 * faces.state_back(x, v, lam1))
    total = 0.5 * faces.state_back(t, u, lam1) - rest + jnp.where(wall, faces.mirror(bar), 0.0)
    total = total + select_rows(local_back_ref[...], take(bar, inverse))
    w = load_tiles(w_ref)
    w1 = load_tiles(w1_ref)
    inner = volume_back(q, derivative_back(w1, backward_ref[...]))
    faced = lifted(total)
    store_tiles(start_ref, [0.5 * w[j] + w1[j] + step_size * (inner[j] + faced[j]) for j in range(3)])


def last_kernel(end_base_ref, start_base_ref, arrived_ref, from_slots_ref, to_columns_ref, index_ref,
                end_ref, start_ref):
    faces = Faces()
    own, other = places()
    mine, theirs = arrived_ref[pl.ds(own, 8)], arrived_ref[pl.ds(other, 8)]
    main = jnp.concatenate(
        [mine[:, 16:32].reshape(G, 128), mine[:, :16].reshape(G, 128), theirs[:, :16].reshape(G, 128)], axis=0)
    lane = lanes()
    tail, next_tail = unfolded(mine[:, 32:].astype(f32)), unfolded(theirs[:, 32:].astype(f32))
    late = mask(lane >= 32)
    shared = jnp.concatenate([mask(lane < 32) * tail, late * tail, late * next_tail], axis=0).astype(bf16)
    node = index_ref[...] & 15
    g = dot(from_slots_ref[...], main)
    b = jnp.concatenate([dot(to_columns_ref[...], main), dot(to_columns_ref[...], shared)], axis=1)
    lane = lanes()
    valid = mask(lane < 80)
    xr = valid * take(g, index_ref[...])
    ur = by_axis(lambda a, g, node: take(g, (a + 1) * 16 + node), g, node)
    pr = take(g, 64 + node)
    faced = lifted((0.5 * step_size * lift_factor) * (xr - 0.5 * faces.flux(xr, ur, pr)))
    base = load_tiles(end_base_ref)
    from_tiles([base[j] + faced[j] for j in range(3)], end_ref)
    high = turn(b[:, 128:], 48) + turn(b[:, 128:], 16)
    bar = mask(lane < 48) * turn(b[:, :128], 48) + mask((lane >= 48) & (lane < 80)) * high
    faced = lifted(step_size * bar)
    base = load_tiles(start_base_ref)
    from_tiles([base[j] + faced[j] for j in range(3)], start_ref)


def shape(*dims, dtype=f32):
    return jax.ShapeDtypeStruct(dims, dtype)


def call(kernel, outs, *args, scratch=(), in_hbm=False):
    return pl.pallas_call(
        kernel,
        out_shape=outs,
        in_specs=[pl.BlockSpec(memory_space=pl.ANY if in_hbm else pltpu.VMEM)] * len(args),
        scratch_shapes=scratch,
        cost_estimate=pl.CostEstimate(flops=200_000_000, bytes_accessed=1_000_000, transcendentals=0),
        compiler_params=pltpu.CompilerParams(vmem_limit_bytes=32 * 1024 * 1024),
    )(*args)


def pair_peers(whole):
    count, peers = lax.axis_size("dom"), lax.axis_size("sub")
    groups = [[d % count * peers + peer for d in (first, first + 1) for peer in range(peers)]
              for first in range(1, count, 2)]
    return lax.all_to_all(
        whole, ("dom", "sub"), split_axis=0, concat_axis=0, tiled=True, axis_index_groups=groups)


def chip_partner(value):
    return lax.ppermute(value, "dom", [(d, d ^ 1) for d in range(lax.axis_size("dom"))])


def shards(state, adjoint_final, send_slot, ext_index, ext_perm):
    forward, backward = derivative_operands()
    forward, backward = jnp.asarray(forward), jnp.asarray(backward)
    state, adjoint_final = jnp.swapaxes(state, 1, 2), jnp.swapaxes(adjoint_final, 1, 2)
    node = shape(E, 384)
    face = shape(F, 128)
    index_face = shape(F, 128, dtype=i32)

    to_chip, out, q, w, t, lam, send_slots, back_slots, inverse, send_slot, ext_index, ext_perm = call(
        pack_kernel,
        (shape(8, 56, 128, dtype=bf16), shape(16, 88, 128, dtype=bf16), node, node, face, face,
         shape(S, F, dtype=bf16), shape(S, F, dtype=bf16), index_face,
         shape(1, S, dtype=i32), shape(6, E, dtype=i32), shape(6, E, dtype=i32)),
        *[pltpu.with_memory_space_constraint(x, pltpu.HBM) for x in (state, adjoint_final, send_slot, ext_index, ext_perm)], in_hbm=True,
        scratch=[pltpu.VMEM((5, E, 64), f32), pltpu.VMEM((5, E, 64), f32), pltpu.SemaphoreType.DMA((5,))])
    from_chip = chip_partner(to_chip)
    base, t_base, z, rest, u, x, v, from_slots, to_columns, local, local_back, index, kind = call(
        first_local_kernel,
        (node, face, shape(96, 384), face, face, face, face, shape(F, S, dtype=bf16), shape(F, S, dtype=bf16),
         shape(F, F, dtype=bf16), shape(F, F, dtype=bf16), index_face, index_face),
        q, w, t, lam, send_slot, ext_index, ext_perm, forward, backward)
    for start in (0, 8):
        out = lax.dynamic_update_slice(out, from_chip[:, 16:], (start, 48, 0))
        out = lax.dynamic_update_slice(out, out[start : start + 8, 32:48] + from_chip[:, :16], (start, 32, 0))
    out, z = lax.optimization_barrier((out, z))
    arrived = pair_peers(out)
    to_chip, out, q1, w1, t1, u1, x1, v1, lam1 = call(
        middle_kernel, (shape(8, 24, 128, dtype=bf16), shape(16, 40, 128, dtype=bf16), node, node, face, face, face, face, face),
        base, t_base, w, lam, rest, z, arrived,
        from_slots, to_columns, local, local_back, send_slots, back_slots, index, inverse, kind)
    from_chip = chip_partner(to_chip)
    end_base, start_base = call(
        second_local_kernel, (node, node),
        q, w, t, u, x, v, q1, w1, t1, u1, x1, v1, lam1, local_back, inverse, kind, forward, backward)
    out = lax.dynamic_update_slice(out, out[:8, 16:] + from_chip, (0, 16, 0))
    out = lax.dynamic_update_slice(out, out[8:, 16:] + from_chip, (8, 16, 0))
    out, end_base = lax.optimization_barrier((out, end_base))
    arrived = pair_peers(out)
    out = shape(5, E, 64)
    end, start = call(
        last_kernel, (out, out),
        end_base, start_base, arrived, from_slots, to_columns, index)
    return jnp.swapaxes(end, 1, 2), jnp.swapaxes(start, 1, 2)


def solution(mesh):
    return jax.shard_map(
        shards,
        mesh=mesh,
        in_specs=(
            P(None, None, ("dom", "sub")),
            P(None, None, ("dom", "sub")),
            P(("dom", "sub"), None),
            P(None, ("dom", "sub")),
            P(None, ("dom", "sub")),
        ),
        out_specs=(P(None, None, ("dom", "sub")), P(None, None, ("dom", "sub"))),
        check_vma=False,
    )
```

```python
import jax
import jax.numpy as jnp
import numpy as np
import ml_dtypes
from jax import lax
from jax.experimental import pallas as pl
from jax.experimental.pallas import tpu as pltpu
from jax.sharding import PartitionSpec as P

step_size = 0.02
mean_flow = 0.3
lift_factor = 12.0

E = 32
F = 192
S = 384
G = 128
f32 = jnp.float32
bf16 = jnp.bfloat16
i32 = jnp.int32


def derivative_table():
    points = np.array([-1.0, -1.0 / np.sqrt(5.0), 1.0 / np.sqrt(5.0), 1.0])
    products = np.array(
        [np.prod([points[t] - points[s] for s in range(4) if s != t]) for t in range(4)]
    )
    result = np.zeros((4, 4))
    for t in range(4):
        for s in range(4):
            if t != s:
                result[t, s] = products[t] / (products[s] * (points[t] - points[s]))
        result[t, t] = -np.sum(result[t])
    return result.astype(np.float32)


def halves_of(matrix):
    hi = matrix.astype(ml_dtypes.bfloat16)
    lo = (matrix - hi.astype(np.float32)).astype(ml_dtypes.bfloat16)
    return hi, lo


def derivative_operands():
    d = -2.0 * derivative_table()
    eye = np.eye(4, dtype=np.float32)
    along = [
        np.kron(d, np.kron(eye, eye)),
        np.kron(eye, np.kron(d, eye)),
        np.kron(eye, np.kron(eye, d)),
    ]
    two = [np.kron(np.eye(2, dtype=np.float32), a).astype(np.float32) for a in along]
    hi, lo = halves_of(np.concatenate([t.T for t in two], axis=0))
    forward = np.concatenate([hi, lo], axis=1)
    hi, lo = halves_of(np.concatenate(two, axis=1))
    backward = np.concatenate([hi, lo], axis=1)
    return forward, backward


def lanes(rows=1):
    return lax.broadcasted_iota(i32, (rows, 128), 1)


def take(x, index):
    return jnp.take_along_axis(x, jnp.broadcast_to(index, x.shape), axis=1)


def mask(condition):
    return jnp.where(condition, 1.0, 0.0).astype(f32)


def turn(x, shift):
    return pltpu.roll(x, shift, 1)


def halves(x):
    hi = x.astype(bf16)
    lo = (x - hi.astype(f32)).astype(bf16)
    return hi, lo


def dot(a, b):
    return jnp.dot(a, b, preferred_element_type=f32)


def select_rows(onehot, x):
    hi, lo = halves(x)
    r = dot(onehot, jnp.concatenate([hi, lo], axis=1))
    return r[:, :128] + r[:, 128:]


def to_tiles(ref):
    zero = jnp.zeros((E, 64), f32)
    tiles = []
    for j in range(3):
        high = ref[2 * j + 1] if j < 2 else zero
        tiles.append(jnp.concatenate([ref[2 * j], high], axis=1))
    return tiles


def from_tiles(tiles, ref):
    for j in range(3):
        ref[2 * j] = tiles[j][:, :64]
        if j < 2:
            ref[2 * j + 1] = tiles[j][:, 64:]


def load_tiles(ref):
    return [ref[:, 128 * j : 128 * (j + 1)] for j in range(3)]


def store_tiles(ref, tiles):
    for j in range(3):
        ref[:, 128 * j : 128 * (j + 1)] = tiles[j]


def spread(tiles):
    low = lanes(E) < 64
    back0, back1, back2 = turn(tiles[0], 64), turn(tiles[1], 64), turn(tiles[2], 64)
    ux = jnp.where(low, back0, tiles[0])
    uy = jnp.where(low, tiles[1], back1)
    uz = jnp.where(low, back1, tiles[1])
    p = tiles[2] + back2
    return low, (ux, uy, uz), p


def volume(tiles, table):
    low, speeds, p = spread(tiles)
    fluxes = []
    for a in range(3):
        u = speeds[a]
        c = u + mean_flow if a == 0 else u
        high0 = p if a == 0 else jnp.zeros_like(p)
        parts = [c * tiles[0] + jnp.where(low, u, high0), c * tiles[1], c * tiles[2] + jnp.where(low, u, 0.0)]
        if a == 1:
            parts[1] = parts[1] + jnp.where(low, p, 0.0)
        if a == 2:
            parts[1] = parts[1] + jnp.where(low, 0.0, p)
        fluxes.append(jnp.concatenate(parts, axis=0))
    hi, lo = halves(jnp.concatenate(fluxes, axis=1))
    r = dot(jnp.concatenate([hi, lo], axis=0), table)
    out = r[:96, :128] + (r[:96, 128:] + r[96:, :128])
    return [out[:32], out[32:64], out[64:96]]


def derivative_back(tiles, table):
    hi, lo = halves(jnp.concatenate(tiles, axis=0))
    r = dot(jnp.concatenate([hi, lo], axis=0), table)
    return r[:96, :384] + (r[:96, 384:] + r[96:, :384])


def volume_back(tiles, z):
    low, speeds, _ = spread(tiles)
    one = jnp.where(low, 1.0, 0.0).astype(f32)
    plus = [tiles[0] + one, tiles[1], tiles[2] + one]
    out = [jnp.zeros((E, 128), f32) for _ in range(3)]
    sums = []
    parts = []
    for a in range(3):
        c = speeds[a] + mean_flow if a == 0 else speeds[a]
        za = [z[32 * j : 32 * (j + 1), 128 * a : 128 * (a + 1)] for j in range(3)]
        total = plus[0] * za[0] + plus[1] * za[1] + plus[2] * za[2]
        sums.append(total + turn(total, 64))
        parts.append(za)
        out = [out[j] + c * za[j] for j in range(3)]
    pressure = turn(parts[0][0], 64) + parts[1][1] + turn(parts[2][1], 64)
    out[0] = out[0] + jnp.where(low, 0.0, sums[0])
    out[1] = out[1] + jnp.where(low, sums[1], sums[2])
    out[2] = out[2] + jnp.where(low, pressure, 0.0)
    return out


def traces(tiles):
    lane = lanes()
    wide = lanes(E)
    m = lane & 15
    r, s = m >> 2, m & 3
    base = ((lane >> 4) & 1) * 64
    rows = []
    for f in range(6):
        b = f % 2
        index = base + (48 * b + m, 16 * r + 12 * b + s, 4 * m + 3 * b)[f // 2]
        index = jnp.where(lane < 80, index, 64)
        t = jnp.where(
            wide < 32,
            take(tiles[0], index),
            jnp.where(wide < 64, take(tiles[1], index), take(tiles[2], index)),
        )
        rows.append(t)
    return jnp.concatenate(rows, axis=0)


def lifted(x):
    lane = lanes()
    wide = lanes(E)
    n = lane & 63
    i, j, k = n >> 4, (n >> 2) & 3, n & 3
    places = (4 * j + k, 4 * i + k, 4 * i + j)
    layers = (i, j, k)
    wide_layers = ((wide >> 4) & 3, (wide >> 2) & 3, wide & 3)
    tiles = [None] * 3
    for a in range(3):
        first, last = x[64 * a : 64 * a + 32], turn(x[64 * a + 32 : 64 * a + 64], 64)
        pair = jnp.where(wide < 64, first, last)
        tail = jnp.where(wide < 16, last, first)
        ends = (wide_layers[a] == 0) | (wide_layers[a] == 3)
        for tile in range(3):
            v = 2 * tile + (lane >> 6)
            index = v * 16 + places[a]
            at_last = jnp.where(layers[a] == 3, 64, 0)
            if tile < 2:
                part = take(pair, index + at_last)
            else:
                part = take(tail, jnp.where(lane < 64, index - at_last, 80))
            part = jnp.where(ends, part, 0.0)
            tiles[tile] = part if tiles[tile] is None else tiles[tile] + part
    return tiles


def lifted_traces(x):
    lane = lanes()
    wide = lanes(E)
    v16 = lane & 112
    r, s = (lane >> 2) & 3, lane & 3
    wide_r, wide_s = (wide >> 2) & 3, wide & 3
    rows = []
    for f in range(6):
        a, b = f // 2, f % 2
        total = x[32 * f : 32 * (f + 1)]
        for place, side in ((0, wide_r), (1, wide_s)):
            axis = [other for other in range(3) if other != a][place]
            free = (s, r)[place]
            node = 12 * b + free if a < [o for o in range(3) if o != axis and o != a][0] else 4 * free + 3 * b
            index = v16 + node
            first = take(x[64 * axis : 64 * axis + 32], index)
            last = take(x[64 * axis + 32 : 64 * axis + 64], index)
            total = total + jnp.where(side == 0, first, jnp.where(side == 3, last, 0.0))
        rows.append(total)
    return jnp.concatenate(rows, axis=0)


def by_axis(function, *arrays):
    return jnp.concatenate(
        [function(a, *[x[64 * a : 64 * (a + 1)] for x in arrays]) for a in range(3)], axis=0)


def signed(x):
    return jnp.concatenate([-x[:32], x[32:]], axis=0)


class Faces:
    def __init__(self):
        lane = lanes()
        self.v = lane >> 4
        self.m = lane & 15
        self.ends = mask((self.v == 0) | (self.v == 4))
        self.last = mask(self.v == 4)
        self.normal = [mask(self.v == a + 1) for a in range(3)]
        self.normal_index = [(a + 1) * 16 + self.m for a in range(3)]
        self.pressure_index = 64 + self.m

    def normal_of(self, x):
        return by_axis(lambda a, x: take(x, self.normal_index[a]), x)

    def pressure_of(self, x):
        return take(x, self.pressure_index)

    def flux(self, x, u=None, p=None):
        u = self.normal_of(x) if u is None else u
        p = self.pressure_of(x) if p is None else p

        def along(a, x, u, p):
            c = u + mean_flow if a == 0 else u
            return signed(c * x + self.ends * u + self.normal[a] * p)

        return by_axis(along, x, u, p)

    def flux_back(self, x, u, w):
        def along(a, x, u, w, h):
            n = take(w, self.normal_index[a])
            c = u + mean_flow if a == 0 else u
            return signed(c * w + self.last * n + self.normal[a] * h)

        return by_axis(along, x, u, w, over_fields((x + self.ends) * w))

    def rest_back(self, w):
        def along(a, w, h):
            n = take(w, self.normal_index[a])
            part = self.last * n + self.normal[a] * h
            return signed(mean_flow * w + part if a == 0 else part)

        return by_axis(along, w, over_fields(self.ends * w))

    def state_back(self, x, u, w):
        def along(a, u, w, h):
            return signed(u * w + self.normal[a] * h)

        return by_axis(along, u, w, over_fields(x * w))

    def shifted(self, d):
        target = self.v + d
        target = jnp.where(target >= 5, target - 5, target)
        return target, jnp.where(self.v < 5, target * 16 + self.m, 16 * self.v + self.m)

    def hessian(self, d, y):
        target, index = self.shifted(d)

        def along(a, y):
            back = mask((self.v < 5) & (target == a + 1))
            return signed(-0.5 * (self.normal[a] * take(y, index) + back * y))

        return by_axis(along, y)

    def mirror(self, x):
        return by_axis(lambda a, x: x * (1.0 - 2.0 * self.normal[a]), x)


def over_fields(h):
    table = ((lax.broadcasted_iota(i32, (128, 128), 0) ^ lax.broadcasted_iota(i32, (128, 128), 1)) & 15) == 0
    table = mask(table).astype(bf16)
    hi, lo = halves(h)
    return dot(jnp.concatenate([hi, lo], axis=1), jnp.concatenate([table, table], axis=0))


def column_of(table_ref):
    x = table_ref[...].astype(f32)
    x = jnp.concatenate([x, jnp.zeros((2, E), f32)], axis=0)
    t = jnp.transpose(x)
    return jnp.concatenate([t[:, f : f + 1] for f in range(6)], axis=0).astype(i32)


def row_of(table_ref):
    return jnp.concatenate([table_ref[f : f + 1, :] for f in range(6)], axis=1)


def slot_column(send):
    x = jnp.broadcast_to(send.astype(f32), (8, S))
    return jnp.transpose(x)[:, :1].astype(i32)


def onehot(rows, columns, first, second):
    return jnp.where(first == second, 1.0, 0.0).astype(bf16)


def faces_from_columns(ext_col):
    return onehot(F, F, ext_col, lax.broadcasted_iota(i32, (F, F), 1))


def columns_from_faces(ext_row):
    return onehot(F, F, ext_row, lax.broadcasted_iota(i32, (F, F), 0))


def faces_from_slots(ext_col):
    return onehot(F, S, ext_col - F, lax.broadcasted_iota(i32, (F, S), 1))


def slots_from_faces(ext_row):
    return onehot(S, F, ext_row - F, lax.broadcasted_iota(i32, (S, F), 0))


def slots_from_columns(send_col):
    return onehot(S, F, send_col, lax.broadcasted_iota(i32, (S, F), 1))


def columns_from_slots(send_row):
    return onehot(F, S, send_row, lax.broadcasted_iota(i32, (F, S), 0))


def orientation(perm_col):
    lane = lanes(F)
    m = lane & 15
    crossed = lane - m + ((m & 3) * 4 + (m >> 2))
    k = jnp.broadcast_to(perm_col, (F, 128))
    flips = (k & 1) * 12 + ((k & 2) >> 1) * 3
    crossed_flips = (k & 1) * 3 + ((k & 2) >> 1) * 12
    swap = (k & 4) == 4
    place = jnp.where(swap, crossed, lane)
    return place ^ jnp.where(swap, crossed_flips, flips), place ^ flips


def peer_tables(send_ref, ext_ref):
    odd = (lax.axis_index("dom") & 1) == 1
    send = send_ref[...]
    swapped = jnp.concatenate([send[:, 2 * G :], send[:, G : 2 * G], send[:, :G]], axis=1)
    send = jnp.where(odd, send, swapped)

    def reordered(table):
        slot = table - F
        turned = jnp.where(slot < G, slot + 2 * G, jnp.where(slot >= 2 * G, slot - 2 * G, slot))
        turned = jnp.where((slot >= 0) & (slot < S), turned + F, table)
        return jnp.where(odd, turned, table)

    return send, reordered(column_of(ext_ref)), reordered(row_of(ext_ref))


def packed(x):
    lane = lanes(F)
    first = jnp.where(lane >= 64, turn(x, 64), 0.0)
    second = jnp.where((lane >= 80) & (lane < 96), turn(x, 16), 0.0)
    return jnp.concatenate([first, second], axis=1).astype(bf16)


def exterior(faces, wall, index, onehot_local, t, u):
    g = select_rows(onehot_local, t)
    node = index & 15
    x = jnp.where(wall, faces.mirror(t), take(g, index))
    v = by_axis(lambda a, g, node: take(g, (a + 1) * 16 + node), g, node)
    return x, jnp.where(wall, -u, v)


def folded(x):
    y = x.reshape(8, 16, 128)
    return (y[:, :8].reshape(64, 128) + turn(y[:, 8:].reshape(64, 128), 64)).reshape(8, 8, 128)


def folded_copies(x, at):
    y = x.reshape(8, 16, 128)
    group = lanes() >> 5
    low, high = mask(group == at), mask(group == at + 2)
    return (low * y[:, :8].reshape(64, 128) + high * y[:, 8:].reshape(64, 128)).reshape(8, 8, 128)


def unfolded(z):
    z = z.reshape(64, 128)
    low = mask(lanes() < 64)
    halves = [(low * part).reshape(8, 8, 128) for part in (z, turn(z, 64))]
    return jnp.concatenate(halves, axis=1).reshape(G, 128)


def places():
    own = jnp.where((lax.axis_index("dom") & 1) == 1, 0, 8)
    return own, 8 - own


def pack_kernel(state_hbm, final_hbm, send_hbm, ext_hbm, perm_hbm,
                chip_ref, out_ref, q_ref, w_ref, t_ref, lam_ref, send_slots_ref, back_slots_ref, inverse_ref,
                send_ref, ext_ref, perm_ref, state_ref, final_ref, sems):
    pairs = ((send_hbm, send_ref), (ext_hbm, ext_ref), (perm_hbm, perm_ref), (final_hbm, final_ref), (state_hbm, state_ref))
    copies = [pltpu.make_async_copy(a, b, sems.at[i]) for i, (a, b) in enumerate(pairs)]
    for copy in copies:
        copy.start()
    faces = Faces()
    for copy in copies[:3]:
        copy.wait()
    send, _, ext_row = peer_tables(send_ref, ext_ref)
    send_slots = slots_from_columns(slot_column(send))
    back_slots = slots_from_faces(ext_row)
    send_slots_ref[...] = send_slots
    back_slots_ref[...] = back_slots
    _, inverse = orientation(column_of(perm_ref))
    inverse_ref[...] = inverse
    for copy in copies[3:]:
        copy.wait()
    q = to_tiles(state_ref)
    w = to_tiles(final_ref)
    store_tiles(q_ref, q)
    store_tiles(w_ref, w)
    t = traces(q)
    lam = lift_factor * traces(w)
    t_ref[...] = t
    lam_ref[...] = lam
    y = take(lam, inverse)
    diagonal = by_axis(lambda a, y: signed(-faces.normal[a] * y), y)
    first = y - 0.5 * faces.rest_back(y) + turn(diagonal, 64)
    stack = jnp.concatenate([x.astype(bf16) for x in (first, faces.hessian(1, y), faces.hessian(2, y))], axis=1)
    back = dot(back_slots, stack)
    forward = dot(send_slots, packed(t))
    parts = [back[:, :128], back[:, 128:256] + forward[:, :128], back[:, 256:] + forward[:, 128:]]
    own, other = places()
    lane = lanes()
    guest = mask(lane >= 96) * turn(parts[2][:G], 32)
    rest = folded(mask(lane < 64) * parts[2][:G])
    for peer in range(8):
        at = 16 * peer
        chip_ref[peer] = jnp.concatenate(
            [guest[at : at + 16], parts[0][at : at + 16], parts[1][at : at + 16], rest[peer]], axis=0).astype(bf16)
        for o, place in ((1, own), (2, other)):
            at = G * o + 16 * peer
            for j in range(3):
                out_ref[place + peer, 16 * j : 16 * (j + 1)] = parts[j][at : at + 16].astype(bf16)


def first_local_kernel(q_ref, w_ref, t_ref, lam_ref, send_ref, ext_ref, perm_ref, forward_ref, backward_ref,
                       base_ref, t_base_ref, z_ref, rest_ref, u_ref, x_ref, v_ref,
                       from_slots_ref, to_columns_ref, local_ref, local_back_ref, index_ref, kind_ref):
    faces = Faces()
    send, ext_col, ext_row = peer_tables(send_ref, ext_ref)
    index, _ = orientation(column_of(perm_ref))
    index_ref[...] = index
    ext_wide = jnp.broadcast_to(ext_col, (F, 128))
    wall = ext_wide == F + S
    kind_ref[...] = jnp.where(wall, 2, jnp.where(ext_wide >= F + G, 1, jnp.where(ext_wide >= F, 3, 0)))
    from_slots_ref[...] = faces_from_slots(ext_col)
    to_columns_ref[...] = columns_from_slots(send)
    local = faces_from_columns(ext_col)
    local_ref[...] = local
    local_back_ref[...] = columns_from_faces(ext_row)
    q = load_tiles(q_ref)
    t = t_ref[...]
    lam = lam_ref[...]
    rest_ref[...] = lam - 0.5 * faces.rest_back(lam)
    u = faces.normal_of(t)
    x, v = exterior(faces, wall, index, local, t, u)
    u_ref[...] = u
    x_ref[...] = x
    v_ref[...] = v
    jump = 0.5 * (faces.flux(t, u) - faces.flux(x, v)) + (x - t)
    faced = lifted(lift_factor * jump)
    inner = volume(q, forward_ref[...])
    base = [q[j] + step_size * (inner[j] + faced[j]) for j in range(3)]
    store_tiles(base_ref, base)
    t_base_ref[...] = traces(base)
    z_ref[...] = derivative_back(load_tiles(w_ref), backward_ref[...])


def middle_kernel(base_ref, t_base_ref, w_ref, lam_ref, rest_ref, z_ref, arrived_ref,
                  from_slots_ref, to_columns_ref, local_ref, local_back_ref, send_slots_ref, back_slots_ref,
                  index_ref, inverse_ref, kind_ref,
                  chip_ref, out_ref, q1_ref, w1_ref, t1_ref, u1_ref, x1_ref, v1_ref, lam1_ref):
    faces = Faces()
    index = index_ref[...]
    inverse = inverse_ref[...]
    kind = kind_ref[...]
    wall = kind == 2
    wide = lanes(F)
    lane = lanes()
    node = index & 15
    own, other = places()
    mine, theirs = arrived_ref[pl.ds(own, 8)], arrived_ref[pl.ds(other, 8)]
    third = raw = mine[:, 32:48].reshape(G, 128)
    guest = mask((lane >= 64) & (lane < 96)) * turn(third.astype(f32), 96)
    rest = unfolded(mine[:, 80:].astype(f32))
    kept = lanes(G) < 96
    zero = jnp.zeros((G, 128), bf16)
    third = jnp.concatenate(
        [jnp.where(kept, third, zero), jnp.where(kept, theirs[:, 32:48].reshape(G, 128), zero)], axis=0)
    tiles = [jnp.concatenate([x.reshape(G, 128) for x in blocks], axis=0) for blocks in (
        (mine[:, 48:64], mine[:, :16], theirs[:, :16]), (mine[:, 64:80], mine[:, 16:32], theirs[:, 16:32]))]
    g = dot(from_slots_ref[...], jnp.concatenate(
        [tiles[1], jnp.concatenate([raw, raw, theirs[:, 32:48].reshape(G, 128)], axis=0)], axis=1))
    sums = dot(to_columns_ref[...], jnp.concatenate(
        tiles + [jnp.concatenate([(guest + rest).astype(bf16), third], axis=0)], axis=1))
    g0, g1 = g[:, :128], g[:, 128:]
    guest_at = (kind & 2) * 16
    place = jnp.where(wide < 64, index + 64, 80 + guest_at + node)
    xr = jnp.where(wide < 64, take(g0, place), mask(lane < 80) * take(g1, place))
    ur = by_axis(lambda a, g, node: take(g, 80 + 16 * a + node), g0, node)
    pr = take(g1, 80 + guest_at + node)
    jump = (lift_factor * step_size) * (xr - 0.5 * faces.flux(xr, ur, pr))
    t1 = t_base_ref[...] + lifted_traces(jump)
    faced = lifted(jump)
    base = load_tiles(base_ref)
    q1 = [base[j] + faced[j] for j in range(3)]
    store_tiles(q1_ref, q1)
    t1_ref[...] = t1
    t1_sent = t1.astype(bf16)
    forward = dot(send_slots_ref[...], t1_sent)
    lam = lam_ref[...]
    rest = rest_ref[...]
    u1 = faces.normal_of(t1)
    u1_ref[...] = u1
    x1, v1 = exterior(faces, wall, index, local_ref[...], t1, u1)
    x1_ref[...] = x1
    v1_ref[...] = v1
    bar = jnp.where((kind & 1) == 1, 0.0, rest - 0.5 * faces.state_back(x1, v1, lam))
    total = 0.5 * faces.state_back(t1, u1, lam) - rest + jnp.where(wall, faces.mirror(bar), 0.0)
    total = total + select_rows(local_back_ref[...], take(bar, inverse))
    sent = t1_sent.astype(f32)
    h0, h1, h2 = sums[:, :128], mask(lane < 64) * sums[:, 128:256], sums[:, 256:]
    ahead1, ahead2, behind2, behind1 = [faces.shifted(d)[1] for d in (1, 2, 3, 4)]
    through = h0 + h1 * take(sent, ahead1) + h2 * take(sent, ahead2)
    through = through + take(h1 * sent, behind1) + take(h2 * sent, behind2)
    through = through + mask((lane >= 16) & (lane < 64)) * turn(h0, 64) * sent
    total = total + mask(lane < 80) * through
    inner = volume_back(q1, z_ref[...])
    w = load_tiles(w_ref)
    half = [0.5 * w[j] + (0.5 * step_size) * inner[j] for j in range(3)]
    lam1 = lift_factor * traces(half) + (0.5 * step_size * lift_factor) * lifted_traces(total)
    faced = lifted(total)
    store_tiles(w1_ref, [half[j] + (0.5 * step_size) * faced[j] for j in range(3)])
    lam1_ref[...] = lam1
    bar = lam1 - 0.5 * faces.flux_back(xr, ur, lam1)
    first = take(bar, jnp.where(wide >= 80, inverse - 80, 80))
    second = take(bar, (inverse & 15) + 48 + (wide & 16))
    back = dot(back_slots_ref[...], jnp.concatenate([first, second], axis=1).astype(bf16))
    main = back[:, :128] + forward
    tail = [folded_copies(back[G * o : G * (o + 1), 128:], min(o, 1)) for o in range(3)]
    zero = jnp.zeros((16, 128), f32)
    for peer in range(8):
        at = 16 * peer
        chip_ref[peer] = jnp.concatenate([main[at : at + 16], tail[0][peer]], axis=0).astype(bf16)
        for o, place in ((1, own), (2, other)):
            at = G * o + 16 * peer
            out_ref[place + peer] = jnp.concatenate([main[at : at + 16], zero, tail[o][peer]], axis=0).astype(bf16)


def second_local_kernel(q_ref, w_ref, t_ref, u_ref, x_ref, v_ref, q1_ref, w1_ref, t1_ref, u1_ref, x1_ref, v1_ref,
                        lam1_ref, local_back_ref, inverse_ref, kind_ref,
                        forward_ref, backward_ref, end_ref, start_ref):
    faces = Faces()
    inverse = inverse_ref[...]
    kind = kind_ref[...]
    wall = kind == 2
    q = load_tiles(q_ref)
    q1 = load_tiles(q1_ref)
    t1 = t1_ref[...]
    x1 = x1_ref[...]
    jump = 0.5 * (faces.flux(t1, u1_ref[...]) - faces.flux(x1, v1_ref[...])) + (x1 - t1)
    faced = lifted(lift_factor * jump)
    inner = volume(q1, forward_ref[...])
    store_tiles(end_ref, [0.5 * q[j] + 0.5 * (q1[j] + step_size * (inner[j] + faced[j])) for j in range(3)])
    t = t_ref[...]
    lam1 = lam1_ref[...]
    u, x, v = u_ref[...], x_ref[...], v_ref[...]
    rest = lam1 - 0.5 * faces.rest_back(lam1)
    bar = jnp.where((kind & 1) == 1, 0.0, rest - 0.5 * faces.state_back(x, v, lam1))
    total = 0.5 * faces.state_back(t, u, lam1) - rest + jnp.where(wall, faces.mirror(bar), 0.0)
    total = total + select_rows(local_back_ref[...], take(bar, inverse))
    w = load_tiles(w_ref)
    w1 = load_tiles(w1_ref)
    inner = volume_back(q, derivative_back(w1, backward_ref[...]))
    faced = lifted(total)
    store_tiles(start_ref, [0.5 * w[j] + w1[j] + step_size * (inner[j] + faced[j]) for j in range(3)])


def last_kernel(end_base_ref, start_base_ref, arrived_ref, from_slots_ref, to_columns_ref, index_ref,
                end_ref, start_ref):
    faces = Faces()
    own, other = places()
    mine, theirs = arrived_ref[pl.ds(own, 8)], arrived_ref[pl.ds(other, 8)]
    main = jnp.concatenate(
        [mine[:, 16:32].reshape(G, 128), mine[:, :16].reshape(G, 128), theirs[:, :16].reshape(G, 128)], axis=0)
    lane = lanes()
    tail, next_tail = unfolded(mine[:, 32:].astype(f32)), unfolded(theirs[:, 32:].astype(f32))
    late = mask(lane >= 32)
    shared = jnp.concatenate([mask(lane < 32) * tail, late * tail, late * next_tail], axis=0).astype(bf16)
    node = index_ref[...] & 15
    g = dot(from_slots_ref[...], main)
    b = jnp.concatenate([dot(to_columns_ref[...], main), dot(to_columns_ref[...], shared)], axis=1)
    lane = lanes()
    valid = mask(lane < 80)
    xr = valid * take(g, index_ref[...])
    ur = by_axis(lambda a, g, node: take(g, (a + 1) * 16 + node), g, node)
    pr = take(g, 64 + node)
    faced = lifted((0.5 * step_size * lift_factor) * (xr - 0.5 * faces.flux(xr, ur, pr)))
    base = load_tiles(end_base_ref)
    from_tiles([base[j] + faced[j] for j in range(3)], end_ref)
    high = turn(b[:, 128:], 48) + turn(b[:, 128:], 16)
    bar = mask(lane < 48) * turn(b[:, :128], 48) + mask((lane >= 48) & (lane < 80)) * high
    faced = lifted(step_size * bar)
    base = load_tiles(start_base_ref)
    from_tiles([base[j] + faced[j] for j in range(3)], start_ref)


def shape(*dims, dtype=f32):
    return jax.ShapeDtypeStruct(dims, dtype)


def call(kernel, outs, *args, scratch=(), in_hbm=False):
    return pl.pallas_call(
        kernel,
        out_shape=outs,
        in_specs=[pl.BlockSpec(memory_space=pl.ANY if in_hbm else pltpu.VMEM)] * len(args),
        scratch_shapes=scratch,
        cost_estimate=pl.CostEstimate(flops=200_000_000, bytes_accessed=1_000_000, transcendentals=0),
        compiler_params=pltpu.CompilerParams(vmem_limit_bytes=32 * 1024 * 1024),
    )(*args)


def pair_peers(whole):
    count, peers = lax.axis_size("dom"), lax.axis_size("sub")
    groups = [[d % count * peers + peer for d in (first, first + 1) for peer in range(peers)]
              for first in range(1, count, 2)]
    return lax.all_to_all(
        whole, ("dom", "sub"), split_axis=0, concat_axis=0, tiled=True, axis_index_groups=groups)


def chip_partner(value):
    return lax.ppermute(value, "dom", [(d, d ^ 1) for d in range(lax.axis_size("dom"))])


def shards(state, adjoint_final, send_slot, ext_index, ext_perm):
    forward, backward = derivative_operands()
    forward, backward = jnp.asarray(forward), jnp.asarray(backward)
    state, adjoint_final = jnp.swapaxes(state, 1, 2), jnp.swapaxes(adjoint_final, 1, 2)
    node = shape(E, 384)
    face = shape(F, 128)
    index_face = shape(F, 128, dtype=i32)

    to_chip, out, q, w, t, lam, send_slots, back_slots, inverse, send_slot, ext_index, ext_perm = call(
        pack_kernel,
        (shape(8, 56, 128, dtype=bf16), shape(16, 88, 128, dtype=bf16), node, node, face, face,
         shape(S, F, dtype=bf16), shape(S, F, dtype=bf16), index_face,
         shape(1, S, dtype=i32), shape(6, E, dtype=i32), shape(6, E, dtype=i32)),
        *[pltpu.with_memory_space_constraint(x, pltpu.HBM) for x in (state, adjoint_final, send_slot, ext_index, ext_perm)], in_hbm=True,
        scratch=[pltpu.VMEM((5, E, 64), f32), pltpu.VMEM((5, E, 64), f32), pltpu.SemaphoreType.DMA((5,))])
    from_chip = chip_partner(to_chip)
    base, t_base, z, rest, u, x, v, from_slots, to_columns, local, local_back, index, kind = call(
        first_local_kernel,
        (node, face, shape(96, 384), face, face, face, face, shape(F, S, dtype=bf16), shape(F, S, dtype=bf16),
         shape(F, F, dtype=bf16), shape(F, F, dtype=bf16), index_face, index_face),
        q, w, t, lam, send_slot, ext_index, ext_perm, forward, backward)
    for start in (0, 8):
        out = lax.dynamic_update_slice(out, from_chip[:, 16:], (start, 48, 0))
        out = lax.dynamic_update_slice(out, out[start : start + 8, 32:48] + from_chip[:, :16], (start, 32, 0))
    out, z = lax.optimization_barrier((out, z))
    arrived = pair_peers(out)
    to_chip, out, q1, w1, t1, u1, x1, v1, lam1 = call(
        middle_kernel, (shape(8, 24, 128, dtype=bf16), shape(16, 40, 128, dtype=bf16), node, node, face, face, face, face, face),
        base, t_base, w, lam, rest, z, arrived,
        from_slots, to_columns, local, local_back, send_slots, back_slots, index, inverse, kind)
    from_chip = chip_partner(to_chip)
    end_base, start_base = call(
        second_local_kernel, (node, node),
        q, w, t, u, x, v, q1, w1, t1, u1, x1, v1, lam1, local_back, inverse, kind, forward, backward)
    out = lax.dynamic_update_slice(out, out[:8, 16:] + from_chip, (0, 16, 0))
    out = lax.dynamic_update_slice(out, out[8:, 16:] + from_chip, (8, 16, 0))
    out, end_base = lax.optimization_barrier((out, end_base))
    arrived = pair_peers(out)
    out = shape(5, E, 64)
    end, start = call(
        last_kernel, (out, out),
        end_base, start_base, arrived, from_slots, to_columns, index)
    return jnp.swapaxes(end, 1, 2), jnp.swapaxes(start, 1, 2)


def solution(mesh):
    return jax.shard_map(
        shards,
        mesh=mesh,
        in_specs=(
            P(None, None, ("dom", "sub")),
            P(None, None, ("dom", "sub")),
            P(("dom", "sub"), None),
            P(None, ("dom", "sub")),
            P(None, ("dom", "sub")),
        ),
        out_specs=(P(None, None, ("dom", "sub")), P(None, None, ("dom", "sub"))),
        check_vma=False,
    )
```
